32 devices in a mesh: rows: 16 (over z, y, x), ch: 2 (over core).
Axes of the slice: x: 2, y: 2, z: 4, core: 2. Of those that a mesh axis runs over, the one named last changes fastest.
Arguments:
- tokens: bfloat16 [2, 16, 256, 768], P(None, 'rows', None, 'ch'), may hold values from -6 to 6
- heights: int32 [2], replicated, may hold values from 4 to 16, as said below
- widths: int32 [2], replicated, may hold values from 64 to 256, as said below
- log_step: float32 [2, 768], P(None, 'ch'), may hold values from -0.7 to 0.7
- log_decay: float32 [2, 768, 32], P(None, 'ch'), as said below
- frequency: float32 [2, 768, 32], P(None, 'ch'), may hold values from 0 to 1
- b_in: float32 [2, 2, 768, 32], P(None, None, 'ch'), may hold values from -6 to 6
- c_out: float32 [2, 2, 768, 32], P(None, None, 'ch'), may hold values from -0.0625 to 0.0625
- skip_gain: float32 [768], P('ch'), may hold values from -3 to 3
- ln_gain: float32 [768], P('ch'), may hold values from 0.5 to 1.5
- ln_bias: float32 [768], P('ch'), may hold values from -1.75 to 1.75
- w_up: bfloat16 [768, 3072], P(None, 'ch'), may hold values from -0.21875 to 0.21875
- b_up: float32 [3072], P('ch'), may hold values from -1.75 to 1.75
- w_down: bfloat16 [3072, 768], P('ch'), may hold values from -0.109375 to 0.109375
- b_down: float32 [768], P('ch'), may hold values from -1.75 to 1.75
- layer_scale: float32 [768], P('ch'), may hold values from 0.5 to 1.5
- cotangent: bfloat16 [2, 16, 256, 768], P(None, 'rows', None, 'ch'), may hold values from -6 to 6
Outputs:
- output: bfloat16 [2, 16, 256, 768], P(None, 'rows', None, 'ch')
- d_tokens: bfloat16 [2, 16, 256, 768], P(None, 'rows', None, 'ch')
- d_log_step: float32 [2, 768], P(None, 'ch')
- d_log_decay: float32 [2, 768, 32], P(None, 'ch')
- d_frequency: float32 [2, 768, 32], P(None, 'ch')
- d_b_in: float32 [2, 2, 768, 32], P(None, None, 'ch')
- d_c_out: float32 [2, 2, 768, 32], P(None, None, 'ch')
- d_skip_gain: float32 [768], P('ch')
- d_ln_gain: float32 [768], P('ch')
- d_ln_bias: float32 [768], P('ch')
- d_w_up: float32 [768, 3072], P(None, 'ch')
- d_b_up: float32 [3072], P('ch')
- d_w_down: float32 [3072, 768], P('ch')
- d_b_down: float32 [768], P('ch')
- d_layer_scale: float32 [768], P('ch')
The draws below stay inside these ranges and needn't reach their ends.
Inputs may be any that keep to these rules, and one draw needn't show every extreme that they name: `heights`: one grid, drawn from the seed, has exactly 16 rows; every other grid has fewer. `widths`: one grid, drawn from the seed, has exactly 256 columns; every other grid has fewer. exp(log_decay) times the axis's length (16 for height, 256 for width) lies between 0.25 and 8.
All inputs are finite; a program needn't handle non-finite values.
Results may differ from the reference program's by a relative error of at most 0.0077.
Values may be sent and summed in bfloat16 or wider, within the bound.
A program may use at most 128 MiB of HBM per device.

```python
import math
import jax
import jax.numpy as jnp
from jax import lax

C = 768
FF = 3072
MODES = 32
GRIDS = 2
WMAX = 256
HMAX = 16


def draw_heights(key, part):
    key = jax.random.fold_in(key, 101)
    first_key, second_key = jax.random.split(key)
    sampled = jax.random.randint(first_key, (GRIDS,), HMAX // 4, HMAX)
    chosen = jax.random.randint(second_key, (), 0, GRIDS)
    return jnp.where(jnp.arange(GRIDS) == chosen, HMAX, sampled).astype(jnp.int32)


def draw_widths(key, part):
    key = jax.random.fold_in(key, 202)
    first_key, second_key = jax.random.split(key)
    sampled = jax.random.randint(first_key, (GRIDS,), WMAX // 4, WMAX)
    chosen = jax.random.randint(second_key, (), 0, GRIDS)
    return jnp.where(jnp.arange(GRIDS) == chosen, WMAX, sampled).astype(jnp.int32)


def draw_log_decay(key, part):
    key = jax.random.fold_in(key, 303)
    lowest, highest = (0.5, 8.0)
    spread = jax.random.uniform(key, (2, C, MODES), jnp.float32, math.log(lowest), math.log(highest))
    lengths = jnp.array([HMAX, WMAX], jnp.float32).reshape(2, 1, 1)
    return spread - jnp.log(lengths)


def levels(stream_key, shape, shards, smallest, high):
    def one(position, shards_of):
        steps = jax.random.uniform(jax.random.fold_in(jax.random.fold_in(stream_key, 6), position), (shards_of,), jnp.float32, smallest / len(shards), high / len(shards))
        return jnp.repeat(jnp.exp(steps), shape[position] // shards_of).reshape((-1,) + (1,) * (len(shape) - position - 1))

    level = one(*shards[0])
    for cut in shards[1:]:
        level = level * one(*cut)
    return level


def scatter_about(key, dims, deviation, limit, pieces=(), held_as=jnp.bfloat16):
    values = deviation * jax.random.normal(key, dims, jnp.float32)
    if pieces:
        values = values * levels(key, dims, pieces, -0.22, 0.18)
    return jnp.clip(values, -limit, limit).astype(held_as)


def setup_inputs(seed: int = 0) -> dict:
    arg_keys = jax.random.split(jax.random.key(seed), 18)
    tokens = scatter_about(arg_keys[0], (GRIDS, HMAX, WMAX, C), 1.0, 6.0, ((1, 16), (3, 2)))
    heights = draw_heights(jax.random.fold_in(arg_keys[17], 71), 0)
    widths = draw_widths(jax.random.fold_in(arg_keys[17], 71), 0)
    log_step = jnp.clip(jax.random.uniform(arg_keys[3], (2, C), jnp.float32, -0.7, 0.7) * levels(arg_keys[3], (2, C), ((1, 2),), -0.4, 0.0), -0.7, 0.7)
    log_decay = draw_log_decay(jax.random.fold_in(arg_keys[17], 71), 0)
    frequency = jnp.clip(1.0 * jax.random.uniform(arg_keys[5], (2, C, MODES), jnp.float32) ** levels(arg_keys[5], (2, C, MODES), ((1, 2),), -0.2, 0.2), 0.0, 1.0)
    b_in = scatter_about(arg_keys[6], (2, 2, C, MODES), 1.0, 6.0, ((2, 2),), jnp.float32)
    c_out = scatter_about(arg_keys[7], (2, 2, C, MODES), (MODES * WMAX) ** -0.5, 0.0625, ((2, 2),), jnp.float32)
    skip_gain = scatter_about(arg_keys[8], (C,), 1.0, 3.0, ((0, 2),), jnp.float32)
    ln_gain = jnp.clip(1.0 + 0.1 * jax.random.normal(arg_keys[9], (C,), jnp.float32), 0.5, 1.5)
    ln_bias = scatter_about(arg_keys[10], (C,), 0.3, 1.75, ((0, 2),), jnp.float32)
    w_up = scatter_about(arg_keys[11], (C, FF), C ** -0.5, 0.21875, ((1, 2),))
    b_up = scatter_about(arg_keys[12], (FF,), 0.3, 1.75, ((0, 2),), jnp.float32)
    w_down = scatter_about(arg_keys[13], (FF, C), FF ** -0.5, 0.109375, ((0, 2),))
    b_down = scatter_about(arg_keys[14], (C,), 0.3, 1.75, ((0, 2),), jnp.float32)
    layer_scale = jnp.clip(0.5 + 1.0 * jax.random.uniform(arg_keys[15], (C,), jnp.float32) ** levels(arg_keys[15], (C,), ((0, 2),), -0.2, 0.2), 0.5, 1.5)
    cotangent = scatter_about(arg_keys[16], (GRIDS, HMAX, WMAX, C), 1.0, 6.0, ((1, 16), (3, 2)))
    return {"tokens": tokens, "heights": heights, "widths": widths, "log_step": log_step, "log_decay": log_decay, "frequency": frequency, "b_in": b_in, "c_out": c_out, "skip_gain": skip_gain, "ln_gain": ln_gain, "ln_bias": ln_bias, "w_up": w_up, "b_up": b_up, "w_down": w_down, "b_down": b_down, "layer_scale": layer_scale, "cotangent": cotangent}


PRECISE = lax.Precision.HIGHEST
EPSILON = 1e-06

@jax.custom_vjp
def low(v):
    return lax.optimization_barrier(v.astype(jnp.bfloat16)).astype(jnp.float32)

@jax.custom_vjp
def low_back(v):
    return v

def low_keep(v):
    return (low(v), None)

def low_pass(kept, grad):
    return (grad,)

def back_keep(v):
    return (v, None)

def back_low(kept, grad):
    return (low(grad),)
low.defvjp(low_keep, low_pass)
low_back.defvjp(back_keep, back_low)

def make_kernel(params, length):
    log_step, log_decay, frequency, b_in, c_out = params
    step_size = jnp.exp(log_step)[:, None]
    decay_re = -jnp.exp(log_decay)
    step_re = step_size * decay_re
    step_im = step_size * frequency
    half_sin = jnp.sin(0.5 * step_im)
    num_re = jnp.expm1(step_re) * jnp.cos(step_im) - 2.0 * half_sin * half_sin
    num_im = jnp.exp(step_re) * jnp.sin(step_im)
    divisor = decay_re * decay_re + frequency * frequency
    zoh_re = (num_re * decay_re + num_im * frequency) / divisor
    zoh_im = (num_im * decay_re - num_re * frequency) / divisor
    prod_re = b_in[0] * c_out[0] - b_in[1] * c_out[1]
    prod_im = b_in[0] * c_out[1] + b_in[1] * c_out[0]
    coef_re = prod_re * zoh_re - prod_im * zoh_im
    coef_im = prod_re * zoh_im + prod_im * zoh_re
    places = jnp.arange(length, dtype=jnp.float32)[:, None, None]
    fading = jnp.exp(step_re[None] * places)
    turning = step_im[None] * places
    return 2.0 * lax.optimization_barrier(jnp.sum(fading * (coef_re * jnp.cos(turning) - coef_im * jnp.sin(turning)), axis=2))

def causal(values, kernel, axis_num):
    length = kernel.shape[0]
    spectrum = jnp.fft.rfft(values, n=2 * length, axis=axis_num)
    kernel_spec = jnp.fft.rfft(kernel, n=2 * length, axis=0)
    if axis_num == 1:
        kernel_spec = kernel_spec[:, None, :]
    result = jnp.fft.irfft(spectrum * kernel_spec, n=2 * length, axis=axis_num)
    return lax.slice_in_dim(result, 0, length, axis=axis_num)

def forward(tokens, log_step, log_decay, frequency, b_in, c_out, skip_gain, ln_gain, ln_bias, w_up, b_up, w_down, b_down, layer_scale, inside):
    k_height = make_kernel((log_step[0], log_decay[0], frequency[0], b_in[0], c_out[0]), HMAX)
    k_width = make_kernel((log_step[1], log_decay[1], frequency[1], b_in[1], c_out[1]), WMAX)
    along = low(low_back(causal(tokens, k_width, 2)))
    spatial = low(low_back(causal(along, k_height, 1)))
    mixed = spatial + skip_gain * tokens

    def one_grid(grid_args):
        grid_mixed, grid_tokens, grid_inside = grid_args
        centre = lax.optimization_barrier(jnp.mean(grid_mixed, axis=-1, keepdims=True))
        centred = grid_mixed - centre
        spread = lax.optimization_barrier(jnp.mean(centred * centred, axis=-1, keepdims=True))
        normed = low(centred * lax.rsqrt(spread + EPSILON) * ln_gain + ln_bias)
        hidden = low_back(jnp.dot(normed, w_up, precision=PRECISE, preferred_element_type=jnp.float32) + b_up)
        active = low(jax.nn.gelu(hidden, approximate=False))
        branch = low_back(jnp.dot(active, w_down, precision=PRECISE, preferred_element_type=jnp.float32) + b_down)
        return grid_tokens + grid_inside[..., None] * layer_scale * branch
    return lax.map(jax.checkpoint(one_grid), (mixed, tokens, inside))

def reference(tokens, heights, widths, log_step, log_decay, frequency, b_in, c_out, skip_gain, ln_gain, ln_bias, w_up, b_up, w_down, b_down, layer_scale, cotangent):
    row_ids = jnp.arange(HMAX, dtype=jnp.int32)
    col_ids = jnp.arange(WMAX, dtype=jnp.int32)
    inside = ((row_ids[None, :, None] < heights[:, None, None]) & (col_ids[None, None, :] < widths[:, None, None])).astype(jnp.float32)
    floats = (tokens.astype(jnp.float32), log_step, log_decay, frequency, b_in, c_out, skip_gain, ln_gain, ln_bias, w_up.astype(jnp.float32), b_up, w_down.astype(jnp.float32), b_down, layer_scale)

    def closed(*params):
        return forward(*params, inside)
    output, pullback = jax.vjp(closed, *floats)
    gradients = pullback(cotangent.astype(jnp.float32))
    return (output.astype(jnp.bfloat16), gradients[0].astype(jnp.bfloat16), gradients[1], gradients[2], gradients[3], gradients[4], gradients[5], gradients[6], gradients[7], gradients[8], gradients[9], gradients[10], gradients[11], gradients[12], gradients[13])
```

```python
import functools

import jax
import jax.numpy as jnp
from jax import lax
from jax.experimental import pallas as pl
from jax.experimental.pallas import tpu as pltpu
from jax.sharding import PartitionSpec as P

PRECISE = lax.Precision.HIGHEST
EPSILON = 1e-06
MESH = pl.DeviceIdType.MESH


def make_tables(length):
    freq_ids = jnp.arange(length + 1, dtype=jnp.int32)[:, None]
    places = jnp.arange(length, dtype=jnp.int32)[None, :]
    turns = freq_ids * places % (2 * length)
    angles = turns.astype(jnp.float32) * (jnp.pi / length)
    cosine = jnp.cos(angles)
    sine_t = jnp.sin(angles)
    weights = jnp.where((freq_ids == 0) | (freq_ids == length), 1.0, 2.0) / (2.0 * length)
    return (cosine, sine_t, cosine * weights, sine_t * weights)


def to_spectrum(values, tables, pattern):
    real_part = jnp.einsum(pattern, tables[0], values, precision=PRECISE)
    imag_part = -jnp.einsum(pattern, tables[1], values, precision=PRECISE)
    return (real_part, imag_part)


def from_spectrum(real_part, imag_part, tables, pattern):
    return jnp.einsum(pattern, tables[2], real_part, precision=PRECISE) - jnp.einsum(
        pattern, tables[3], imag_part, precision=PRECISE
    )


def kernel_spectrum(kernel, tables):
    real_part = jnp.dot(tables[0], kernel, precision=PRECISE)
    imag_part = -jnp.dot(tables[1], kernel, precision=PRECISE)
    return (real_part, imag_part)


def kernel_from_cross(cross_re, cross_im, tables):
    contract = (((0,), (0,)), ((), ()))
    return lax.dot_general(tables[2], cross_re, contract, precision=PRECISE) - lax.dot_general(
        tables[3], cross_im, contract, precision=PRECISE
    )


def make_kernel(params, length):
    log_step, log_decay, frequency, b_in, c_out = params
    step_size = jnp.exp(log_step)[:, None]
    decay_re = -jnp.exp(log_decay)
    step_re = step_size * decay_re
    step_im = step_size * frequency
    half_sin = jnp.sin(0.5 * step_im)
    num_re = jnp.expm1(step_re) * jnp.cos(step_im) - 2.0 * half_sin * half_sin
    num_im = jnp.exp(step_re) * jnp.sin(step_im)
    divisor = decay_re * decay_re + frequency * frequency
    zoh_re = (num_re * decay_re + num_im * frequency) / divisor
    zoh_im = (num_im * decay_re - num_re * frequency) / divisor
    prod_re = b_in[0] * c_out[0] - b_in[1] * c_out[1]
    prod_im = b_in[0] * c_out[1] + b_in[1] * c_out[0]
    coef_re = prod_re * zoh_re - prod_im * zoh_im
    coef_im = prod_re * zoh_im + prod_im * zoh_re
    places = jnp.arange(length, dtype=jnp.float32)[:, None, None]
    fading = jnp.exp(step_re[None] * places)
    turning = step_im[None] * places
    return 2.0 * jnp.sum(fading * (coef_re * jnp.cos(turning) - coef_im * jnp.sin(turning)), axis=2)


STAGES = 8


def reduce_places():
    rank, core = lax.axis_index("rows"), lax.axis_index("ch")
    x, y, z = rank % 2, (rank // 2) % 2, rank // 4
    near = z // 2
    toward = 4 * (2 * near - 1)
    middle = jnp.minimum(z * (3 - z), 1)
    beside = (rank + 1 - 2 * x, core)
    across = (rank + 2 - 4 * y, core)
    return (
        x,
        y,
        near,
        middle,
        beside,
        across,
        (rank - toward, core),
        (rank + toward, core),
    )


def reduce_barrier(places):
    middle = places[3]
    barrier = pltpu.get_barrier_semaphore()
    for target in places[4:7]:
        pl.semaphore_signal(barrier, inc=1, device_id=target, device_id_type=MESH)

    @pl.when(middle == 1)
    def _():
        pl.semaphore_signal(barrier, inc=1, device_id=places[7], device_id_type=MESH)

    pl.semaphore_wait(barrier, 3 + middle)


def reduce_stage(stage, c, role, places, keep, first, third, bufs):
    near, inner, outer = places[2], places[6], places[7]
    far = 1 - near
    part, from_first, from_outer, from_inner, from_third, full, send, recv = bufs

    def remote(src, dst, kind, target):
        return pltpu.make_async_remote_copy(
            src_ref=src,
            dst_ref=dst,
            send_sem=send.at[kind, c],
            recv_sem=recv.at[kind, c],
            device_id=target,
            device_id_type=MESH,
        )

    def added(*refs):
        total = refs[0][...].astype(jnp.float32)
        for ref in refs[1:]:
            total = total + ref[...].astype(jnp.float32)
        return total.astype(jnp.bfloat16)

    to_first = functools.partial(remote, part.at[c, 1 - keep], from_first.at[c], 0, first)
    far_in = functools.partial(remote, part.at[c, keep, far], from_outer.at[c, 0], 1, inner)
    near_in = functools.partial(remote, part.at[c, keep, near], from_outer.at[c, 1], 2, inner)
    far_over = functools.partial(remote, part.at[c, keep, far], from_inner.at[c], 3, inner)
    to_third = functools.partial(remote, part.at[c, keep, near], from_third.at[c], 4, third)
    own_out = functools.partial(remote, full.at[c, keep, near], full.at[c, keep, near], 5, outer)
    own_over = functools.partial(remote, full.at[c, keep, near], full.at[c, keep, near], 6, inner)
    over_in = functools.partial(remote, full.at[c, keep, far], full.at[c, keep, far], 6, inner)
    over_out = functools.partial(remote, full.at[c, keep, far], full.at[c, keep, far], 7, outer)
    back = functools.partial(remote, full.at[c, keep], full.at[c, keep], 8, first)
    back_in = functools.partial(remote, full.at[c, 1 - keep], full.at[c, 1 - keep], 8, first)
    near_back = functools.partial(remote, full.at[c, keep, near], full.at[c, keep, near], 5, inner)
    far_back = functools.partial(remote, full.at[c, keep, far], full.at[c, keep, far], 7, inner)
    if stage == 0:

        @pl.when(role > 0)
        def _():
            to_first().start()

    elif stage == 1:

        @pl.when(role > 0)
        def _():
            to_first().wait_recv()
            part[c, keep] = added(part.at[c, keep], from_first.at[c])

        @pl.when(role == 1)
        def _():
            far_in().start()
            near_in().start()

    elif stage == 2:

        @pl.when(role == 2)
        def _():
            far_in().wait_recv()
            part[c, keep, far] = added(part.at[c, keep, far], from_outer.at[c, 0])
            far_over().start()

    elif stage == 3:

        @pl.when(role == 2)
        def _():
            near_in().wait_recv()
            far_over().wait_recv()
            part[c, keep, near] = added(
                part.at[c, keep, near], from_outer.at[c, 1], from_inner.at[c]
            )
            to_third().start()

    elif stage == 4:

        @pl.when(role == 2)
        def _():
            to_third().wait_recv()
            full[c, keep, near] = added(part.at[c, keep, near], from_third.at[c])
            own_out().start()
            own_over().start()

    elif stage == 5:

        @pl.when(role == 2)
        def _():
            over_in().wait_recv()
            over_out().start()
            back().start()

    elif stage == 6:

        @pl.when(role == 1)
        def _():
            near_back().wait_recv()
            far_back().wait_recv()
            back().start()

    else:

        @pl.when(role > 0)
        def _():
            back_in().wait_recv()
            to_first().wait_send()
            back().wait_send()

        @pl.when(role == 2)
        def _():
            far_over().wait_send()
            to_third().wait_send()
            own_out().wait_send()
            own_over().wait_send()
            over_out().wait_send()

        @pl.when(role == 1)
        def _():
            far_in().wait_send()
            near_in().wait_send()


def reduce_kernel(down_ref, up_ref, down_full, up_full, *scratch):
    count = down_ref.shape[0]
    places = reduce_places()
    x, y, middle = places[0], places[1], places[3]
    beside, across = places[4], places[5]
    half = len(scratch) // 2
    down = (down_ref,) + scratch[: half - 2] + (down_full,) + scratch[half - 2 : half]
    up = (up_ref,) + scratch[half : 2 * half - 2] + (up_full,) + scratch[2 * half - 2 :]
    reduce_barrier(places)

    def tick(t, carry):
        for stage in range(STAGES):
            c = t - stage

            live = (c * (count - 1 - c) >= 0).astype(jnp.int32)
            role = live * (1 + middle)
            reduce_stage(stage, c, role, places, x, beside, across, down)
            reduce_stage(stage, c, role, places, y, across, beside, up)

        return carry

    lax.fori_loop(0, count + STAGES - 1, tick, 0)


def reduce_scratch(shape):
    count, _, _, rows, columns = shape
    return [
        pltpu.VMEM((count, 2, rows, columns), jnp.bfloat16),
        pltpu.VMEM((count, 2, rows, columns), jnp.bfloat16),
        pltpu.VMEM((count, rows, columns), jnp.bfloat16),
        pltpu.VMEM((count, rows, columns), jnp.bfloat16),
        pltpu.SemaphoreType.DMA((9, count)),
        pltpu.SemaphoreType.DMA((9, count)),
    ]


def sum_weights(d_w_down, d_w_up, part):
    hidden, channels = d_w_down.shape
    count = hidden // part
    down = d_w_down.astype(jnp.bfloat16).reshape(count, 2, 2, part // 4, channels)
    up = d_w_up.astype(jnp.bfloat16).reshape(channels, count, part)
    up = up.transpose(1, 0, 2).reshape(count, 2, 2, channels // 4, part)
    in_vmem = pl.BlockSpec(memory_space=pltpu.VMEM)
    down, up = pl.pallas_call(
        reduce_kernel,
        out_shape=(
            jax.ShapeDtypeStruct(down.shape, down.dtype),
            jax.ShapeDtypeStruct(up.shape, up.dtype),
        ),
        in_specs=[in_vmem] * 2,
        out_specs=(in_vmem, in_vmem),
        scratch_shapes=reduce_scratch(down.shape) + reduce_scratch(up.shape),
        compiler_params=pltpu.CompilerParams(
            collective_id=0, has_side_effects=True, vmem_limit_bytes=48 << 20
        ),
    )(down, up)
    up = up.reshape(count, channels, part).transpose(1, 0, 2).reshape(channels, hidden)
    return down.reshape(hidden, channels).astype(jnp.float32), up.astype(jnp.float32)


def shards(
    tokens,
    heights,
    widths,
    log_step,
    log_decay,
    frequency,
    b_in,
    c_out,
    skip_gain,
    ln_gain,
    ln_bias,
    w_up,
    b_up,
    w_down,
    b_down,
    layer_scale,
    cotangent,
):
    row_count = lax.axis_size("rows")
    row_rank = lax.axis_index("rows")
    grid_count, rows_here, columns, channels = tokens.shape
    all_channels = channels * lax.axis_size("ch")
    height = rows_here * row_count
    own_count = channels // row_count
    first_chan = row_rank * own_count
    pixels = grid_count * rows_here * columns
    token_f = tokens.astype(jnp.float32)
    width_tables = make_tables(columns)
    height_tables = make_tables(height)
    own_params = tuple(
        lax.dynamic_slice_in_dim(param, first_chan, own_count, param.ndim - trailing)
        for param, trailing in (
            (log_step, 1),
            (log_decay, 2),
            (frequency, 2),
            (b_in, 2),
            (c_out, 2),
        )
    )
    width_params = tuple(param[1] for param in own_params)
    height_params = tuple(param[0] for param in own_params)
    k_width, width_pull = jax.vjp(lambda params: make_kernel(params, columns), width_params)
    k_height, height_pull = jax.vjp(lambda params: make_kernel(params, height), height_params)
    kw_re, kw_im = kernel_spectrum(k_width, width_tables)
    kh_re, kh_im = kernel_spectrum(k_height, height_tables)
    kh_re = kh_re[:, None, :]
    kh_im = kh_im[:, None, :]
    pencil_tokens = lax.all_to_all(tokens, "rows", split_axis=3, concat_axis=1, tiled=True)
    x_re, x_im = to_spectrum(pencil_tokens.astype(jnp.float32), width_tables, "fw,grwc->grfc")
    along_width = from_spectrum(
        x_re * kw_re - x_im * kw_im, x_re * kw_im + x_im * kw_re, width_tables, "fw,grfc->grwc"
    ).astype(jnp.bfloat16)
    p_re, p_im = to_spectrum(along_width.astype(jnp.float32), height_tables, "fh,ghwc->gfwc")
    mixed_cols = from_spectrum(
        p_re * kh_re - p_im * kh_im, p_re * kh_im + p_im * kh_re, height_tables, "fh,gfwc->ghwc"
    ).astype(jnp.bfloat16)
    back_rows = lax.all_to_all(mixed_cols, "rows", split_axis=1, concat_axis=3, tiled=True)
    mixed = back_rows.astype(jnp.float32) + skip_gain * token_f
    flat_mixed = mixed.reshape(pixels, channels)
    sum_one, sum_two = lax.psum(
        (jnp.sum(flat_mixed, axis=1), jnp.sum(flat_mixed * flat_mixed, axis=1)), "ch"
    )
    centre = sum_one / all_channels
    spread = sum_two / all_channels - centre * centre
    inv_std = lax.rsqrt(spread + EPSILON)[:, None]
    x_hat = (flat_mixed - centre[:, None]) * inv_std
    normed = (x_hat * ln_gain + ln_bias).astype(jnp.bfloat16)
    hidden = (
        jnp.dot(
            lax.all_gather(normed, "ch", axis=1, tiled=True),
            w_up,
            preferred_element_type=jnp.float32,
        )
        + b_up
    )
    active = jax.nn.gelu(hidden, approximate=False).astype(jnp.bfloat16)
    partials = jnp.dot(active, w_down, preferred_element_type=jnp.float32)
    branch = (
        lax.psum_scatter(
            partials.astype(jnp.bfloat16), "ch", scatter_dimension=1, tiled=True
        ).astype(jnp.float32)
        + b_down
    )
    row_ids = row_rank * rows_here + jnp.arange(rows_here, dtype=jnp.int32)
    col_ids = jnp.arange(columns, dtype=jnp.int32)
    inside = (row_ids[None, :, None] < heights[:, None, None]) & (
        col_ids[None, None, :] < widths[:, None, None]
    )
    inside = inside.astype(jnp.float32).reshape(pixels, 1)
    flat_tokens = token_f.reshape(pixels, channels)
    output = (
        (flat_tokens + inside * layer_scale * branch).astype(jnp.bfloat16).reshape(tokens.shape)
    )
    over_rows = (((0,), (0,)), ((), ()))
    over_cols = (((1,), (1,)), ((), ()))
    g_flat = cotangent.astype(jnp.float32).reshape(pixels, channels)
    g_masked = g_flat * inside
    g_branch = (g_masked * layer_scale).astype(jnp.bfloat16)
    d_layer_scale = jnp.sum(g_masked * branch, axis=0)
    d_b_down = jnp.sum(g_branch.astype(jnp.float32), axis=0)
    g_branch_all = lax.all_gather(g_branch, "ch", axis=1, tiled=True)
    d_w_down = lax.dot_general(active, g_branch_all, over_rows, preferred_element_type=jnp.float32)
    g_active = lax.dot_general(g_branch_all, w_down, over_cols, preferred_element_type=jnp.float32)
    gelu_pull = jax.vjp(lambda values: jax.nn.gelu(values, approximate=False), hidden)[1]
    g_hidden = gelu_pull(g_active)[0].astype(jnp.bfloat16)
    d_b_up = jnp.sum(g_hidden.astype(jnp.float32), axis=0)
    d_w_up = lax.dot_general(
        lax.all_gather(normed, "ch", axis=1, tiled=True),
        g_hidden,
        over_rows,
        preferred_element_type=jnp.float32,
    )
    g_terms = lax.dot_general(g_hidden, w_up, over_cols, preferred_element_type=jnp.float32)
    g_normed = lax.psum_scatter(g_terms, "ch", scatter_dimension=1, tiled=True)
    d_ln_gain = jnp.sum(g_normed * x_hat, axis=0)
    d_ln_bias = jnp.sum(g_normed, axis=0)
    g_hat = g_normed * ln_gain
    sum_grad, sum_cross = lax.psum((jnp.sum(g_hat, axis=1), jnp.sum(g_hat * x_hat, axis=1)), "ch")
    g_mixed = inv_std * (
        g_hat - sum_grad[:, None] / all_channels - x_hat * sum_cross[:, None] / all_channels
    )
    d_skip_gain = jnp.sum(g_mixed * flat_tokens, axis=0)
    g_spatial = g_mixed.astype(jnp.bfloat16).reshape(tokens.shape)
    pencil_grad = lax.all_to_all(g_spatial, "rows", split_axis=3, concat_axis=1, tiled=True)
    gp_re, gp_im = to_spectrum(pencil_grad.astype(jnp.float32), height_tables, "fh,ghwc->gfwc")
    vp_re, vp_im = p_re, p_im
    g_pencil_along = from_spectrum(
        gp_re * kh_re + gp_im * kh_im, gp_im * kh_re - gp_re * kh_im, height_tables, "fh,gfwc->ghwc"
    ).astype(jnp.bfloat16)
    cross_re = jnp.sum(vp_re * gp_re + vp_im * gp_im, axis=(0, 2))
    cross_im = jnp.sum(vp_re * gp_im - vp_im * gp_re, axis=(0, 2))
    dk_height = kernel_from_cross(cross_re, cross_im, height_tables)
    g_along = g_pencil_along
    ga_re, ga_im = to_spectrum(g_along.astype(jnp.float32), width_tables, "fw,grwc->grfc")
    g_conv = from_spectrum(
        ga_re * kw_re + ga_im * kw_im, ga_im * kw_re - ga_re * kw_im, width_tables, "fw,grfc->grwc"
    )
    g_conv = lax.all_to_all(
        g_conv.astype(jnp.bfloat16), "rows", split_axis=1, concat_axis=3, tiled=True
    ).astype(jnp.float32)
    wide_re = jnp.sum(x_re * ga_re + x_im * ga_im, axis=(0, 1))
    wide_im = jnp.sum(x_re * ga_im - x_im * ga_re, axis=(0, 1))
    dk_width = kernel_from_cross(wide_re, wide_im, width_tables)
    d_tokens = ((g_flat + g_mixed * skip_gain).reshape(tokens.shape) + g_conv).astype(jnp.bfloat16)
    width_grads = width_pull(dk_width)[0]
    height_grads = height_pull(dk_height)[0]

    def gathered(pieces, dim_num):
        return lax.all_gather(jnp.stack(pieces), "rows", axis=dim_num, tiled=True)

    param_grads = tuple(
        gathered(pair, dim_num)
        for pair, dim_num in zip(zip(height_grads, width_grads), (1, 1, 1, 2, 2))
    )
    if row_count == 16:
        d_w_down, d_w_up = sum_weights(d_w_down, d_w_up, w_up.shape[1] // 12)
    else:
        d_w_down, d_w_up = lax.psum((d_w_down, d_w_up), "rows")
    d_skip_gain, d_ln_gain, d_ln_bias, d_b_up, d_b_down, d_layer_scale = lax.psum(
        (d_skip_gain, d_ln_gain, d_ln_bias, d_b_up, d_b_down, d_layer_scale), "rows"
    )
    return (output, d_tokens) + param_grads + (
        d_skip_gain,
        d_ln_gain,
        d_ln_bias,
        d_w_up,
        d_b_up,
        d_w_down,
        d_b_down,
        d_layer_scale,
    )


def solution(mesh):
    return jax.shard_map(
        shards,
        mesh=mesh,
        in_specs=(
            P(None, "rows", None, "ch"),
            P(),
            P(),
            P(None, "ch"),
            P(None, "ch", None),
            P(None, "ch", None),
            P(None, None, "ch", None),
            P(None, None, "ch", None),
            P("ch"),
            P("ch"),
            P("ch"),
            P(None, "ch"),
            P("ch"),
            P("ch", None),
            P("ch"),
            P("ch"),
            P(None, "rows", None, "ch"),
        ),
        out_specs=(
            P(None, "rows", None, "ch"),
            P(None, "rows", None, "ch"),
            P(None, "ch"),
            P(None, "ch", None),
            P(None, "ch", None),
            P(None, None, "ch", None),
            P(None, None, "ch", None),
            P("ch"),
            P("ch"),
            P("ch"),
            P(None, "ch"),
            P("ch"),
            P("ch", None),
            P("ch"),
            P("ch"),
        ),
        check_vma=False,
    )
```

```python
import functools
import types

import jax
import jax.numpy as jnp
import numpy as np
from jax import lax
from jax.experimental import pallas as pl
from jax.experimental.pallas import tpu as pltpu
from jax.sharding import PartitionSpec as P

PRECISE = lax.Precision.HIGHEST
EPSILON = 1e-06
MESH = pl.DeviceIdType.MESH


def make_tables(length):
    freq_ids = jnp.arange(length + 1, dtype=jnp.int32)[:, None]
    places = jnp.arange(length, dtype=jnp.int32)[None, :]
    turns = freq_ids * places % (2 * length)
    angles = turns.astype(jnp.float32) * (jnp.pi / length)
    cosine = jnp.cos(angles)
    sine_t = jnp.sin(angles)
    weights = jnp.where((freq_ids == 0) | (freq_ids == length), 1.0, 2.0) / (2.0 * length)
    return (cosine, sine_t, cosine * weights, sine_t * weights)


def to_spectrum(values, tables, pattern):
    real_part = jnp.einsum(pattern, tables[0], values, precision=PRECISE)
    imag_part = -jnp.einsum(pattern, tables[1], values, precision=PRECISE)
    return (real_part, imag_part)


def from_spectrum(real_part, imag_part, tables, pattern):
    return jnp.einsum(pattern, tables[2], real_part, precision=PRECISE) - jnp.einsum(
        pattern, tables[3], imag_part, precision=PRECISE
    )


def kernel_spectrum(kernel, tables):
    real_part = jnp.dot(tables[0], kernel, precision=PRECISE)
    imag_part = -jnp.dot(tables[1], kernel, precision=PRECISE)
    return (real_part, imag_part)


def kernel_from_cross(cross_re, cross_im, tables):
    contract = (((0,), (0,)), ((), ()))
    return lax.dot_general(tables[2], cross_re, contract, precision=PRECISE) - lax.dot_general(
        tables[3], cross_im, contract, precision=PRECISE
    )


def make_kernel(params, length):
    log_step, log_decay, frequency, b_in, c_out = params
    step_size = jnp.exp(log_step)[:, None]
    decay_re = -jnp.exp(log_decay)
    step_re = step_size * decay_re
    step_im = step_size * frequency
    half_sin = jnp.sin(0.5 * step_im)
    num_re = jnp.expm1(step_re) * jnp.cos(step_im) - 2.0 * half_sin * half_sin
    num_im = jnp.exp(step_re) * jnp.sin(step_im)
    divisor = decay_re * decay_re + frequency * frequency
    zoh_re = (num_re * decay_re + num_im * frequency) / divisor
    zoh_im = (num_im * decay_re - num_re * frequency) / divisor
    prod_re = b_in[0] * c_out[0] - b_in[1] * c_out[1]
    prod_im = b_in[0] * c_out[1] + b_in[1] * c_out[0]
    coef_re = prod_re * zoh_re - prod_im * zoh_im
    coef_im = prod_re * zoh_im + prod_im * zoh_re
    places = jnp.arange(length, dtype=jnp.float32)[:, None, None]
    fading = jnp.exp(step_re[None] * places)
    turning = step_im[None] * places
    return 2.0 * jnp.sum(fading * (coef_re * jnp.cos(turning) - coef_im * jnp.sin(turning)), axis=2)


RANKS = 16
STAGES = 8
HIGH = lax.Precision.HIGH
BF16 = jnp.bfloat16
F32 = jnp.float32
NT = (((1,), (1,)), ((), ()))
TN = (((0,), (0,)), ((), ()))


def spectral_tables(length):
    turns = np.outer(np.arange(length), np.arange(length)) % (2 * length)
    cosine = np.cos(np.pi * turns / length)
    sine = np.sin(np.pi * turns / length)
    sign = np.where(np.arange(length) % 2, -1.0, 1.0)
    to_re, to_im = cosine.copy(), -sine
    to_im[:, 0] = sign
    from_re, from_im = cosine / length, -sine / length
    from_re[0] /= 2
    from_im[0] = sign / (2 * length)
    return tuple(t.astype(np.float32) for t in (to_re, to_im, from_re, from_im))


def times(a, b):
    return a[0] * b[0] - a[1] * b[1], a[0] * b[1] + a[1] * b[0]


def reduce_stage(stage, c, role, places, keep, first, third, bufs):
    near, inner, outer = places
    far = 1 - near
    part, from_first, from_outer, from_inner, from_third, full, send, recv = bufs

    def remote(src, dst, kind, target):
        return pltpu.make_async_remote_copy(
            src_ref=src,
            dst_ref=dst,
            send_sem=send.at[kind, c],
            recv_sem=recv.at[kind, c],
            device_id=target,
            device_id_type=MESH,
        )

    def piece(which, kind, target):
        place = full.at[c, keep, which]
        return remote(place, place, kind, target)

    def added(*refs):
        total = refs[0][...].astype(F32)
        for ref in refs[1:]:
            total = total + ref[...].astype(F32)
        return total.astype(BF16)

    def to_first():
        return remote(part.at[c, 1 - keep], from_first.at[c], 0, first)

    def far_in():
        return remote(part.at[c, keep, far], from_outer.at[c, 0], 1, inner)

    def near_in():
        return remote(part.at[c, keep, near], from_outer.at[c, 1], 2, inner)

    def far_over():
        return remote(part.at[c, keep, far], from_inner.at[c], 3, inner)

    def to_third():
        return remote(part.at[c, keep, near], from_third.at[c], 4, third)

    def back(half):
        return remote(full.at[c, half], full.at[c, half], 8, first)

    if stage == 0:

        @pl.when(role > 0)
        def _():
            to_first().start()

    elif stage == 1:

        @pl.when(role > 0)
        def _():
            to_first().wait_recv()
            part[c, keep] = added(part.at[c, keep], from_first.at[c])

        @pl.when(role == 1)
        def _():
            far_in().start()
            near_in().start()

    elif stage == 2:

        @pl.when(role == 2)
        def _():
            far_in().wait_recv()
            part[c, keep, far] = added(part.at[c, keep, far], from_outer.at[c, 0])
            far_over().start()

    elif stage == 3:

        @pl.when(role == 2)
        def _():
            near_in().wait_recv()
            far_over().wait_recv()
            part[c, keep, near] = added(
                part.at[c, keep, near], from_outer.at[c, 1], from_inner.at[c]
            )
            to_third().start()

    elif stage == 4:

        @pl.when(role == 2)
        def _():
            to_third().wait_recv()
            full[c, keep, near] = added(part.at[c, keep, near], from_third.at[c])
            piece(near, 5, outer).start()
            piece(near, 6, inner).start()

    elif stage == 5:

        @pl.when(role == 2)
        def _():
            piece(far, 6, inner).wait_recv()
            piece(far, 7, outer).start()
            back(keep).start()

    elif stage == 6:

        @pl.when(role == 1)
        def _():
            piece(near, 5, inner).wait_recv()
            piece(far, 7, inner).wait_recv()
            back(keep).start()

    else:

        @pl.when(role > 0)
        def _():
            back(1 - keep).wait_recv()
            to_first().wait_send()
            back(keep).wait_send()

        @pl.when(role == 2)
        def _():
            far_over().wait_send()
            to_third().wait_send()
            piece(near, 5, outer).wait_send()
            piece(near, 6, inner).wait_send()
            piece(far, 7, outer).wait_send()

        @pl.when(role == 1)
        def _():
            far_in().wait_send()
            near_in().wait_send()


def mode_values(modes):
    log_step, log_decay, freq, b_re, b_im, c_re, c_im = (modes[2 * q : 2 * q + 2] for q in range(7))
    step = jnp.exp(log_step)
    decay = -jnp.exp(log_decay)
    step_re = step * decay
    step_im = step * freq
    half_sin = jnp.sin(0.5 * step_im)
    series = jnp.ones_like(step_re)
    for order in range(11, 1, -1):
        series = 1.0 + series * step_re * (1.0 / order)
    grown = jnp.exp(step_re)
    less_one = jnp.where(step_re > -0.5, step_re * series, grown - 1.0)
    num_re = less_one * jnp.cos(step_im) - 2.0 * half_sin * half_sin
    num_im = grown * jnp.sin(step_im)
    inverse = 1.0 / (decay * decay + freq * freq)
    over = (decay * inverse, -freq * inverse)
    zoh = times((num_re, num_im), over)
    b, c = (b_re, b_im), (c_re, c_im)
    prod = times(b, c)
    return types.SimpleNamespace(
        step=step,
        rate=(decay, freq),
        over=over,
        step_re=step_re,
        step_im=step_im,
        once=(num_re + 1.0, num_im),
        zoh=zoh,
        b=b,
        c=c,
        prod=prod,
        coef=times(prod, zoh),
    )


def block_kernel(names, *refs):
    v = types.SimpleNamespace(**dict(zip(names, refs)))
    rank, core = lax.axis_index("rows"), lax.axis_index("ch")
    x, y, z = rank % 2, (rank // 2) % 2, rank // 4
    near = z // 2
    toward = 4 * (2 * near - 1)
    middle = jnp.minimum(z * (3 - z), 1)
    beside, across = (rank + 1 - 2 * x, core), (rank + 2 - 4 * y, core)
    places = (near, (rank - toward, core), (rank + toward, core))
    twin = (rank, 1 - core)
    heights, widths = v.heights, v.widths
    chunks, part = v.wd.shape[0], v.wd.shape[1]
    slab, columns = v.rb1.shape[1:]
    own = slab // 2
    here = own * RANKS
    pixels = 2 * columns
    per = v.log_decay.shape[1]
    lanes = own * per

    def copy(src, dst, sems, index, target):
        return pltpu.make_async_remote_copy(
            src_ref=src,
            dst_ref=dst,
            send_sem=sems.at[0, index],
            recv_sem=sems.at[1, index],
            device_id=target,
            device_id_type=MESH,
        )

    def loop(count, body, start=0):
        def step(i, carry):
            body(i)
            return carry

        lax.fori_loop(start, count, step, 0)

    def wide(column):
        return jnp.concatenate([column] * (pixels // column.shape[1]), axis=1)

    def scatter(sems, src, dst):
        def start(k):
            d = lax.rem(rank + k, RANKS)
            copy(src(d), dst, sems, k, (d, core)).start()

        loop(RANKS, start, 1)

    def arrived(sems, src, dst, then=None):
        def wait(k):
            s = lax.rem(rank + RANKS - k, RANKS)
            copy(src(s), dst(s), sems, k, (s, core)).wait_recv()
            if then is not None:
                then(k, s)

        loop(RANKS, wait, 1)

    def scattered(sems, src, dst):
        def wait(k):
            d = lax.rem(rank + k, RANKS)
            copy(src(d), dst, sems, k, (d, core)).wait_send()

        loop(RANKS, wait, 1)

    barrier = pltpu.get_barrier_semaphore()

    def greet(k):
        pl.semaphore_signal(
            barrier, inc=1, device_id=(lax.rem(rank + k, RANKS), core), device_id_type=MESH
        )

    loop(RANKS, greet, 1)
    pl.semaphore_signal(barrier, inc=1, device_id=twin, device_id_type=MESH)

    def fetch_up(m):
        cols = pl.ds(pl.multiple_of(m * part, part), part)
        return pltpu.make_async_copy(v.w_up.at[:, cols], v.wu.at[m], v.fetch.at[0, m])

    def fetch_down(m):
        rows = pl.ds(pl.multiple_of(m * part, part), part)
        return pltpu.make_async_copy(v.w_down.at[rows], v.wd.at[m], v.fetch.at[1, m])

    def fetch(m):
        fetch_up(m).start()
        fetch_down(m).start()

    loop(chunks, fetch)

    for g in range(2):
        v.tok[:, g * columns : (g + 1) * columns] = v.tokens[g, 0].astype(F32).T

    def cut_tokens(d):
        rows = v.tok[pl.ds(pl.multiple_of(d * own, 8), own), :]
        both = jnp.concatenate([rows[:, :columns], rows[:, columns:]], axis=0)
        v.tb[core, d] = both.astype(BF16)

    loop(RANKS, cut_tokens)
    lines = []
    for vector in (v.b_up, v.skip_gain, v.ln_gain, v.ln_bias, v.layer_scale, v.b_down):
        line = vector[...].reshape(1, vector.shape[0])
        lines += [line[:, q * 128 : (q + 1) * 128] for q in range(vector.shape[0] // 128)]
    lines.append(jnp.zeros((32 - len(lines), 128), F32))
    v.vx[core] = jnp.concatenate(lines, axis=0)
    pl.semaphore_wait(barrier, RANKS)
    scatter(v.a1, lambda d: v.tb.at[core, d], v.rb1.at[rank])
    v.rb1[rank] = v.tb[core, rank]
    copy(v.tb.at[core], v.tb.at[core], v.tw, 0, twin).start()
    copy(v.vx.at[core], v.vx.at[core], v.tw, 1, twin).start()

    def spread(which, rows):
        block = jnp.concatenate([rows, jnp.zeros((128 - rows.shape[0], 128), F32)], axis=0)
        cols = block.T
        for q in range(15):
            v.vb[q // 3, which, q % 3 * 128 : (q % 3 + 1) * 128, :] = jnp.broadcast_to(
                cols[:, 12 + q : 13 + q], (128, 128)
            )
        return cols

    cols = spread(core, v.vx[core])
    for m in range(chunks):
        for q in range(2):
            v.bias[m, q * 128 : (q + 1) * 128, :] = jnp.broadcast_to(
                cols[:, 2 * m + q : 2 * m + q + 1], (128, 128)
            )
    for g in range(2):
        v.cot[:, g * columns : (g + 1) * columns] = v.cotangent[g, 0].astype(F32).T
    places_w = lax.broadcasted_iota(jnp.int32, (1, columns), 1)
    inside = jnp.concatenate(
        [(places_w < jnp.where(rank < heights[g], widths[g], 0)).astype(F32) for g in range(2)],
        axis=1,
    )
    v.inside[...] = jnp.broadcast_to(inside, (8, pixels))

    def mask_rows(q):
        rows = pl.ds(pl.multiple_of(q * 128, 128), 128)
        masked = v.cot[rows, :] * v.inside[0:1, :]
        v.gb[core, rows, :] = (masked * wide(v.vb[3, core, rows, :])).astype(BF16)

    loop(here // 128, mask_rows)
    copy(v.gb.at[core], v.gb.at[core], v.tw, 2, twin).start()

    lane = lax.broadcasted_iota(jnp.int32, (slab, lanes), 1) // per
    row = lax.broadcasted_iota(jnp.int32, (slab, lanes), 0)
    row = jnp.where(row >= own, row - own, row)
    v.pick[...] = (lane == row).astype(F32)
    chosen = lax.broadcasted_iota(jnp.int32, (here, lanes), 1) // per + rank * own
    chosen = (lax.broadcasted_iota(jnp.int32, (here, lanes), 0) == chosen).astype(F32)
    all_modes = jnp.concatenate(
        [v.log_step[...], jnp.zeros((6, here), F32)]
        + [v.log_decay[a] for a in range(2)]
        + [v.frequency[a] for a in range(2)]
        + [v.b_in[a, i] for i in range(2) for a in range(2)]
        + [v.c_out[a, i] for i in range(2) for a in range(2)],
        axis=0,
    )
    all_modes = jnp.dot(all_modes, chosen, precision=PRECISE, preferred_element_type=F32)
    mode = lax.broadcasted_iota(jnp.int32, (per, lanes), 1) % per
    mode = (mode == lax.broadcasted_iota(jnp.int32, (per, lanes), 0)).astype(F32)
    v.of_mode[...] = mode
    own_modes = jnp.sum(all_modes[8:].reshape(12, per, lanes) * mode[None], axis=1)
    v.modes[...] = jnp.concatenate([all_modes[:2], own_modes, own_modes[:2]], axis=0)
    mv = mode_values(v.modes[...])

    def powers(axis, place):
        angle = mv.step_im[axis : axis + 1] * place
        fade = jnp.exp(mv.step_re[axis : axis + 1] * place)
        return fade * jnp.cos(angle), fade * jnp.sin(angle)

    high_place = lax.broadcasted_iota(jnp.int32, (RANKS, lanes), 0).astype(F32)
    v.eh[0], v.eh[1] = powers(0, high_place)
    low_place = lax.broadcasted_iota(jnp.int32, (8, lanes), 0).astype(F32)
    base = powers(1, low_place)
    many = columns // 8
    v.ej[0], v.ej[1] = powers(
        1, 8.0 * lax.broadcasted_iota(jnp.int32, (many, lanes), 0).astype(F32)
    )
    coef_w = tuple(2.0 * part_of[1:2] for part_of in mv.coef)

    def fill(j):
        at = pl.ds(pl.multiple_of(j * 8, 8), 8)
        jump = (v.ej[0, pl.ds(j, 1), :], v.ej[1, pl.ds(j, 1), :])
        e_re, e_im = times(base, jump)
        v.ew[0, at, :] = e_re
        v.ew[1, at, :] = e_im
        v.kt[at, :] = coef_w[0] * e_re - coef_w[1] * e_im

    loop(many, fill)
    k_width = lax.dot_general(
        v.pick[...], v.kt[...], NT, precision=PRECISE, preferred_element_type=F32
    )
    k_re = jnp.dot(k_width, v.to_re[...], precision=PRECISE, preferred_element_type=F32)
    k_im = jnp.dot(k_width, v.to_im[...], precision=PRECISE, preferred_element_type=F32)
    first_lane = lax.broadcasted_iota(jnp.int32, (slab, columns), 1) == 0
    v.ks[0] = k_re
    v.ks[1] = jnp.where(first_lane, 0.0, k_im)
    v.ks[2] = jnp.where(first_lane, k_im, k_re)
    coef_h = tuple(2.0 * part_of[0:1] for part_of in mv.coef)
    v.kt[0:RANKS, :] = coef_h[0] * v.eh[0] - coef_h[1] * v.eh[1]

    def k_height(l):
        taps = jnp.sum(v.pick[...] * v.kt[pl.ds(l, 1), :], axis=1, keepdims=True)
        v.kh[l] = jnp.broadcast_to(taps, (slab, 128))

    loop(RANKS, k_height)

    def turn(m):
        fetch_up(m).wait()
        fetch_down(m).wait()
        v.wut[m] = v.wu[m].T
        v.wdt[m] = v.wd[m].T

    loop(chunks // 2, turn)

    arrived(v.a1, lambda s: v.tb.at[core, s], lambda s: v.rb1.at[s])
    step_rows = 4

    def convolve(b):
        at = pl.ds(b * step_rows, step_rows)
        values = v.rb1[at].reshape(step_rows * slab, columns).astype(F32)
        shape = (step_rows, slab, columns)
        x_re = jnp.dot(values, v.to_re[...], precision=HIGH, preferred_element_type=F32)
        x_im = jnp.dot(values, v.to_im[...], precision=HIGH, preferred_element_type=F32)
        x_re, x_im = x_re.reshape(shape), x_im.reshape(shape)
        v.xs[0, at] = x_re
        v.xs[1, at] = x_im
        k0, k1, k2 = v.ks[0], v.ks[1], v.ks[2]
        y_re = (x_re * k0 - x_im * k1).reshape(step_rows * slab, columns)
        y_im = (x_re * k1 + x_im * k2).reshape(step_rows * slab, columns)
        along = jnp.dot(y_re, v.from_re[...], precision=HIGH, preferred_element_type=F32)
        along += jnp.dot(y_im, v.from_im[...], precision=HIGH, preferred_element_type=F32)
        v.along[at] = along.astype(BF16).astype(F32).reshape(shape)

    loop(RANKS // step_rows, convolve)

    def by_tiles(body):
        def rows(r):
            for half in range(columns // 128):
                body(pl.ds(pl.multiple_of(r * 8, 8), 8), slice(half * 128, half * 128 + 128))

        loop(slab // 8, rows)

    def down_rows(at, cut):
        taps = [v.kh[l, at, :] for l in range(RANKS)]
        values = [v.along[i, at, cut] for i in range(RANKS)]
        for i in range(RANKS):
            total = taps[0] * values[i]
            for l in range(1, i + 1):
                total += taps[l] * values[i - l]
            v.tall[i, at, cut] = total

    by_tiles(down_rows)
    v.sb2[...] = v.tall[...].astype(BF16)
    scatter(v.a2, lambda d: v.sb2.at[d], v.rb2.at[core, rank])
    v.rb2[core, rank] = v.sb2[rank]
    copy(v.rb2.at[core, rank], v.rb2.at[core, rank], v.fw, 0, twin).start()

    copy(v.vx.at[core], v.vx.at[1 - core], v.tw, 1, twin).wait_recv()
    spread(1 - core, v.vx[1 - core])
    loop(chunks, turn, chunks // 2)
    v.branch[...] = jnp.zeros_like(v.branch)
    v.gn[...] = jnp.zeros_like(v.gn)

    def forward(k, s):
        copy(v.rb2.at[core, s], v.rb2.at[core, s], v.fw, k, twin).start()

    arrived(v.a2, lambda s: v.sb2.at[s], lambda s: v.rb2.at[core, s], forward)
    copy(v.tb.at[core], v.tb.at[1 - core], v.tw, 0, twin).wait_recv()

    def forwarded(k):
        s = lax.rem(rank + RANKS - k, RANKS)
        copy(v.rb2.at[core, s], v.rb2.at[1 - core, s], v.fw, k, twin).wait_recv()

    loop(RANKS, forwarded)

    eight = jnp.zeros((8, pixels), F32)

    def folded(values):
        return values.reshape(own // 8, 8, pixels).sum(axis=0)

    def mix(i, total):
        which, d = i // RANKS, lax.rem(i, RANKS)
        spatial = v.rb2[which, d].astype(F32)
        token = v.tb[which, d].astype(F32)
        skip = wide(v.vb[0, which, pl.ds(pl.multiple_of(d * own, 8), own), :])
        spatial = jnp.concatenate([spatial[:own], spatial[own:]], axis=1)
        token = jnp.concatenate([token[:own], token[own:]], axis=1)
        mixed = spatial + skip * token
        v.xhat[i] = mixed
        return total + folded(mixed)

    channels = 2 * here
    total = lax.fori_loop(0, 2 * RANKS, mix, eight)
    centre = jnp.sum(total, axis=0, keepdims=True) * (1.0 / channels)

    def squares(i, total):
        off = v.xhat[i] - centre
        return total + folded(off * off)

    total = lax.fori_loop(0, 2 * RANKS, squares, eight)
    spread_of = jnp.sum(total, axis=0, keepdims=True) * (1.0 / channels)
    inv_std = lax.rsqrt(spread_of + EPSILON)
    v.inv[...] = jnp.broadcast_to(inv_std, (8, pixels))

    def normalize(q):
        rows = []
        for k in range(2):
            i = 2 * q + k
            which, d = i // RANKS, lax.rem(i, RANKS)
            at = pl.ds(pl.multiple_of(d * own, 8), own)
            x_hat = (v.xhat[i] - centre) * inv_std
            v.xhat[i] = x_hat
            rows.append(x_hat * wide(v.vb[1, which, at, :]) + wide(v.vb[2, which, at, :]))
        at = pl.ds(pl.multiple_of(q * 2 * own, 16), 2 * own)
        v.normed[at, :] = jnp.concatenate(rows, axis=0).astype(BF16)

    loop(RANKS, normalize)
    copy(v.gb.at[core], v.gb.at[1 - core], v.tw, 2, twin).wait_recv()

    def feed(t):
        normed = v.normed[...]
        g_branch = v.gb[...].reshape(channels, pixels)
        hidden = jnp.dot(v.wut[t], normed, preferred_element_type=F32) + wide(v.bias[t])
        phi = 0.5 + 0.5 * lax.erf(hidden * (0.5**0.5))
        density = jnp.exp(-0.5 * hidden * hidden) * ((2.0 * jnp.pi) ** -0.5)
        active = (hidden * phi).astype(BF16)
        slope = phi + hidden * density
        g_active = jnp.dot(v.wd[t], g_branch, preferred_element_type=F32)
        g_hidden = (g_active * slope).astype(BF16)
        down = lax.dot_general(active, g_branch, NT, preferred_element_type=F32)
        v.pd[t] = down.astype(BF16).reshape(2, 2, part // 4, channels)
        up = lax.dot_general(normed, g_hidden, NT, preferred_element_type=F32)
        v.pu[t] = up.astype(BF16).reshape(2, 2, channels // 4, part)
        v.gn[...] += jnp.dot(v.wu[t], g_hidden, preferred_element_type=F32)
        v.branch[...] += jnp.dot(v.wdt[t], active, preferred_element_type=F32)
        ones = jnp.ones((8, pixels), BF16)
        v.dbu[t] = lax.dot_general(ones, g_hidden, NT, preferred_element_type=F32)

    def share():
        v.gn_out[...] = v.gn[...].astype(BF16)
        copy(v.gn_out, v.gn_in, v.tw, 3, twin).start()
        theirs = pl.ds(pl.multiple_of((1 - core) * here, here), here)
        v.br_out[...] = v.branch[theirs, :].astype(BF16)
        copy(v.br_out, v.br_in, v.tw, 4, twin).start()

    def lane_sum(values):
        return sum(values[:, q * 128 : (q + 1) * 128] for q in range(pixels // 128))

    def norm_back():
        copy(v.gn_out, v.gn_in, v.tw, 3, twin).wait_recv()

        def whole(q, totals):
            at = pl.ds(pl.multiple_of(q * 2 * own, 16), 2 * own)
            g_normed = v.gn[at, :] + v.gn_in[at, :].astype(F32)
            v.gn[at, :] = g_normed
            one, two = totals
            for k in range(2):
                i = 2 * q + k
                which, d = i // RANKS, lax.rem(i, RANKS)
                gain = wide(v.vb[1, which, pl.ds(pl.multiple_of(d * own, 8), own), :])
                g_hat = g_normed[k * own : (k + 1) * own] * gain
                one = one + folded(g_hat)
                two = two + folded(g_hat * v.xhat[i])
            return one, two

        one, two = lax.fori_loop(0, RANKS, whole, (eight, eight))
        one = jnp.sum(one, axis=0, keepdims=True) * (1.0 / channels)
        two = jnp.sum(two, axis=0, keepdims=True) * (1.0 / channels)
        scale = v.inv[0:1, :]

        def each(d):
            at = pl.ds(pl.multiple_of(d * own, 8), own)
            x_hat = v.xhat[core * RANKS + d]
            g_normed = v.gn[pl.ds(pl.multiple_of(core * here + d * own, 8), own), :]
            g_mixed = scale * (g_normed * wide(v.vb[1, core, at, :]) - one - x_hat * two)
            v.gmix[at, :] = g_mixed
            v.sums[0, at, :] = lane_sum(g_mixed * v.tok[at, :])
            v.sums[1, at, :] = lane_sum(g_normed * x_hat)
            v.sums[2, at, :] = lane_sum(g_normed)
            both = jnp.concatenate([g_mixed[:, :columns], g_mixed[:, columns:]], axis=0)
            v.sb3[d] = both.astype(BF16)

        loop(RANKS, each)
        scatter(v.a3, lambda d: v.sb3.at[d], v.rb3.at[rank])
        v.rb3[rank] = v.sb3[rank]

    def outputs():
        copy(v.br_out, v.br_in, v.tw, 4, twin).wait_recv()
        mask = v.inside[0:1, :]

        def rows(q):
            at = pl.ds(pl.multiple_of(q * 128, 128), 128)
            branch = v.branch[pl.ds(pl.multiple_of(core * here + q * 128, 128), 128), :]
            branch = branch + v.br_in[at, :].astype(F32) + wide(v.vb[4, core, at, :])
            masked = branch * mask
            v.sums[3, at, :] = lane_sum(v.gb[core, at, :].astype(F32))
            v.sums[4, at, :] = lane_sum(masked * v.cot[at, :])
            v.res[at, :] = v.tok[at, :] + masked * wide(v.vb[3, core, at, :])

        loop(here // 128, rows)
        for g in range(2):
            v.output[g, 0] = v.res[:, g * columns : (g + 1) * columns].T.astype(BF16)

    def convolve_back():
        arrived(v.a3, lambda s: v.sb3.at[s], lambda s: v.rb3.at[s])
        v.tall[...] = v.rb3[...].astype(F32)

        def up_rows(at, cut):
            taps = [v.kh[l, at, :] for l in range(RANKS)]
            values = [v.tall[i, at, cut] for i in range(RANKS)]
            for i in range(RANKS):
                total = taps[0] * values[i]
                for l in range(1, RANKS - i):
                    total += taps[l] * values[i + l]
                v.galong[i, at, cut] = total.astype(BF16).astype(F32)

        by_tiles(up_rows)

        def lag_rows(at, cut):
            grads = [v.tall[i, at, cut] for i in range(RANKS)]
            values = [v.along[i, at, cut] for i in range(RANKS)]
            for l in range(RANKS):
                total = grads[l] * values[0]
                for i in range(l + 1, RANKS):
                    total += grads[i] * values[i - l]
                v.lags[l, at, cut] = total

        by_tiles(lag_rows)
        none = jnp.zeros((slab, columns), F32)

        def one_step(b, totals):
            at = pl.ds(b * step_rows, step_rows)
            shape = (step_rows, slab, columns)
            values = v.galong[at].reshape(step_rows * slab, columns)
            g_re = jnp.dot(values, v.to_re[...], precision=HIGH, preferred_element_type=F32)
            g_im = jnp.dot(values, v.to_im[...], precision=HIGH, preferred_element_type=F32)
            g_re, g_im = g_re.reshape(shape), g_im.reshape(shape)
            x_re, x_im = v.xs[0, at], v.xs[1, at]
            k0, k1, k2 = v.ks[0], v.ks[1], v.ks[2]
            y_re = (g_re * k0 + g_im * k1).reshape(step_rows * slab, columns)
            y_im = (g_im * k2 - g_re * k1).reshape(step_rows * slab, columns)
            conv = jnp.dot(y_re, v.from_re[...], precision=HIGH, preferred_element_type=F32)
            conv += jnp.dot(y_im, v.from_im[...], precision=HIGH, preferred_element_type=F32)
            v.sb4[at] = conv.reshape(shape).astype(BF16)
            return (
                totals[0] + (x_re * g_re).sum(axis=0),
                totals[1] + (x_im * g_im).sum(axis=0),
                totals[2] + (x_re * g_im - x_im * g_re).sum(axis=0),
            )

        cross = lax.fori_loop(0, RANKS // step_rows, one_step, (none, none, none))
        scatter(v.a4, lambda d: v.sb4.at[d], v.rb4.at[rank])
        v.rb4[rank] = v.sb4[rank]
        zero_lane = lax.broadcasted_iota(jnp.int32, (slab, columns), 1) == 0
        c_re = cross[0] + jnp.where(zero_lane, 0.0, cross[1])
        c_im = jnp.where(zero_lane, cross[1], cross[2])
        dk_width = jnp.dot(c_re, v.from_re[...], precision=PRECISE, preferred_element_type=F32)
        dk_width += jnp.dot(c_im, v.from_im[...], precision=PRECISE, preferred_element_type=F32)
        v.kt[...] = lax.dot_general(
            dk_width, v.pick[...], TN, precision=PRECISE, preferred_element_type=F32
        )

        def lag_height(l):
            at = pl.ds(l, 1)
            lag = jnp.sum(v.lags[l], axis=1, keepdims=True)
            v.kth[at, :] = jnp.sum(lag * v.pick[...], axis=0, keepdims=True)

        loop(RANKS, lag_height)
        parameters()

    def parameters():
        def moments(dk, e_re, e_im):
            place = lax.broadcasted_iota(jnp.int32, dk.shape, 0).astype(F32)
            terms = (dk * e_re, dk * e_im)
            plain = [jnp.sum(term, axis=0, keepdims=True) for term in terms]
            timed = [jnp.sum(term * place, axis=0, keepdims=True) for term in terms]
            return plain + timed

        rows_h = moments(v.kth[...], v.eh[0], v.eh[1])
        rows_w = moments(v.kt[...], v.ew[0], v.ew[1])
        p_re, p_im, t_re, t_im = (
            2.0 * jnp.concatenate([h, w], axis=0) for h, w in zip(rows_h, rows_w)
        )
        plain, timed = (p_re, p_im), (t_re, t_im)
        mv = mode_values(v.modes[...])
        step, rate = mv.step, mv.rate
        zoh_plain = times(mv.zoh, plain)
        g_b = times(mv.c, zoh_plain)
        g_c = times(mv.b, zoh_plain)
        coef_timed = times(mv.coef, timed)
        prod_plain = times(mv.prod, plain)
        slope = times(
            (step * mv.once[0] - mv.zoh[0], step * mv.once[1] - mv.zoh[1]), mv.over
        )
        g_rate = times(prod_plain, slope)
        g_rate = (g_rate[0] + step * coef_timed[0], g_rate[1] + step * coef_timed[1])
        g_step = times(prod_plain, mv.once)[0] + times(coef_timed, rate)[0]
        rows = [
            step * g_step,
            g_rate[0] * rate[0],
            -g_rate[1],
            g_b[0],
            -g_b[1],
            g_c[0],
            -g_c[1],
            jnp.zeros_like(step),
        ]
        table = jnp.concatenate(rows, axis=0)
        z, y, x = rank // 4, (rank // 2) % 2, rank % 2
        for five in range(3):
            block = jnp.zeros((per, 128), F32)
            for k in range(5 if five < 2 else 4):
                r = 5 * five + k
                at = lax.broadcasted_iota(jnp.int32, (128, lanes), 0) - k * own
                at = (at == lax.broadcasted_iota(jnp.int32, (128, lanes), 1) // per).astype(BF16)
                values = (v.of_mode[...] * table[r : r + 1]).astype(BF16)
                block += lax.dot_general(values, at, NT, preferred_element_type=F32)
            v.pack[five * per : (five + 1) * per, :] = block.astype(BF16)
        ones = jnp.ones((8, 128), F32)
        vectors = [
            v.dbu[m, 0:1, q * 128 : (q + 1) * 128] for m in range(chunks) for q in range(part // 128)
        ]
        for k in range(5):
            line = lax.dot_general(
                ones, v.sums[k], NT, precision=PRECISE, preferred_element_type=F32
            )
            vectors += [line[0:1, q * 128 : (q + 1) * 128] for q in range(here // 128)]
        vectors.append(jnp.zeros((32 - len(vectors), 128), F32))
        v.pack[3 * per :, :] = jnp.concatenate(vectors, axis=0).astype(BF16)
        v.gathered[z, y, x] = v.pack[...]

        def to(k):
            target = (lax.rem(z + k, 4) * 4 + y * 2 + x, core)
            copy(v.pack, v.gathered.at[z, y, x], v.ga, k, target).start()

        loop(4, to, 1)

    def gather_across():
        def wait(k):
            s = lax.rem(z + 4 - k, 4)
            copy(v.pack, v.gathered.at[s, y, x], v.ga, k, (s * 4 + y * 2 + x, core)).wait_recv()

        loop(4, wait, 1)
        mine = v.gathered.at[:, y, x]
        copy(mine, mine, v.ga, 4, across).start()

    def gather_beside():
        theirs = v.gathered.at[:, 1 - y, x]
        copy(theirs, theirs, v.ga, 4, across).wait_recv()
        mine = v.gathered.at[:, :, x]
        copy(mine, mine, v.ga, 5, beside).start()

    def token_grads():
        arrived(v.a4, lambda s: v.sb4.at[s], lambda s: v.rb4.at[s])

        def rows(d):
            at = pl.ds(pl.multiple_of(d * own, 8), own)
            conv = v.rb4[d].astype(F32)
            conv = jnp.concatenate([conv[:own], conv[own:]], axis=1)
            skip = wide(v.vb[0, core, at, :])
            v.res[at, :] = v.cot[at, :] + skip * v.gmix[at, :] + conv

        loop(RANKS, rows)
        for g in range(2):
            v.d_tokens[g, 0] = v.res[:, g * columns : (g + 1) * columns].T.astype(BF16)

    down = (v.pd, v.d1, v.d2, v.d3, v.d4, v.fd, v.d_sems.at[0], v.d_sems.at[1])
    up = (v.pu, v.u1, v.u2, v.u3, v.u4, v.fu, v.u_sems.at[0], v.u_sems.at[1])

    def leave(c):
        return (
            pltpu.make_async_copy(v.fd.at[c], v.down.at[c], v.leave.at[0, c]),
            pltpu.make_async_copy(v.fu.at[c], v.up.at[c], v.leave.at[1, c]),
        )

    events = {
        chunks: norm_back,
        chunks + 1: outputs,
        chunks + 3: convolve_back,
        chunks + 4: gather_across,
        chunks + 5: gather_beside,
        chunks + 6: token_grads,
    }

    def tick(t, carry):
        @pl.when(t < chunks)
        def _():
            feed(t)

        pl.when(t == chunks - 1)(share)
        for when, event in events.items():
            pl.when(t == when)(event)
        for stage in range(STAGES - 1, -1, -1):
            c = t - stage
            live = (c * (chunks - 1 - c) >= 0).astype(jnp.int32)
            role = live * (1 + middle)
            reduce_stage(stage, c, role, places, x, beside, across, down)
            reduce_stage(stage, c, role, places, y, across, beside, up)
            if stage == STAGES - 1:

                @pl.when(live > 0)
                def _():
                    for one in leave(c):
                        one.start()

        return carry

    lax.fori_loop(0, chunks + STAGES - 1, tick, 0)

    theirs = v.gathered.at[:, :, 1 - x]
    copy(theirs, theirs, v.ga, 5, beside).wait_recv()

    def left(c):
        for one in leave(c):
            one.wait()

    loop(chunks, left)
    scattered(v.a1, lambda d: v.tb.at[core, d], v.rb1.at[rank])
    scattered(v.a2, lambda d: v.sb2.at[d], v.rb2.at[core, rank])
    scattered(v.a3, lambda d: v.sb3.at[d], v.rb3.at[rank])
    scattered(v.a4, lambda d: v.sb4.at[d], v.rb4.at[rank])
    copy(v.tb.at[core], v.tb.at[core], v.tw, 0, twin).wait_send()
    copy(v.vx.at[core], v.vx.at[core], v.tw, 1, twin).wait_send()
    copy(v.gb.at[core], v.gb.at[core], v.tw, 2, twin).wait_send()
    copy(v.gn_out, v.gn_in, v.tw, 3, twin).wait_send()
    copy(v.br_out, v.br_in, v.tw, 4, twin).wait_send()

    def forward_sent(k):
        s = lax.rem(rank + RANKS - k, RANKS)
        copy(v.rb2.at[core, s], v.rb2.at[core, s], v.fw, k, twin).wait_send()

    loop(RANKS, forward_sent)

    def gather_sent(k):
        target = (lax.rem(z + k, 4) * 4 + y * 2 + x, core)
        copy(v.pack, v.gathered.at[z, y, x], v.ga, k, target).wait_send()

    loop(4, gather_sent, 1)
    mine = v.gathered.at[:, y, x]
    copy(mine, mine, v.ga, 4, across).wait_send()
    mine = v.gathered.at[:, :, x]
    copy(mine, mine, v.ga, 5, beside).wait_send()


def finish_kernel(own, down, up, gathered, output, d_tokens, *outs):
    d_w_down, d_w_up, output_out, d_tokens_out = outs[:4]
    d_log_step, d_log_decay, d_frequency, d_b_in, d_c_out = outs[4:9]
    d_w_down[...] = down[...].reshape(d_w_down.shape).astype(F32)
    d_w_up[...] = up[...].reshape(d_w_up.shape).astype(F32)
    per, here = d_log_decay.shape[1:]

    @pl.when(pl.program_id(0) == 0)
    def _():
        output_out[...] = output[...]
        d_tokens_out[...] = d_tokens[...]
        lane = lax.broadcasted_iota(jnp.int32, (per, 128), 1)
        whole = []
        for r in range(14):
            five, k = divmod(r, 5)
            windows = [jnp.zeros((per, 128), F32) for _ in range(here // 128)]
            for s in range(RANKS):
                block = gathered[s // 4, s // 2 % 2, s % 2, five * per : (five + 1) * per, :]
                turned = pltpu.roll(block.astype(F32), (own * (s - k)) % 128, 1)
                window, low = divmod(own * s, 128)
                inside = (lane >= low) & (lane < low + own)
                windows[window] = jnp.where(inside, turned, windows[window])
                if low + own > 128:
                    inside = lane < low + own - 128
                    windows[window + 1] = jnp.where(inside, turned, windows[window + 1])
            whole.append(jnp.concatenate(windows, axis=1))
        for a in range(2):
            d_log_step[a : a + 1, :] = jnp.sum(whole[a], axis=0, keepdims=True)
            d_log_decay[a] = whole[2 + a]
            d_frequency[a] = whole[4 + a]
            for i in range(2):
                d_b_in[a, i] = whole[6 + 2 * i + a]
                d_c_out[a, i] = whole[10 + 2 * i + a]
        sums = jnp.zeros((32, 128), F32)
        for s in range(RANKS):
            sums += gathered[s // 4, s // 2 % 2, s % 2, 3 * per :, :].astype(F32)
        row = 0
        for vector in outs[9:]:
            for q in range(vector.shape[0] // 128):
                vector[pl.ds(q * 128, 128)] = sums[row]
                row += 1


def block_shards(
    tokens,
    heights,
    widths,
    log_step,
    log_decay,
    frequency,
    b_in,
    c_out,
    skip_gain,
    ln_gain,
    ln_bias,
    w_up,
    b_up,
    w_down,
    b_down,
    layer_scale,
    cotangent,
):
    columns, here = tokens.shape[2:]
    modes_each = log_decay.shape[2]
    hidden = w_up.shape[1]
    own = here // RANKS
    chunks = hidden // 256
    part = hidden // chunks
    channels = 2 * here
    pixels = 2 * columns
    lanes = own * modes_each
    tables = spectral_tables(columns)
    slabs = (RANKS, 2 * own, columns)
    tall = pltpu.VMEM(slabs, F32)
    in_vmem = pl.BlockSpec(memory_space=pltpu.VMEM)
    in_smem = pl.BlockSpec(memory_space=pltpu.SMEM)
    anywhere = pl.BlockSpec(memory_space=pl.ANY)
    inputs = dict(
        tokens=(tokens, in_vmem),
        cotangent=(cotangent, in_vmem),
        heights=(heights, in_smem),
        widths=(widths, in_smem),
        log_step=(log_step, in_vmem),
        log_decay=(log_decay.swapaxes(-1, -2), in_vmem),
        frequency=(frequency.swapaxes(-1, -2), in_vmem),
        b_in=(b_in.swapaxes(-1, -2), in_vmem),
        c_out=(c_out.swapaxes(-1, -2), in_vmem),
        b_up=(b_up, in_vmem),
        skip_gain=(skip_gain, in_vmem),
        ln_gain=(ln_gain, in_vmem),
        ln_bias=(ln_bias, in_vmem),
        layer_scale=(layer_scale, in_vmem),
        b_down=(b_down, in_vmem),
        w_up=(w_up, anywhere),
        w_down=(w_down, anywhere),
        to_re=(tables[0], in_vmem),
        to_im=(tables[1], in_vmem),
        from_re=(tables[2], in_vmem),
        from_im=(tables[3], in_vmem),
    )
    down_shape = (chunks, 2, 2, part // 4, channels)
    up_shape = (chunks, 2, 2, channels // 4, part)
    outs = dict(
        output=(jax.ShapeDtypeStruct(tokens.shape, BF16), in_vmem),
        d_tokens=(jax.ShapeDtypeStruct(tokens.shape, BF16), in_vmem),
        down=(jax.ShapeDtypeStruct(down_shape, BF16), anywhere),
        up=(jax.ShapeDtypeStruct(up_shape, BF16), anywhere),
        gathered=(jax.ShapeDtypeStruct((4, 2, 2, 3 * modes_each + 32, 128), BF16), in_vmem),
    )
    low_slabs = pltpu.VMEM(slabs, BF16)
    both_slabs = pltpu.VMEM((2,) + slabs, BF16)
    scratch = dict(
        wu=pltpu.VMEM((chunks, channels, part), BF16),
        wd=pltpu.VMEM((chunks, part, channels), BF16),
        wut=pltpu.VMEM((chunks, part, channels), BF16),
        wdt=pltpu.VMEM((chunks, channels, part), BF16),
        tok=pltpu.VMEM((here, pixels), F32),
        cot=pltpu.VMEM((here, pixels), F32),
        gmix=pltpu.VMEM((here, pixels), F32),
        res=pltpu.VMEM((here, pixels), F32),
        tb=both_slabs,
        rb1=low_slabs,
        sb2=low_slabs,
        rb2=both_slabs,
        sb3=low_slabs,
        rb3=low_slabs,
        sb4=low_slabs,
        rb4=low_slabs,
        vx=pltpu.VMEM((2, 32, 128), F32),
        vb=pltpu.VMEM((5, 2, here, 128), F32),
        bias=pltpu.VMEM((chunks, part, 128), F32),
        inside=pltpu.VMEM((8, pixels), F32),
        inv=pltpu.VMEM((8, pixels), F32),
        gb=pltpu.VMEM((2, here, pixels), BF16),
        modes=pltpu.VMEM((16, lanes), F32),
        of_mode=pltpu.VMEM((modes_each, lanes), F32),
        pick=pltpu.VMEM((2 * own, lanes), F32),
        eh=pltpu.VMEM((2, RANKS, lanes), F32),
        ej=pltpu.VMEM((2, columns // 8, lanes), F32),
        ew=pltpu.VMEM((2, columns, lanes), F32),
        kt=pltpu.VMEM((columns, lanes), F32),
        kth=pltpu.VMEM((RANKS, lanes), F32),
        ks=pltpu.VMEM((3, 2 * own, columns), F32),
        kh=pltpu.VMEM((RANKS, 2 * own, 128), F32),
        xs=pltpu.VMEM((2,) + slabs, F32),
        along=tall,
        tall=tall,
        galong=tall,
        lags=tall,
        xhat=pltpu.VMEM((2 * RANKS, own, pixels), F32),
        normed=pltpu.VMEM((channels, pixels), BF16),
        branch=pltpu.VMEM((channels, pixels), F32),
        gn=pltpu.VMEM((channels, pixels), F32),
        gn_out=pltpu.VMEM((channels, pixels), BF16),
        gn_in=pltpu.VMEM((channels, pixels), BF16),
        br_out=pltpu.VMEM((here, pixels), BF16),
        br_in=pltpu.VMEM((here, pixels), BF16),
        dbu=pltpu.VMEM((chunks, 8, part), F32),
        sums=pltpu.VMEM((5, here, 128), F32),
        pack=pltpu.VMEM((3 * modes_each + 32, 128), BF16),
        fetch=pltpu.SemaphoreType.DMA((2, chunks)),
        leave=pltpu.SemaphoreType.DMA((2, chunks)),
    )

    def reduction(shape):
        count, halves, pieces, rows, width = shape
        whole = pltpu.VMEM(shape, BF16)
        half = pltpu.VMEM((count, pieces, rows, width), BF16)
        piece = pltpu.VMEM((count, rows, width), BF16)
        return whole, half, half, piece, piece, whole, pltpu.SemaphoreType.DMA((2, 9, count))

    down_scratch, up_scratch = reduction(down_shape), reduction(up_shape)
    scratch.update(
        zip(("pd", "d1", "d2", "d3", "d4", "fd", "d_sems"), down_scratch),
    )
    scratch.update(
        zip(("pu", "u1", "u2", "u3", "u4", "fu", "u_sems"), up_scratch),
    )
    several = pltpu.SemaphoreType.DMA((2, RANKS))
    scratch.update(a1=several, a2=several, a3=several, a4=several, fw=several)
    scratch.update(tw=pltpu.SemaphoreType.DMA((2, 5)), ga=pltpu.SemaphoreType.DMA((2, 6)))
    names = tuple(inputs) + tuple(outs) + tuple(scratch)
    output, d_tokens, down, up, gathered = pl.pallas_call(
        functools.partial(block_kernel, names),
        out_shape=tuple(shape for shape, _ in outs.values()),
        in_specs=[spec for _, spec in inputs.values()],
        out_specs=tuple(spec for _, spec in outs.values()),
        scratch_shapes=list(scratch.values()),
        compiler_params=pltpu.CompilerParams(
            collective_id=0, has_side_effects=True, vmem_limit_bytes=62 << 20
        ),
    )(*(value for value, _ in inputs.values()))
    def fixed(shape):
        return pl.BlockSpec(shape, lambda m, rank=len(shape): (0,) * rank)

    result = (
        jax.ShapeDtypeStruct((hidden, channels), F32),
        jax.ShapeDtypeStruct((channels, hidden), F32),
        output,
        d_tokens,
        log_step,
        jax.ShapeDtypeStruct((2, modes_each, here), F32),
        jax.ShapeDtypeStruct((2, modes_each, here), F32),
        jax.ShapeDtypeStruct((2, 2, modes_each, here), F32),
        jax.ShapeDtypeStruct((2, 2, modes_each, here), F32),
        b_up,
        skip_gain,
        ln_gain,
        ln_bias,
        b_down,
        layer_scale,
    )
    result = tuple(jax.ShapeDtypeStruct(one.shape, one.dtype) for one in result)
    (
        d_w_down,
        d_w_up,
        output,
        d_tokens,
        d_log_step,
        d_log_decay,
        d_frequency,
        d_b_in,
        d_c_out,
        d_b_up,
        d_skip_gain,
        d_ln_gain,
        d_ln_bias,
        d_b_down,
        d_layer_scale,
    ) = pl.pallas_call(
        functools.partial(finish_kernel, own),
        grid=(chunks,),
        out_shape=result,
        in_specs=[
            pl.BlockSpec((1,) + down_shape[1:], lambda m: (m, 0, 0, 0, 0)),
            pl.BlockSpec((1,) + up_shape[1:], lambda m: (m, 0, 0, 0, 0)),
            fixed(gathered.shape),
            fixed(tokens.shape),
            fixed(tokens.shape),
        ],
        out_specs=(
            pl.BlockSpec((part, channels), lambda m: (m, 0)),
            pl.BlockSpec((channels, part), lambda m: (0, m)),
        )
        + tuple(fixed(one.shape) for one in result[2:]),
        compiler_params=pltpu.CompilerParams(vmem_limit_bytes=62 << 20),
    )(down, up, gathered, output, d_tokens)
    return (
        output,
        d_tokens,
        d_log_step,
        d_log_decay.swapaxes(-1, -2),
        d_frequency.swapaxes(-1, -2),
        d_b_in.swapaxes(-1, -2),
        d_c_out.swapaxes(-1, -2),
        d_skip_gain,
        d_ln_gain,
        d_ln_bias,
        d_w_up,
        d_b_up,
        d_w_down,
        d_b_down,
        d_layer_scale,
    )


def shards(
    tokens,
    heights,
    widths,
    log_step,
    log_decay,
    frequency,
    b_in,
    c_out,
    skip_gain,
    ln_gain,
    ln_bias,
    w_up,
    b_up,
    w_down,
    b_down,
    layer_scale,
    cotangent,
):
    row_count = lax.axis_size("rows")
    row_rank = lax.axis_index("rows")
    grid_count, rows_here, columns, channels = tokens.shape
    all_channels = channels * lax.axis_size("ch")
    height = rows_here * row_count
    own_count = channels // row_count
    first_chan = row_rank * own_count
    pixels = grid_count * rows_here * columns
    token_f = tokens.astype(jnp.float32)
    width_tables = make_tables(columns)
    height_tables = make_tables(height)
    own_params = tuple(
        lax.dynamic_slice_in_dim(param, first_chan, own_count, param.ndim - trailing)
        for param, trailing in (
            (log_step, 1),
            (log_decay, 2),
            (frequency, 2),
            (b_in, 2),
            (c_out, 2),
        )
    )
    width_params = tuple(param[1] for param in own_params)
    height_params = tuple(param[0] for param in own_params)
    k_width, width_pull = jax.vjp(lambda params: make_kernel(params, columns), width_params)
    k_height, height_pull = jax.vjp(lambda params: make_kernel(params, height), height_params)
    kw_re, kw_im = kernel_spectrum(k_width, width_tables)
    kh_re, kh_im = kernel_spectrum(k_height, height_tables)
    kh_re = kh_re[:, None, :]
    kh_im = kh_im[:, None, :]
    pencil_tokens = lax.all_to_all(tokens, "rows", split_axis=3, concat_axis=1, tiled=True)
    x_re, x_im = to_spectrum(pencil_tokens.astype(jnp.float32), width_tables, "fw,grwc->grfc")
    along_width = from_spectrum(
        x_re * kw_re - x_im * kw_im, x_re * kw_im + x_im * kw_re, width_tables, "fw,grfc->grwc"
    ).astype(jnp.bfloat16)
    p_re, p_im = to_spectrum(along_width.astype(jnp.float32), height_tables, "fh,ghwc->gfwc")
    mixed_cols = from_spectrum(
        p_re * kh_re - p_im * kh_im, p_re * kh_im + p_im * kh_re, height_tables, "fh,gfwc->ghwc"
    ).astype(jnp.bfloat16)
    back_rows = lax.all_to_all(mixed_cols, "rows", split_axis=1, concat_axis=3, tiled=True)
    mixed = back_rows.astype(jnp.float32) + skip_gain * token_f
    flat_mixed = mixed.reshape(pixels, channels)
    sum_one, sum_two = lax.psum(
        (jnp.sum(flat_mixed, axis=1), jnp.sum(flat_mixed * flat_mixed, axis=1)), "ch"
    )
    centre = sum_one / all_channels
    spread = sum_two / all_channels - centre * centre
    inv_std = lax.rsqrt(spread + EPSILON)[:, None]
    x_hat = (flat_mixed - centre[:, None]) * inv_std
    normed = (x_hat * ln_gain + ln_bias).astype(jnp.bfloat16)
    hidden = (
        jnp.dot(
            lax.all_gather(normed, "ch", axis=1, tiled=True),
            w_up,
            preferred_element_type=jnp.float32,
        )
        + b_up
    )
    active = jax.nn.gelu(hidden, approximate=False).astype(jnp.bfloat16)
    partials = jnp.dot(active, w_down, preferred_element_type=jnp.float32)
    branch = (
        lax.psum_scatter(
            partials.astype(jnp.bfloat16), "ch", scatter_dimension=1, tiled=True
        ).astype(jnp.float32)
        + b_down
    )
    row_ids = row_rank * rows_here + jnp.arange(rows_here, dtype=jnp.int32)
    col_ids = jnp.arange(columns, dtype=jnp.int32)
    inside = (row_ids[None, :, None] < heights[:, None, None]) & (
        col_ids[None, None, :] < widths[:, None, None]
    )
    inside = inside.astype(jnp.float32).reshape(pixels, 1)
    flat_tokens = token_f.reshape(pixels, channels)
    output = (
        (flat_tokens + inside * layer_scale * branch).astype(jnp.bfloat16).reshape(tokens.shape)
    )
    over_rows = (((0,), (0,)), ((), ()))
    over_cols = (((1,), (1,)), ((), ()))
    g_flat = cotangent.astype(jnp.float32).reshape(pixels, channels)
    g_masked = g_flat * inside
    g_branch = (g_masked * layer_scale).astype(jnp.bfloat16)
    d_layer_scale = jnp.sum(g_masked * branch, axis=0)
    d_b_down = jnp.sum(g_branch.astype(jnp.float32), axis=0)
    g_branch_all = lax.all_gather(g_branch, "ch", axis=1, tiled=True)
    d_w_down = lax.dot_general(active, g_branch_all, over_rows, preferred_element_type=jnp.float32)
    g_active = lax.dot_general(g_branch_all, w_down, over_cols, preferred_element_type=jnp.float32)
    gelu_pull = jax.vjp(lambda values: jax.nn.gelu(values, approximate=False), hidden)[1]
    g_hidden = gelu_pull(g_active)[0].astype(jnp.bfloat16)
    d_b_up = jnp.sum(g_hidden.astype(jnp.float32), axis=0)
    d_w_up = lax.dot_general(
        lax.all_gather(normed, "ch", axis=1, tiled=True),
        g_hidden,
        over_rows,
        preferred_element_type=jnp.float32,
    )
    g_terms = lax.dot_general(g_hidden, w_up, over_cols, preferred_element_type=jnp.float32)
    g_normed = lax.psum_scatter(g_terms, "ch", scatter_dimension=1, tiled=True)
    d_ln_gain = jnp.sum(g_normed * x_hat, axis=0)
    d_ln_bias = jnp.sum(g_normed, axis=0)
    g_hat = g_normed * ln_gain
    sum_grad, sum_cross = lax.psum((jnp.sum(g_hat, axis=1), jnp.sum(g_hat * x_hat, axis=1)), "ch")
    g_mixed = inv_std * (
        g_hat - sum_grad[:, None] / all_channels - x_hat * sum_cross[:, None] / all_channels
    )
    d_skip_gain = jnp.sum(g_mixed * flat_tokens, axis=0)
    g_spatial = g_mixed.astype(jnp.bfloat16).reshape(tokens.shape)
    pencil_grad = lax.all_to_all(g_spatial, "rows", split_axis=3, concat_axis=1, tiled=True)
    gp_re, gp_im = to_spectrum(pencil_grad.astype(jnp.float32), height_tables, "fh,ghwc->gfwc")
    vp_re, vp_im = p_re, p_im
    g_pencil_along = from_spectrum(
        gp_re * kh_re + gp_im * kh_im, gp_im * kh_re - gp_re * kh_im, height_tables, "fh,gfwc->ghwc"
    ).astype(jnp.bfloat16)
    cross_re = jnp.sum(vp_re * gp_re + vp_im * gp_im, axis=(0, 2))
    cross_im = jnp.sum(vp_re * gp_im - vp_im * gp_re, axis=(0, 2))
    dk_height = kernel_from_cross(cross_re, cross_im, height_tables)
    g_along = g_pencil_along
    ga_re, ga_im = to_spectrum(g_along.astype(jnp.float32), width_tables, "fw,grwc->grfc")
    g_conv = from_spectrum(
        ga_re * kw_re + ga_im * kw_im, ga_im * kw_re - ga_re * kw_im, width_tables, "fw,grfc->grwc"
    )
    g_conv = lax.all_to_all(
        g_conv.astype(jnp.bfloat16), "rows", split_axis=1, concat_axis=3, tiled=True
    ).astype(jnp.float32)
    wide_re = jnp.sum(x_re * ga_re + x_im * ga_im, axis=(0, 1))
    wide_im = jnp.sum(x_re * ga_im - x_im * ga_re, axis=(0, 1))
    dk_width = kernel_from_cross(wide_re, wide_im, width_tables)
    d_tokens = ((g_flat + g_mixed * skip_gain).reshape(tokens.shape) + g_conv).astype(jnp.bfloat16)
    width_grads = width_pull(dk_width)[0]
    height_grads = height_pull(dk_height)[0]

    def gathered(pieces, dim_num):
        return lax.all_gather(jnp.stack(pieces), "rows", axis=dim_num, tiled=True)

    param_grads = tuple(
        gathered(pair, dim_num)
        for pair, dim_num in zip(zip(height_grads, width_grads), (1, 1, 1, 2, 2))
    )
    d_w_down, d_w_up, d_skip_gain, d_ln_gain, d_ln_bias, d_b_up, d_b_down, d_layer_scale = lax.psum(
        (d_w_down, d_w_up, d_skip_gain, d_ln_gain, d_ln_bias, d_b_up, d_b_down, d_layer_scale),
        "rows",
    )
    return (output, d_tokens) + param_grads + (
        d_skip_gain,
        d_ln_gain,
        d_ln_bias,
        d_w_up,
        d_b_up,
        d_w_down,
        d_b_down,
        d_layer_scale,
    )


def solution(mesh):
    one_row_each = mesh.shape["rows"] == RANKS and mesh.shape["ch"] == 2
    return jax.shard_map(
        block_shards if one_row_each else shards,
        mesh=mesh,
        in_specs=(
            P(None, "rows", None, "ch"),
            P(),
            P(),
            P(None, "ch"),
            P(None, "ch", None),
            P(None, "ch", None),
            P(None, None, "ch", None),
            P(None, None, "ch", None),
            P("ch"),
            P("ch"),
            P("ch"),
            P(None, "ch"),
            P("ch"),
            P("ch", None),
            P("ch"),
            P("ch"),
            P(None, "rows", None, "ch"),
        ),
        out_specs=(
            P(None, "rows", None, "ch"),
            P(None, "rows", None, "ch"),
            P(None, "ch"),
            P(None, "ch", None),
            P(None, "ch", None),
            P(None, None, "ch", None),
            P(None, None, "ch", None),
            P("ch"),
            P("ch"),
            P("ch"),
            P(None, "ch"),
            P("ch"),
            P("ch", None),
            P("ch"),
            P("ch"),
        ),
        check_vma=False,
    )
```

```python
import functools
import types

import jax
import jax.numpy as jnp
import numpy as np
from jax import lax
from jax.experimental import pallas as pl
from jax.experimental.pallas import tpu as pltpu
from jax.sharding import PartitionSpec as P

PRECISE = lax.Precision.HIGHEST
EPSILON = 1e-06
MESH = pl.DeviceIdType.MESH


def make_tables(length):
    freq_ids = jnp.arange(length + 1, dtype=jnp.int32)[:, None]
    places = jnp.arange(length, dtype=jnp.int32)[None, :]
    turns = freq_ids * places % (2 * length)
    angles = turns.astype(jnp.float32) * (jnp.pi / length)
    cosine = jnp.cos(angles)
    sine_t = jnp.sin(angles)
    weights = jnp.where((freq_ids == 0) | (freq_ids == length), 1.0, 2.0) / (2.0 * length)
    return (cosine, sine_t, cosine * weights, sine_t * weights)


def to_spectrum(values, tables, pattern):
    real_part = jnp.einsum(pattern, tables[0], values, precision=PRECISE)
    imag_part = -jnp.einsum(pattern, tables[1], values, precision=PRECISE)
    return (real_part, imag_part)


def from_spectrum(real_part, imag_part, tables, pattern):
    return jnp.einsum(pattern, tables[2], real_part, precision=PRECISE) - jnp.einsum(
        pattern, tables[3], imag_part, precision=PRECISE
    )


def kernel_spectrum(kernel, tables):
    real_part = jnp.dot(tables[0], kernel, precision=PRECISE)
    imag_part = -jnp.dot(tables[1], kernel, precision=PRECISE)
    return (real_part, imag_part)


def kernel_from_cross(cross_re, cross_im, tables):
    contract = (((0,), (0,)), ((), ()))
    return lax.dot_general(tables[2], cross_re, contract, precision=PRECISE) - lax.dot_general(
        tables[3], cross_im, contract, precision=PRECISE
    )


def make_kernel(params, length):
    log_step, log_decay, frequency, b_in, c_out = params
    step_size = jnp.exp(log_step)[:, None]
    decay_re = -jnp.exp(log_decay)
    step_re = step_size * decay_re
    step_im = step_size * frequency
    half_sin = jnp.sin(0.5 * step_im)
    num_re = jnp.expm1(step_re) * jnp.cos(step_im) - 2.0 * half_sin * half_sin
    num_im = jnp.exp(step_re) * jnp.sin(step_im)
    divisor = decay_re * decay_re + frequency * frequency
    zoh_re = (num_re * decay_re + num_im * frequency) / divisor
    zoh_im = (num_im * decay_re - num_re * frequency) / divisor
    prod_re = b_in[0] * c_out[0] - b_in[1] * c_out[1]
    prod_im = b_in[0] * c_out[1] + b_in[1] * c_out[0]
    coef_re = prod_re * zoh_re - prod_im * zoh_im
    coef_im = prod_re * zoh_im + prod_im * zoh_re
    places = jnp.arange(length, dtype=jnp.float32)[:, None, None]
    fading = jnp.exp(step_re[None] * places)
    turning = step_im[None] * places
    return 2.0 * jnp.sum(fading * (coef_re * jnp.cos(turning) - coef_im * jnp.sin(turning)), axis=2)


RANKS = 16
STAGES = 10
CUTS = 2
ASYNC = (
    ("cotangent_in", "cotangent"),
    ("log_step_in", "log_step"),
    ("log_decay_in", "log_decay"),
    ("frequency_in", "frequency"),
    ("b_in_in", "b_in"),
    ("c_out_in", "c_out"),
    ("to_hi_in", "to_hi"),
    ("to_lo_in", "to_lo"),
    ("from_hi_in", "from_hi"),
    ("from_lo_in", "from_lo"),
)
BF16 = jnp.bfloat16
F32 = jnp.float32
NT = (((1,), (1,)), ((), ()))
TN = (((0,), (0,)), ((), ()))


def spectral_tables(length):
    turns = np.outer(np.arange(length), np.arange(length)) % (2 * length)
    cosine = np.cos(np.pi * turns / length)
    sine = np.sin(np.pi * turns / length)
    sign = np.where(np.arange(length) % 2, -1.0, 1.0)
    to_re, to_im = cosine.copy(), -sine
    to_im[:, 0] = sign
    from_re, from_im = cosine / length, -sine / length
    from_re[0] /= 2
    from_im[0] = sign / (2 * length)
    tables = []
    for table in (np.concatenate([to_re, to_im], 1), np.concatenate([from_re, from_im], 0)):
        high = table.astype(BF16)
        tables += [high, (table - high.astype(np.float64)).astype(BF16)]
    return tuple(tables)


def by_table(values, high, low):
    def dot(a, b):
        return jnp.dot(a, b[...], preferred_element_type=F32)

    if values.dtype == BF16:
        return dot(values, high) + dot(values, low)
    first = values.astype(BF16)
    second = (values - first.astype(F32)).astype(BF16)
    return dot(first, high) + (dot(first, low) + dot(second, high))


def times(a, b):
    return a[0] * b[0] - a[1] * b[1], a[0] * b[1] + a[1] * b[0]


def up_cut(shape, q):
    rows, cols = shape[0] * 2 // CUTS, shape[1] // 2
    return (
        slice(q // 2 * rows, (q // 2 + 1) * rows),
        slice(q % 2 * cols, (q % 2 + 1) * cols),
    )


def reduce_stage(stage, c, role, places, lines, send, recv):
    near, inner, outer = places
    far = 1 - near

    def start(kind, src, dst, target):
        pltpu.make_async_remote_copy(
            src_ref=src,
            dst_ref=dst,
            send_sem=send.at[kind],
            recv_sem=recv.at[kind, c],
            device_id=target,
            device_id_type=MESH,
        ).start()

    def landed(kind, ref):
        pltpu.make_async_copy(ref, ref, recv.at[kind, c]).wait()

    halves = lines[0].part.at[c]
    quarters = lines[0].from_first.at[c]

    def added(*refs):
        total = refs[0][...].astype(F32)
        for ref in refs[1:]:
            total = total + ref[...].astype(F32)
        return total.astype(BF16)

    def give(kind, which, target):
        for line in lines:
            place = line.full.at[c, line.keep, which]
            start(kind, place, place, target)

    def give_back():
        for line in lines:
            place = line.full.at[c, line.keep]
            start(8, place, place, line.first)

    if stage == 0:

        @pl.when(role > 0)
        def _():
            for line in lines:
                start(0, line.part.at[c, 1 - line.keep], line.from_first.at[c], line.first)

    elif stage == 1:

        @pl.when(role > 0)
        def _():
            landed(0, halves)
            for line in lines:
                line.part[c, line.keep] = added(line.part.at[c, line.keep], line.from_first.at[c])

        @pl.when(role == 1)
        def _():
            for line in lines:
                start(1, line.part.at[c, line.keep, far], line.from_outer.at[c], inner)

    elif stage == 2:

        @pl.when(role == 2)
        def _():
            landed(1, quarters)
            for line in lines:
                mine = line.part.at[c, line.keep, far]
                mine[...] = added(mine, line.from_outer.at[c])
                start(2, mine, line.from_inner.at[c], inner)

    elif stage == 3:

        @pl.when(role == 2)
        def _():
            landed(2, quarters)
            for line in lines:
                mine = line.part.at[c, line.keep, near]
                mine[...] = added(mine, line.from_inner.at[c])
                start(3, mine, line.from_inner.at[c], outer)

    elif stage == 4:

        @pl.when(role == 1)
        def _():
            landed(3, quarters)
            for line in lines:
                mine = line.part.at[c, line.keep, near]
                mine[...] = added(mine, line.from_inner.at[c])
                start(4, mine, line.from_third.at[c], line.third)

    elif stage == 5:

        @pl.when(role == 1)
        def _():
            landed(4, quarters)
            for line in lines:
                mine = line.part.at[c, line.keep, near]
                line.full[c, line.keep, near] = added(mine, line.from_third.at[c])
            give(5, near, inner)

    elif stage == 6:

        @pl.when(role == 2)
        def _():
            landed(5, quarters)
            give(6, near, inner)

    elif stage == 7:

        @pl.when(role == 2)
        def _():
            landed(6, quarters)
            give(7, far, outer)
            give_back()

    elif stage == 8:

        @pl.when(role == 1)
        def _():
            landed(7, quarters)
            give_back()

    else:

        @pl.when(role > 0)
        def _():
            landed(8, halves)


def reduce_sent(middle, lines, send):
    halves, quarters = lines[0].part, lines[0].from_first

    def gone(kinds):
        for kind in kinds:
            ref = halves if kind in (0, 8) else quarters
            pltpu.make_async_copy(ref, ref, send.at[kind]).wait()

    gone((0, 8))

    @pl.when(middle == 0)
    def _():
        gone((1, 4, 5))

    @pl.when(middle == 1)
    def _():
        gone((2, 3, 6, 7))


def mode_values(modes):
    log_step, log_decay, freq, b_re, b_im, c_re, c_im = (modes[2 * q : 2 * q + 2] for q in range(7))
    step = jnp.exp(log_step)
    decay = -jnp.exp(log_decay)
    step_re = step * decay
    step_im = step * freq
    half_sin = jnp.sin(0.5 * step_im)
    series = jnp.ones_like(step_re)
    for order in range(11, 1, -1):
        series = 1.0 + series * step_re * (1.0 / order)
    grown = jnp.exp(step_re)
    less_one = jnp.where(step_re > -0.5, step_re * series, grown - 1.0)
    num_re = less_one * jnp.cos(step_im) - 2.0 * half_sin * half_sin
    num_im = grown * jnp.sin(step_im)
    inverse = 1.0 / (decay * decay + freq * freq)
    over = (decay * inverse, -freq * inverse)
    zoh = times((num_re, num_im), over)
    b, c = (b_re, b_im), (c_re, c_im)
    prod = times(b, c)
    return types.SimpleNamespace(
        step=step,
        rate=(decay, freq),
        over=over,
        step_re=step_re,
        step_im=step_im,
        once=(num_re + 1.0, num_im),
        zoh=zoh,
        b=b,
        c=c,
        prod=prod,
        coef=times(prod, zoh),
    )


def block_kernel(names, *refs):
    v = types.SimpleNamespace(**dict(zip(names, refs)))
    rank, core = lax.axis_index("rows"), lax.axis_index("ch")
    x, y, z = rank % 2, (rank // 2) % 2, rank // 4
    near = z // 2
    toward = 4 * (2 * near - 1)
    middle = jnp.minimum(z * (3 - z), 1)
    beside, across = (rank + 1 - 2 * x, core), (rank + 2 - 4 * y, core)
    places = (near, (rank - toward, core), (rank + toward, core))
    twin = (rank, 1 - core)
    heights, widths = v.heights, v.widths
    chunks, part = v.wd.shape[0], v.wd.shape[1]
    pieces = CUTS * chunks
    slab, columns = v.rb1.shape[1:]
    own = slab // 2
    here = own * RANKS
    pixels = 2 * columns
    per = v.log_decay.shape[1]
    lanes = own * per

    def copy(src, dst, sems, index, target):
        return pltpu.make_async_remote_copy(
            src_ref=src,
            dst_ref=dst,
            send_sem=sems.at[0, index],
            recv_sem=sems.at[1, index],
            device_id=target,
            device_id_type=MESH,
        )

    def loop(count, body, start=0):
        def step(i, carry):
            body(i)
            return carry

        lax.fori_loop(start, count, step, 0)

    def wide(column):
        return jnp.concatenate([column] * (pixels // column.shape[1]), axis=1)

    def partner(k):
        return rank ^ lax.rem(7 * k, RANKS)

    def slab_copy(sems, index, src, dst, d):
        return pltpu.make_async_remote_copy(
            src_ref=src,
            dst_ref=dst,
            send_sem=sems.at[0, 0],
            recv_sem=sems.at[1, index],
            device_id=(d, core),
            device_id_type=MESH,
        )

    def scatter(sems, src, dst, each=False, first=1, count=RANKS - 1):
        def start(k):
            d = partner(k)

            @pl.when(k < RANKS)
            def _():
                slab_copy(sems, k if each else 0, src.at[d], dst, d).start()

        loop(first + count, start, first)

    def all_slabs(sems, which, ref):
        most = ref.at[pl.ds(0, RANKS - 1)]
        pltpu.make_async_copy(most, most, sems.at[which, 0]).wait()

    def bring(which):
        far_ref, near_ref = ASYNC[which]
        return pltpu.make_async_copy(getattr(v, far_ref), getattr(v, near_ref), v.bring.at[which])

    barrier = pltpu.get_barrier_semaphore()

    def greet(k):
        pl.semaphore_signal(
            barrier, inc=1, device_id=(lax.rem(rank + k, RANKS), core), device_id_type=MESH
        )

    loop(RANKS, greet, 1)
    pl.semaphore_signal(barrier, inc=1, device_id=twin, device_id_type=MESH)

    def fetch_up(m):
        cols = pl.ds(pl.multiple_of(m * part, part), part)
        return pltpu.make_async_copy(v.w_up.at[:, cols], v.wu.at[m], v.fetch.at[0])

    def fetch_down(m):
        rows = pl.ds(pl.multiple_of(m * part, part), part)
        return pltpu.make_async_copy(v.w_down.at[rows], v.wd.at[m], v.fetch.at[1])

    def fetch(m):
        fetch_up(m).start()
        fetch_down(m).start()


    for g in range(2):
        v.tok[:, g * columns : (g + 1) * columns] = v.tokens[g, 0].astype(F32).T

    def cut_tokens(d):
        rows = v.tok[pl.ds(pl.multiple_of(d * own, 8), own), :]
        both = jnp.concatenate([rows[:, :columns], rows[:, columns:]], axis=0)
        v.tb[core, d] = both.astype(BF16)

    loop(RANKS, cut_tokens)
    lines = []
    for vector in (v.b_up, v.skip_gain, v.ln_gain, v.ln_bias, v.layer_scale, v.b_down):
        line = vector[...].reshape(1, vector.shape[0])
        lines += [line[:, q * 128 : (q + 1) * 128] for q in range(vector.shape[0] // 128)]
    lines.append(jnp.zeros((32 - len(lines), 128), F32))
    v.vx[core] = jnp.concatenate(lines, axis=0)
    pl.semaphore_wait(barrier, RANKS)
    scatter(v.a1, v.tb.at[core], v.rb1.at[rank])
    v.rb1[rank] = v.tb[core, rank]
    for which in range(len(ASYNC)):
        bring(which).start()
    loop(chunks, fetch)
    copy(v.tb.at[core], v.tb.at[core], v.tw, 0, twin).start()
    copy(v.vx.at[core], v.vx.at[core], v.tw, 1, twin).start()

    def spread(which, rows):
        block = jnp.concatenate([rows, jnp.zeros((128 - rows.shape[0], 128), F32)], axis=0)
        cols = block.T
        for q in range(15):
            v.vb[q // 3, which, q % 3 * 128 : (q % 3 + 1) * 128, :] = jnp.broadcast_to(
                cols[:, 12 + q : 13 + q], (128, 128)
            )
        return cols

    cols = spread(core, v.vx[core])
    for m in range(chunks):
        for q in range(2):
            v.bias[m, q * 128 : (q + 1) * 128, :] = jnp.broadcast_to(
                cols[:, 2 * m + q : 2 * m + q + 1], (128, 128)
            )
    for which in range(len(ASYNC)):
        bring(which).wait()
    for g in range(2):
        v.cot[:, g * columns : (g + 1) * columns] = v.cotangent[g, 0].astype(F32).T
    places_w = lax.broadcasted_iota(jnp.int32, (1, columns), 1)
    inside = jnp.concatenate(
        [(places_w < jnp.where(rank < heights[g], widths[g], 0)).astype(F32) for g in range(2)],
        axis=1,
    )
    v.inside[...] = jnp.broadcast_to(inside, (8, pixels))

    def mask_rows(q):
        rows = pl.ds(pl.multiple_of(q * 128, 128), 128)
        masked = v.cot[rows, :] * v.inside[0:1, :]
        v.gb[core, rows, :] = (masked * wide(v.vb[3, core, rows, :])).astype(BF16)

    loop(here // 128, mask_rows)
    copy(v.gb.at[core], v.gb.at[core], v.tw, 2, twin).start()

    lane = lax.broadcasted_iota(jnp.int32, (slab, lanes), 1) // per
    row = lax.broadcasted_iota(jnp.int32, (slab, lanes), 0)
    row = jnp.where(row >= own, row - own, row)
    v.pick[...] = (lane == row).astype(F32)
    chosen = lax.broadcasted_iota(jnp.int32, (here, lanes), 1) // per + rank * own
    chosen = (lax.broadcasted_iota(jnp.int32, (here, lanes), 0) == chosen).astype(F32)
    all_modes = jnp.concatenate(
        [v.log_step[...], jnp.zeros((6, here), F32)]
        + [v.log_decay[a] for a in range(2)]
        + [v.frequency[a] for a in range(2)]
        + [v.b_in[a, i] for i in range(2) for a in range(2)]
        + [v.c_out[a, i] for i in range(2) for a in range(2)],
        axis=0,
    )
    all_modes = jnp.dot(all_modes, chosen, precision=PRECISE, preferred_element_type=F32)
    mode = lax.broadcasted_iota(jnp.int32, (per, lanes), 1) % per
    mode = (mode == lax.broadcasted_iota(jnp.int32, (per, lanes), 0)).astype(F32)
    v.of_mode[...] = mode
    own_modes = jnp.sum(all_modes[8:].reshape(12, per, lanes) * mode[None], axis=1)
    v.modes[...] = jnp.concatenate([all_modes[:2], own_modes, own_modes[:2]], axis=0)
    mv = mode_values(v.modes[...])

    def powers(axis, place):
        angle = mv.step_im[axis : axis + 1] * place
        fade = jnp.exp(mv.step_re[axis : axis + 1] * place)
        return fade * jnp.cos(angle), fade * jnp.sin(angle)

    high_place = lax.broadcasted_iota(jnp.int32, (RANKS, lanes), 0).astype(F32)
    v.eh[0], v.eh[1] = powers(0, high_place)
    low_place = lax.broadcasted_iota(jnp.int32, (8, lanes), 0).astype(F32)
    base = powers(1, low_place)
    many = columns // 8
    v.ej[0], v.ej[1] = powers(
        1, 8.0 * lax.broadcasted_iota(jnp.int32, (many, lanes), 0).astype(F32)
    )
    coef_w = tuple(2.0 * part_of[1:2] for part_of in mv.coef)

    def fill(j):
        at = pl.ds(pl.multiple_of(j * 8, 8), 8)
        jump = (v.ej[0, pl.ds(j, 1), :], v.ej[1, pl.ds(j, 1), :])
        e_re, e_im = times(base, jump)
        v.ew[0, at, :] = e_re
        v.ew[1, at, :] = e_im
        v.kt[at, :] = coef_w[0] * e_re - coef_w[1] * e_im

    loop(many, fill)
    k_width = lax.dot_general(
        v.pick[...], v.kt[...], NT, precision=PRECISE, preferred_element_type=F32
    )
    k_both = by_table(k_width, v.to_hi, v.to_lo)
    k_re, k_im = k_both[:, :columns], k_both[:, columns:]
    first_lane = lax.broadcasted_iota(jnp.int32, (slab, columns), 1) == 0
    v.ks[0] = k_re
    v.ks[1] = jnp.where(first_lane, 0.0, k_im)
    v.ks[2] = jnp.where(first_lane, k_im, k_re)
    coef_h = tuple(2.0 * part_of[0:1] for part_of in mv.coef)
    v.kt[0:RANKS, :] = coef_h[0] * v.eh[0] - coef_h[1] * v.eh[1]

    taps = lax.dot_general(
        v.pick[...], v.kt[0:RANKS, :], NT, precision=PRECISE, preferred_element_type=F32
    )
    for l in range(RANKS):
        v.kh[l] = jnp.broadcast_to(taps[:, l : l + 1], (slab, 128))

    pltpu.make_async_copy(v.wu, v.wu, v.fetch.at[0]).wait()
    pltpu.make_async_copy(v.wd, v.wd, v.fetch.at[1]).wait()

    def turn(m):
        v.wut[m] = v.wu[m].T
        v.wdt[m] = v.wd[m].T

    loop(chunks // 2, turn)

    all_slabs(v.a1, 1, v.rb1)
    step_rows = 4

    def convolve(b):
        at = pl.ds(b * step_rows, step_rows)
        values = v.rb1[at].reshape(step_rows * slab, columns)
        shape = (step_rows, slab, columns)
        x_both = by_table(values, v.to_hi, v.to_lo)
        x_re, x_im = x_both[:, :columns].reshape(shape), x_both[:, columns:].reshape(shape)
        v.xs[0, at] = x_re
        v.xs[1, at] = x_im
        k0, k1, k2 = v.ks[0], v.ks[1], v.ks[2]
        y_both = jnp.concatenate([x_re * k0 - x_im * k1, x_re * k1 + x_im * k2], axis=2)
        y_both = y_both.reshape(step_rows * slab, 2 * columns)
        along = by_table(y_both, v.from_hi, v.from_lo)
        v.along[at] = along.astype(BF16).astype(F32).reshape(shape)

    loop(RANKS // step_rows, convolve)

    def by_tiles(body):
        def rows(r):
            for half in range(columns // 128):
                body(pl.ds(pl.multiple_of(r * 8, 8), 8), slice(half * 128, half * 128 + 128))

        loop(slab // 8, rows)

    def down_rows(at, cut):
        taps = [v.kh[l, at, :] for l in range(RANKS)]
        values = [v.along[i, at, cut] for i in range(RANKS)]
        for i in range(RANKS):
            total = taps[0] * values[i]
            for l in range(1, i + 1):
                total += taps[l] * values[i - l]
            v.tall[i, at, cut] = total

    by_tiles(down_rows)
    v.sb2[...] = v.tall[...].astype(BF16)
    scatter(v.a2, v.sb2, v.rb2.at[core, rank], each=True)
    v.rb2[core, rank] = v.sb2[rank]
    copy(v.rb2.at[core, rank], v.rb2.at[core, rank], v.fw, 0, twin).start()

    copy(v.vx.at[core], v.vx.at[1 - core], v.tw, 1, twin).wait_recv()
    spread(1 - core, v.vx[1 - core])
    loop(chunks, turn, chunks // 2)
    v.branch[...] = jnp.zeros_like(v.branch)
    v.gn[...] = jnp.zeros_like(v.gn)

    def forward(k):
        d = partner(k)
        slab_copy(v.a2, k, v.sb2.at[d], v.rb2.at[core, d], d).wait_recv()
        copy(v.rb2.at[core, d], v.rb2.at[core, d], v.fw, 0, twin).start()

    loop(RANKS, forward, 1)
    copy(v.tb.at[core], v.tb.at[1 - core], v.tw, 0, twin).wait_recv()
    copy(v.rb2.at[core], v.rb2.at[1 - core], v.fw, 0, twin).wait_recv()

    eight = jnp.zeros((8, pixels), F32)

    def folded(values):
        return values.reshape(own // 8, 8, pixels).sum(axis=0)

    def mix(i, total):
        which, d = i // RANKS, lax.rem(i, RANKS)
        spatial = v.rb2[which, d].astype(F32)
        token = v.tb[which, d].astype(F32)
        skip = wide(v.vb[0, which, pl.ds(pl.multiple_of(d * own, 8), own), :])
        spatial = jnp.concatenate([spatial[:own], spatial[own:]], axis=1)
        token = jnp.concatenate([token[:own], token[own:]], axis=1)
        mixed = spatial + skip * token
        v.xhat[i] = mixed
        return total + folded(mixed)

    channels = 2 * here
    total = lax.fori_loop(0, 2 * RANKS, mix, eight)
    centre = jnp.sum(total, axis=0, keepdims=True) * (1.0 / channels)

    def squares(i, total):
        off = v.xhat[i] - centre
        return total + folded(off * off)

    total = lax.fori_loop(0, 2 * RANKS, squares, eight)
    spread_of = jnp.sum(total, axis=0, keepdims=True) * (1.0 / channels)
    inv_std = lax.rsqrt(spread_of + EPSILON)
    v.inv[...] = jnp.broadcast_to(inv_std, (8, pixels))

    def normalize(q):
        rows = []
        for k in range(2):
            i = 2 * q + k
            which, d = i // RANKS, lax.rem(i, RANKS)
            at = pl.ds(pl.multiple_of(d * own, 8), own)
            x_hat = (v.xhat[i] - centre) * inv_std
            v.xhat[i] = x_hat
            rows.append(x_hat * wide(v.vb[1, which, at, :]) + wide(v.vb[2, which, at, :]))
        at = pl.ds(pl.multiple_of(q * 2 * own, 16), 2 * own)
        v.normed[at, :] = jnp.concatenate(rows, axis=0).astype(BF16)

    loop(RANKS, normalize)
    copy(v.gb.at[core], v.gb.at[1 - core], v.tw, 2, twin).wait_recv()

    def feed(t):
        normed = v.normed[...]
        g_branch = v.gb[...].reshape(channels, pixels)
        hidden = jnp.dot(v.wut[t], normed, preferred_element_type=F32) + wide(v.bias[t])
        phi = 0.5 + 0.5 * lax.erf(hidden * (0.5**0.5))
        density = jnp.exp(-0.5 * hidden * hidden) * ((2.0 * jnp.pi) ** -0.5)
        active = (hidden * phi).astype(BF16)
        slope = phi + hidden * density
        g_active = jnp.dot(v.wd[t], g_branch, preferred_element_type=F32)
        g_hidden = (g_active * slope).astype(BF16)
        down = lax.dot_general(active, g_branch, NT, preferred_element_type=F32)
        down = down.astype(BF16).reshape(CUTS, 2, 2, part // CUTS // 4, channels)
        v.pd[pl.ds(CUTS * t, CUTS)] = down
        up = lax.dot_general(normed, g_hidden, NT, preferred_element_type=F32)
        up = up.astype(BF16)
        for q in range(CUTS):
            v.pu[CUTS * t + q] = up[up_cut(up.shape, q)].reshape(v.pu.shape[1:])
        v.gn[...] += jnp.dot(v.wu[t], g_hidden, preferred_element_type=F32)
        v.branch[...] += jnp.dot(v.wdt[t], active, preferred_element_type=F32)
        ones = jnp.ones((8, pixels), BF16)
        v.dbu[t] = lax.dot_general(ones, g_hidden, NT, preferred_element_type=F32)

    def share():
        v.gn_out[...] = v.gn[...].astype(BF16)
        copy(v.gn_out, v.gn_in, v.tw, 3, twin).start()
        theirs = pl.ds(pl.multiple_of((1 - core) * here, here), here)
        v.br_out[...] = v.branch[theirs, :].astype(BF16)
        copy(v.br_out, v.br_in, v.tw, 4, twin).start()

    def lane_sum(values):
        return sum(values[:, q * 128 : (q + 1) * 128] for q in range(pixels // 128))

    def norm_back():
        copy(v.gn_out, v.gn_in, v.tw, 3, twin).wait_recv()

        def whole(q, totals):
            at = pl.ds(pl.multiple_of(q * 2 * own, 16), 2 * own)
            g_normed = v.gn[at, :] + v.gn_in[at, :].astype(F32)
            v.gn[at, :] = g_normed
            one, two = totals
            for k in range(2):
                i = 2 * q + k
                which, d = i // RANKS, lax.rem(i, RANKS)
                gain = wide(v.vb[1, which, pl.ds(pl.multiple_of(d * own, 8), own), :])
                g_hat = g_normed[k * own : (k + 1) * own] * gain
                one = one + folded(g_hat)
                two = two + folded(g_hat * v.xhat[i])
            return one, two

        one, two = lax.fori_loop(0, RANKS, whole, (eight, eight))
        one = jnp.sum(one, axis=0, keepdims=True) * (1.0 / channels)
        two = jnp.sum(two, axis=0, keepdims=True) * (1.0 / channels)
        scale = v.inv[0:1, :]

        def each(d):
            at = pl.ds(pl.multiple_of(d * own, 8), own)
            x_hat = v.xhat[core * RANKS + d]
            g_normed = v.gn[pl.ds(pl.multiple_of(core * here + d * own, 8), own), :]
            g_mixed = scale * (g_normed * wide(v.vb[1, core, at, :]) - one - x_hat * two)
            v.gmix[at, :] = g_mixed
            v.sums[0, at, :] = lane_sum(g_mixed * v.tok[at, :])
            v.sums[1, at, :] = lane_sum(g_normed * x_hat)
            v.sums[2, at, :] = lane_sum(g_normed)
            both = jnp.concatenate([g_mixed[:, :columns], g_mixed[:, columns:]], axis=0)
            v.sb3[d] = both.astype(BF16)

        loop(RANKS, each)
        v.rb3[rank] = v.sb3[rank]

    def outputs():
        copy(v.br_out, v.br_in, v.tw, 4, twin).wait_recv()
        mask = v.inside[0:1, :]

        def rows(q):
            at = pl.ds(pl.multiple_of(q * 128, 128), 128)
            branch = v.branch[pl.ds(pl.multiple_of(core * here + q * 128, 128), 128), :]
            branch = branch + v.br_in[at, :].astype(F32) + wide(v.vb[4, core, at, :])
            masked = branch * mask
            v.sums[3, at, :] = lane_sum(v.gb[core, at, :].astype(F32))
            v.sums[4, at, :] = lane_sum(masked * v.cot[at, :])
            v.res[at, :] = v.tok[at, :] + masked * wide(v.vb[3, core, at, :])

        loop(here // 128, rows)
        for g in range(2):
            v.o_out[g, 0] = v.res[:, g * columns : (g + 1) * columns].T.astype(BF16)
        pltpu.make_async_copy(v.o_out, v.output, v.leave.at[2]).start()

    def convolve_back():
        all_slabs(v.a3, 1, v.rb3)
        v.tall[...] = v.rb3[...].astype(F32)

        def up_rows(at, cut):
            taps = [v.kh[l, at, :] for l in range(RANKS)]
            values = [v.tall[i, at, cut] for i in range(RANKS)]
            for i in range(RANKS):
                total = taps[0] * values[i]
                for l in range(1, RANKS - i):
                    total += taps[l] * values[i + l]
                v.galong[i, at, cut] = total.astype(BF16).astype(F32)

        by_tiles(up_rows)

        def lag_rows(at, cut):
            grads = [v.tall[i, at, cut] for i in range(RANKS)]
            values = [v.along[i, at, cut] for i in range(RANKS)]
            for l in range(RANKS):
                total = grads[l] * values[0]
                for i in range(l + 1, RANKS):
                    total += grads[i] * values[i - l]
                v.lags[l, at, cut] = total

        by_tiles(lag_rows)
        none = jnp.zeros((slab, columns), F32)

        def one_step(b, totals):
            at = pl.ds(b * step_rows, step_rows)
            shape = (step_rows, slab, columns)
            values = v.galong[at].reshape(step_rows * slab, columns).astype(BF16)
            g_both = by_table(values, v.to_hi, v.to_lo)
            g_re, g_im = g_both[:, :columns].reshape(shape), g_both[:, columns:].reshape(shape)
            x_re, x_im = v.xs[0, at], v.xs[1, at]
            k0, k1, k2 = v.ks[0], v.ks[1], v.ks[2]
            y_both = jnp.concatenate([g_re * k0 + g_im * k1, g_im * k2 - g_re * k1], axis=2)
            y_both = y_both.reshape(step_rows * slab, 2 * columns)
            conv = by_table(y_both, v.from_hi, v.from_lo)
            v.sb4[at] = conv.reshape(shape).astype(BF16)
            return (
                totals[0] + (x_re * g_re).sum(axis=0),
                totals[1] + (x_im * g_im).sum(axis=0),
                totals[2] + (x_re * g_im - x_im * g_re).sum(axis=0),
            )

        cross = lax.fori_loop(0, RANKS // step_rows, one_step, (none, none, none))
        v.rb4[rank] = v.sb4[rank]
        for q in range(3):
            v.cross[q] = cross[q]

    def kernel_grads():
        cross = [v.cross[q] for q in range(3)]
        zero_lane = lax.broadcasted_iota(jnp.int32, (slab, columns), 1) == 0
        c_re = cross[0] + jnp.where(zero_lane, 0.0, cross[1])
        c_im = jnp.where(zero_lane, cross[1], cross[2])
        dk_width = by_table(jnp.concatenate([c_re, c_im], axis=1), v.from_hi, v.from_lo)
        v.kt[...] = lax.dot_general(
            dk_width, v.pick[...], TN, precision=PRECISE, preferred_element_type=F32
        )

        lags = v.lags[...].reshape(RANKS * slab, columns)
        first = lags.astype(BF16)
        second = (lags - first.astype(F32)).astype(BF16)
        ones = jnp.ones((columns, 128), BF16)
        lags = jnp.dot(first, ones, preferred_element_type=F32)
        lags += jnp.dot(second, ones, preferred_element_type=F32)
        lags = lags.reshape(RANKS, slab, 128)
        for q in range(lanes // 128):
            cut = slice(q * 128, (q + 1) * 128)
            v.kth[:, cut] = jnp.sum(lags * v.pick[:, cut][None], axis=1)
        parameters()

    def parameters():
        def moments(dk, e_re, e_im):
            place = lax.broadcasted_iota(jnp.int32, dk.shape, 0).astype(F32)
            terms = (dk * e_re, dk * e_im)
            plain = [jnp.sum(term, axis=0, keepdims=True) for term in terms]
            timed = [jnp.sum(term * place, axis=0, keepdims=True) for term in terms]
            return plain + timed

        rows_h = moments(v.kth[...], v.eh[0], v.eh[1])
        rows_w = moments(v.kt[...], v.ew[0], v.ew[1])
        p_re, p_im, t_re, t_im = (
            2.0 * jnp.concatenate([h, w], axis=0) for h, w in zip(rows_h, rows_w)
        )
        plain, timed = (p_re, p_im), (t_re, t_im)
        mv = mode_values(v.modes[...])
        step, rate = mv.step, mv.rate
        zoh_plain = times(mv.zoh, plain)
        g_b = times(mv.c, zoh_plain)
        g_c = times(mv.b, zoh_plain)
        coef_timed = times(mv.coef, timed)
        prod_plain = times(mv.prod, plain)
        slope = times(
            (step * mv.once[0] - mv.zoh[0], step * mv.once[1] - mv.zoh[1]), mv.over
        )
        g_rate = times(prod_plain, slope)
        g_rate = (g_rate[0] + step * coef_timed[0], g_rate[1] + step * coef_timed[1])
        g_step = times(prod_plain, mv.once)[0] + times(coef_timed, rate)[0]
        rows = [
            step * g_step,
            g_rate[0] * rate[0],
            -g_rate[1],
            g_b[0],
            -g_b[1],
            g_c[0],
            -g_c[1],
            jnp.zeros_like(step),
        ]
        table = jnp.concatenate(rows, axis=0)
        z, y, x = rank // 4, (rank // 2) % 2, rank % 2
        for five in range(3):
            block = jnp.zeros((per, 128), F32)
            for k in range(5 if five < 2 else 4):
                r = 5 * five + k
                at = lax.broadcasted_iota(jnp.int32, (128, lanes), 0) - k * own
                at = (at == lax.broadcasted_iota(jnp.int32, (128, lanes), 1) // per).astype(BF16)
                values = (v.of_mode[...] * table[r : r + 1]).astype(BF16)
                block += lax.dot_general(values, at, NT, preferred_element_type=F32)
            v.pack[five * per : (five + 1) * per, :] = block.astype(BF16)
        ones = jnp.ones((8, 128), F32)
        vectors = [
            v.dbu[m, 0:1, q * 128 : (q + 1) * 128] for m in range(chunks) for q in range(part // 128)
        ]
        for k in range(5):
            line = lax.dot_general(
                ones, v.sums[k], NT, precision=PRECISE, preferred_element_type=F32
            )
            vectors += [line[0:1, q * 128 : (q + 1) * 128] for q in range(here // 128)]
        vectors.append(jnp.zeros((32 - len(vectors), 128), F32))
        v.pack[3 * per :, :] = jnp.concatenate(vectors, axis=0).astype(BF16)
        v.gathered[z, y, x] = v.pack[...]

        def to(k):
            target = (lax.rem(z + k, 4) * 4 + y * 2 + x, core)
            copy(v.pack, v.gathered.at[z, y, x], v.ga, k, target).start()

        loop(4, to, 1)

    def gather_across():
        def wait(k):
            s = lax.rem(z + 4 - k, 4)
            copy(v.pack, v.gathered.at[s, y, x], v.ga, k, (s * 4 + y * 2 + x, core)).wait_recv()

        loop(4, wait, 1)
        mine = v.gathered.at[:, y, x]
        copy(mine, mine, v.ga, 4, across).start()

    def gather_beside():
        theirs = v.gathered.at[:, 1 - y, x]
        copy(theirs, theirs, v.ga, 4, across).wait_recv()
        mine = v.gathered.at[:, :, x]
        copy(mine, mine, v.ga, 5, beside).start()

    def token_grads():
        all_slabs(v.a4, 1, v.rb4)

        def rows(d):
            at = pl.ds(pl.multiple_of(d * own, 8), own)
            conv = v.rb4[d].astype(F32)
            conv = jnp.concatenate([conv[:own], conv[own:]], axis=1)
            skip = wide(v.vb[0, core, at, :])
            v.res[at, :] = v.cot[at, :] + skip * v.gmix[at, :] + conv

        loop(RANKS, rows)
        for g in range(2):
            v.t_out[g, 0] = v.res[:, g * columns : (g + 1) * columns].T.astype(BF16)
        pltpu.make_async_copy(v.t_out, v.d_tokens, v.leave.at[3]).start()

    down = types.SimpleNamespace(
        part=v.pd,
        from_first=v.d1,
        from_outer=v.d2,
        from_inner=v.d3,
        from_third=v.d4,
        full=v.fd,
        keep=x,
        first=beside,
        third=across,
    )
    up = types.SimpleNamespace(
        part=v.pu,
        from_first=v.u1,
        from_outer=v.u2,
        from_inner=v.u3,
        from_third=v.u4,
        full=v.fu,
        keep=y,
        first=across,
        third=beside,
    )

    def leave(c):
        return (
            pltpu.make_async_copy(v.fd.at[c], v.down.at[c], v.leave.at[0]),
            pltpu.make_async_copy(v.fu.at[c], v.up.at[c], v.leave.at[1]),
        )


    def advance(stage, c, role):
        reduce_stage(stage, c, role, places, (down, up), v.sent, v.landed)

    def known(stage, c):
        live = (c * (pieces - 1 - c) >= 0).astype(jnp.int32)
        advance(stage, c, live * (1 + middle))
        if stage == STAGES - 1:

            @pl.when(live > 0)
            def _():
                for one in leave(c):
                    one.start()

    events = {
        0: norm_back,
        3: outputs,
        9: convolve_back,
        11: kernel_grads,
        13: gather_across,
        15: gather_beside,
        21: token_grads,
    }

    def feed_and_send(t):
        feed(t)
        for q in range(CUTS):
            c = CUTS * t + q
            advance(0, c, (c < 4).astype(jnp.int32) * (1 + middle))

    loop(chunks, feed_and_send)
    share()

    def tick(t, carry):
        for when, event in events.items():
            pl.when(t == when)(event)
        for when, sems, src, dst in (
            (0, v.a3, v.sb3, v.rb3),
            (9, v.a4, v.sb4, v.rb4),
        ):
            batch = t - when

            @pl.when(batch * (8 - 1 - batch) >= 0)
            def _():
                scatter(sems, src, dst.at[rank], first=1 + 2 * batch, count=2)

        for q in range(1):
            c = 4 + 1 * (t - 0) + q
            known(0, jnp.where(t < 0, pieces, c))
        for stage, start in enumerate((0,2,4,6,8,10,12,14,16), 1):
            for q in range(1):
                known(stage, 1 * (t - start) + q)
        return carry

    lax.fori_loop(0, pieces // 1 + (0,2,4,6,8,10,12,14,16)[-1], tick, 0)

    theirs = v.gathered.at[:, :, 1 - x]
    copy(theirs, theirs, v.ga, 5, beside).wait_recv()

    pltpu.make_async_copy(v.fd, v.down, v.leave.at[0]).wait()
    pltpu.make_async_copy(v.fu, v.up, v.leave.at[1]).wait()
    pltpu.make_async_copy(v.o_out, v.output, v.leave.at[2]).wait()
    pltpu.make_async_copy(v.t_out, v.d_tokens, v.leave.at[3]).wait()
    all_slabs(v.a1, 0, v.rb1)
    all_slabs(v.a2, 0, v.sb2)
    all_slabs(v.a3, 0, v.sb3)
    all_slabs(v.a4, 0, v.sb4)
    reduce_sent(middle, (down, up), v.sent)
    copy(v.tb.at[core], v.tb.at[core], v.tw, 0, twin).wait_send()
    copy(v.vx.at[core], v.vx.at[core], v.tw, 1, twin).wait_send()
    copy(v.gb.at[core], v.gb.at[core], v.tw, 2, twin).wait_send()
    copy(v.gn_out, v.gn_in, v.tw, 3, twin).wait_send()
    copy(v.br_out, v.br_in, v.tw, 4, twin).wait_send()

    copy(v.rb2.at[core], v.rb2.at[core], v.fw, 0, twin).wait_send()

    def gather_sent(k):
        target = (lax.rem(z + k, 4) * 4 + y * 2 + x, core)
        copy(v.pack, v.gathered.at[z, y, x], v.ga, k, target).wait_send()

    loop(4, gather_sent, 1)
    mine = v.gathered.at[:, y, x]
    copy(mine, mine, v.ga, 4, across).wait_send()
    mine = v.gathered.at[:, :, x]
    copy(mine, mine, v.ga, 5, beside).wait_send()


def finish_kernel(own, *refs):
    ins, outs, small, near, wide, sems = refs[:5], refs[5:20], refs[20:33], refs[33:36], refs[36:38], refs[38:]
    brought, moved, left = sems
    pieces, rows = near[0].shape[0], wide[0].shape[1]
    group = pieces // brought.shape[1]

    def bring(which, m):
        some = pl.ds(m * group, group)
        return pltpu.make_async_copy(
            ins[which].at[some], near[which].at[some], brought.at[which, m]
        )

    def leave(which, m):
        if which == 0:
            place = outs[0].at[pl.ds(pl.multiple_of(m * rows, rows), rows)]
        else:
            up_rows, up_cols = wide[1].shape[1:]
            place = outs[1].at[
                pl.ds(pl.multiple_of(m % CUTS // 2 * up_rows, 16), up_rows),
                pl.ds(pl.multiple_of((m // CUTS * 2 + m % 2) * up_cols, 128), up_cols),
            ]
        return pltpu.make_async_copy(wide[which].at[m], place, left.at[which])

    brings = [
        pltpu.make_async_copy(src, dst, brought.at[2, k])
        for k, (src, dst) in enumerate(zip(ins[2:], (near[2],) + small[:2]))
    ]
    moves = [
        pltpu.make_async_copy(src, dst, moved.at[k])
        for k, (src, dst) in enumerate(zip(small, outs[2:]))
    ]

    def each(count, body):
        def step(m, carry):
            for which in range(2):
                body(which, m)
            return carry

        lax.fori_loop(0, count, step, 0)

    def widen(which, m):
        bring(which, m).wait()
        for q in range(group):
            one = group * m + q
            wide[which][one] = near[which][one].reshape(wide[which].shape[1:]).astype(F32)
            leave(which, one).start()

    for one in brings:
        one.start()
    each(brought.shape[1], lambda which, m: bring(which, m).start())
    for one in brings:
        one.wait()
    widen_small(own, near[2], small[2:])
    for one in moves:
        one.start()
    each(brought.shape[1], widen)
    for which in range(2):
        pltpu.make_async_copy(wide[which], wide[which], left.at[which]).wait()
    for one in moves:
        one.wait()


def widen_small(own, gathered, small):
    d_log_step, d_log_decay, d_frequency, d_b_in, d_c_out = small[:5]
    per, here = d_log_decay.shape[1:]
    lane = lax.broadcasted_iota(jnp.int32, (per, 128), 1)
    whole = []
    for r in range(14):
        five, k = divmod(r, 5)
        windows = [jnp.zeros((per, 128), F32) for _ in range(here // 128)]
        for s in range(RANKS):
            block = gathered[s // 4, s // 2 % 2, s % 2, five * per : (five + 1) * per, :]
            turned = pltpu.roll(block.astype(F32), (own * (s - k)) % 128, 1)
            window, low = divmod(own * s, 128)
            inside = (lane >= low) & (lane < low + own)
            windows[window] = jnp.where(inside, turned, windows[window])
            if low + own > 128:
                inside = lane < low + own - 128
                windows[window + 1] = jnp.where(inside, turned, windows[window + 1])
        whole.append(jnp.concatenate(windows, axis=1))
    for a in range(2):
        d_log_step[a : a + 1, :] = jnp.sum(whole[a], axis=0, keepdims=True)
        d_log_decay[a] = whole[2 + a]
        d_frequency[a] = whole[4 + a]
        for i in range(2):
            d_b_in[a, i] = whole[6 + 2 * i + a]
            d_c_out[a, i] = whole[10 + 2 * i + a]
    sums = jnp.zeros((32, 128), F32)
    for s in range(RANKS):
        sums += gathered[s // 4, s // 2 % 2, s % 2, 3 * per :, :].astype(F32)
    row = 0
    for vector in small[5:]:
        for q in range(vector.shape[0] // 128):
            vector[pl.ds(q * 128, 128)] = sums[row]
            row += 1


def block_shards(
    tokens,
    heights,
    widths,
    log_step,
    log_decay,
    frequency,
    b_in,
    c_out,
    skip_gain,
    ln_gain,
    ln_bias,
    w_up,
    b_up,
    w_down,
    b_down,
    layer_scale,
    cotangent,
):
    columns, here = tokens.shape[2:]
    modes_each = log_decay.shape[2]
    hidden = w_up.shape[1]
    own = here // RANKS
    chunks = hidden // 256
    part = hidden // chunks
    channels = 2 * here
    pixels = 2 * columns
    lanes = own * modes_each
    tables = spectral_tables(columns)
    slabs = (RANKS, 2 * own, columns)
    tall = pltpu.VMEM(slabs, F32)
    in_vmem = pl.BlockSpec(memory_space=pltpu.VMEM)
    in_smem = pl.BlockSpec(memory_space=pltpu.SMEM)
    anywhere = pl.BlockSpec(memory_space=pl.ANY)
    inputs = dict(
        tokens=(tokens, in_vmem),
        cotangent_in=(cotangent, anywhere),
        heights=(heights, in_smem),
        widths=(widths, in_smem),
        log_step_in=(log_step, anywhere),
        log_decay_in=(log_decay.swapaxes(-1, -2), anywhere),
        frequency_in=(frequency.swapaxes(-1, -2), anywhere),
        b_in_in=(b_in.swapaxes(-1, -2), anywhere),
        c_out_in=(c_out.swapaxes(-1, -2), anywhere),
        b_up=(b_up, in_vmem),
        skip_gain=(skip_gain, in_vmem),
        ln_gain=(ln_gain, in_vmem),
        ln_bias=(ln_bias, in_vmem),
        layer_scale=(layer_scale, in_vmem),
        b_down=(b_down, in_vmem),
        w_up=(w_up, anywhere),
        w_down=(w_down, anywhere),
        to_hi_in=(tables[0], anywhere),
        to_lo_in=(tables[1], anywhere),
        from_hi_in=(tables[2], anywhere),
        from_lo_in=(tables[3], anywhere),
    )
    down_shape = (CUTS * chunks, 2, 2, part // CUTS // 4, channels)
    up_shape = (CUTS * chunks, 2, 2, channels // (2 * CUTS), part // 2)
    outs = dict(
        output=(jax.ShapeDtypeStruct(tokens.shape, BF16), anywhere),
        d_tokens=(jax.ShapeDtypeStruct(tokens.shape, BF16), anywhere),
        down=(jax.ShapeDtypeStruct(down_shape, BF16), anywhere),
        up=(jax.ShapeDtypeStruct(up_shape, BF16), anywhere),
        gathered=(jax.ShapeDtypeStruct((4, 2, 2, 3 * modes_each + 32, 128), BF16), in_vmem),
    )
    low_slabs = pltpu.VMEM(slabs, BF16)
    both_slabs = pltpu.VMEM((2,) + slabs, BF16)
    scratch = dict(
        wu=pltpu.VMEM((chunks, channels, part), BF16),
        wd=pltpu.VMEM((chunks, part, channels), BF16),
        wut=pltpu.VMEM((chunks, part, channels), BF16),
        wdt=pltpu.VMEM((chunks, channels, part), BF16),
        tok=pltpu.VMEM((here, pixels), F32),
        cot=pltpu.VMEM((here, pixels), F32),
        gmix=pltpu.VMEM((here, pixels), F32),
        res=pltpu.VMEM((here, pixels), F32),
        tb=both_slabs,
        rb1=low_slabs,
        sb2=low_slabs,
        rb2=both_slabs,
        sb3=low_slabs,
        rb3=low_slabs,
        sb4=low_slabs,
        rb4=low_slabs,
        vx=pltpu.VMEM((2, 32, 128), F32),
        vb=pltpu.VMEM((5, 2, here, 128), F32),
        bias=pltpu.VMEM((chunks, part, 128), F32),
        inside=pltpu.VMEM((8, pixels), F32),
        inv=pltpu.VMEM((8, pixels), F32),
        gb=pltpu.VMEM((2, here, pixels), BF16),
        modes=pltpu.VMEM((16, lanes), F32),
        of_mode=pltpu.VMEM((modes_each, lanes), F32),
        cross=pltpu.VMEM((3, 2 * own, columns), F32),
        pick=pltpu.VMEM((2 * own, lanes), F32),
        eh=pltpu.VMEM((2, RANKS, lanes), F32),
        ej=pltpu.VMEM((2, columns // 8, lanes), F32),
        ew=pltpu.VMEM((2, columns, lanes), F32),
        kt=pltpu.VMEM((columns, lanes), F32),
        kth=pltpu.VMEM((RANKS, lanes), F32),
        ks=pltpu.VMEM((3, 2 * own, columns), F32),
        kh=pltpu.VMEM((RANKS, 2 * own, 128), F32),
        xs=pltpu.VMEM((2,) + slabs, F32),
        along=tall,
        tall=tall,
        galong=tall,
        lags=tall,
        xhat=pltpu.VMEM((2 * RANKS, own, pixels), F32),
        normed=pltpu.VMEM((channels, pixels), BF16),
        branch=pltpu.VMEM((channels, pixels), F32),
        gn=pltpu.VMEM((channels, pixels), F32),
        gn_out=pltpu.VMEM((channels, pixels), BF16),
        gn_in=pltpu.VMEM((channels, pixels), BF16),
        br_out=pltpu.VMEM((here, pixels), BF16),
        br_in=pltpu.VMEM((here, pixels), BF16),
        dbu=pltpu.VMEM((chunks, 8, part), F32),
        sums=pltpu.VMEM((5, here, 128), F32),
        pack=pltpu.VMEM((3 * modes_each + 32, 128), BF16),
        fetch=pltpu.SemaphoreType.DMA((2,)),
        leave=pltpu.SemaphoreType.DMA((4,)),
        bring=pltpu.SemaphoreType.DMA((len(ASYNC),)),
        o_out=pltpu.VMEM(tokens.shape, BF16),
        t_out=pltpu.VMEM(tokens.shape, BF16),
        cotangent=pltpu.VMEM(cotangent.shape, BF16),
        log_step=pltpu.VMEM(log_step.shape, F32),
        log_decay=pltpu.VMEM((2, modes_each, here), F32),
        frequency=pltpu.VMEM((2, modes_each, here), F32),
        b_in=pltpu.VMEM((2, 2, modes_each, here), F32),
        c_out=pltpu.VMEM((2, 2, modes_each, here), F32),
        to_hi=pltpu.VMEM(tables[0].shape, BF16),
        to_lo=pltpu.VMEM(tables[1].shape, BF16),
        from_hi=pltpu.VMEM(tables[2].shape, BF16),
        from_lo=pltpu.VMEM(tables[3].shape, BF16),
    )

    def reduction(shape):
        count, halves, pieces, rows, width = shape
        whole = pltpu.VMEM(shape, BF16)
        half = pltpu.VMEM((count, pieces, rows, width), BF16)
        piece = pltpu.VMEM((count, rows, width), BF16)
        return whole, half, piece, piece, piece, whole

    down_scratch, up_scratch = reduction(down_shape), reduction(up_shape)
    scratch.update(
        zip(("pd", "d1", "d2", "d3", "d4", "fd"), down_scratch),
    )
    scratch.update(
        zip(("pu", "u1", "u2", "u3", "u4", "fu"), up_scratch),
    )
    one_each = pltpu.SemaphoreType.DMA((2, 1))
    scratch.update(a1=one_each, a3=one_each, a4=one_each, fw=one_each)
    scratch.update(a2=pltpu.SemaphoreType.DMA((2, RANKS)))
    scratch.update(sent=pltpu.SemaphoreType.DMA((9,)))
    scratch.update(landed=pltpu.SemaphoreType.DMA((9, CUTS * chunks)))
    scratch.update(tw=pltpu.SemaphoreType.DMA((2, 5)), ga=pltpu.SemaphoreType.DMA((2, 6)))
    names = tuple(inputs) + tuple(outs) + tuple(scratch)
    output, d_tokens, down, up, gathered = pl.pallas_call(
        functools.partial(block_kernel, names),
        out_shape=tuple(shape for shape, _ in outs.values()),
        in_specs=[spec for _, spec in inputs.values()],
        out_specs=tuple(spec for _, spec in outs.values()),
        scratch_shapes=list(scratch.values()),
        compiler_params=pltpu.CompilerParams(
            collective_id=0, has_side_effects=True, vmem_limit_bytes=62 << 20
        ),
    )(*(value for value, _ in inputs.values()))
    result = (
        jax.ShapeDtypeStruct((hidden, channels), F32),
        jax.ShapeDtypeStruct((channels, hidden), F32),
        output,
        d_tokens,
        log_step,
        jax.ShapeDtypeStruct((2, modes_each, here), F32),
        jax.ShapeDtypeStruct((2, modes_each, here), F32),
        jax.ShapeDtypeStruct((2, 2, modes_each, here), F32),
        jax.ShapeDtypeStruct((2, 2, modes_each, here), F32),
        b_up,
        skip_gain,
        ln_gain,
        ln_bias,
        b_down,
        layer_scale,
    )
    result = tuple(jax.ShapeDtypeStruct(one.shape, one.dtype) for one in result)
    (
        d_w_down,
        d_w_up,
        output,
        d_tokens,
        d_log_step,
        d_log_decay,
        d_frequency,
        d_b_in,
        d_c_out,
        d_b_up,
        d_skip_gain,
        d_ln_gain,
        d_ln_bias,
        d_b_down,
        d_layer_scale,
    ) = pl.pallas_call(
        functools.partial(finish_kernel, own),
        out_shape=result,
        in_specs=[anywhere] * 5,
        out_specs=(anywhere,) * 15,
        scratch_shapes=[pltpu.VMEM(one.shape, one.dtype) for one in result[2:]]
        + [pltpu.VMEM(one.shape, BF16) for one in (down, up, gathered)]
        + [
            pltpu.VMEM((CUTS * chunks, part // CUTS, channels), F32),
            pltpu.VMEM((CUTS * chunks, channels * 2 // CUTS, part // 2), F32),
            pltpu.SemaphoreType.DMA((3, chunks)),
            pltpu.SemaphoreType.DMA((13,)),
            pltpu.SemaphoreType.DMA((2,)),
        ],
        compiler_params=pltpu.CompilerParams(vmem_limit_bytes=62 << 20),
    )(down, up, gathered, output, d_tokens)
    return (
        output,
        d_tokens,
        d_log_step,
        d_log_decay.swapaxes(-1, -2),
        d_frequency.swapaxes(-1, -2),
        d_b_in.swapaxes(-1, -2),
        d_c_out.swapaxes(-1, -2),
        d_skip_gain,
        d_ln_gain,
        d_ln_bias,
        d_w_up,
        d_b_up,
        d_w_down,
        d_b_down,
        d_layer_scale,
    )


def shards(
    tokens,
    heights,
    widths,
    log_step,
    log_decay,
    frequency,
    b_in,
    c_out,
    skip_gain,
    ln_gain,
    ln_bias,
    w_up,
    b_up,
    w_down,
    b_down,
    layer_scale,
    cotangent,
):
    row_count = lax.axis_size("rows")
    row_rank = lax.axis_index("rows")
    grid_count, rows_here, columns, channels = tokens.shape
    all_channels = channels * lax.axis_size("ch")
    height = rows_here * row_count
    own_count = channels // row_count
    first_chan = row_rank * own_count
    pixels = grid_count * rows_here * columns
    token_f = tokens.astype(jnp.float32)
    width_tables = make_tables(columns)
    height_tables = make_tables(height)
    own_params = tuple(
        lax.dynamic_slice_in_dim(param, first_chan, own_count, param.ndim - trailing)
        for param, trailing in (
            (log_step, 1),
            (log_decay, 2),
            (frequency, 2),
            (b_in, 2),
            (c_out, 2),
        )
    )
    width_params = tuple(param[1] for param in own_params)
    height_params = tuple(param[0] for param in own_params)
    k_width, width_pull = jax.vjp(lambda params: make_kernel(params, columns), width_params)
    k_height, height_pull = jax.vjp(lambda params: make_kernel(params, height), height_params)
    kw_re, kw_im = kernel_spectrum(k_width, width_tables)
    kh_re, kh_im = kernel_spectrum(k_height, height_tables)
    kh_re = kh_re[:, None, :]
    kh_im = kh_im[:, None, :]
    pencil_tokens = lax.all_to_all(tokens, "rows", split_axis=3, concat_axis=1, tiled=True)
    x_re, x_im = to_spectrum(pencil_tokens.astype(jnp.float32), width_tables, "fw,grwc->grfc")
    along_width = from_spectrum(
        x_re * kw_re - x_im * kw_im, x_re * kw_im + x_im * kw_re, width_tables, "fw,grfc->grwc"
    ).astype(jnp.bfloat16)
    p_re, p_im = to_spectrum(along_width.astype(jnp.float32), height_tables, "fh,ghwc->gfwc")
    mixed_cols = from_spectrum(
        p_re * kh_re - p_im * kh_im, p_re * kh_im + p_im * kh_re, height_tables, "fh,gfwc->ghwc"
    ).astype(jnp.bfloat16)
    back_rows = lax.all_to_all(mixed_cols, "rows", split_axis=1, concat_axis=3, tiled=True)
    mixed = back_rows.astype(jnp.float32) + skip_gain * token_f
    flat_mixed = mixed.reshape(pixels, channels)
    sum_one, sum_two = lax.psum(
        (jnp.sum(flat_mixed, axis=1), jnp.sum(flat_mixed * flat_mixed, axis=1)), "ch"
    )
    centre = sum_one / all_channels
    spread = sum_two / all_channels - centre * centre
    inv_std = lax.rsqrt(spread + EPSILON)[:, None]
    x_hat = (flat_mixed - centre[:, None]) * inv_std
    normed = (x_hat * ln_gain + ln_bias).astype(jnp.bfloat16)
    hidden = (
        jnp.dot(
            lax.all_gather(normed, "ch", axis=1, tiled=True),
            w_up,
            preferred_element_type=jnp.float32,
        )
        + b_up
    )
    active = jax.nn.gelu(hidden, approximate=False).astype(jnp.bfloat16)
    partials = jnp.dot(active, w_down, preferred_element_type=jnp.float32)
    branch = (
        lax.psum_scatter(
            partials.astype(jnp.bfloat16), "ch", scatter_dimension=1, tiled=True
        ).astype(jnp.float32)
        + b_down
    )
    row_ids = row_rank * rows_here + jnp.arange(rows_here, dtype=jnp.int32)
    col_ids = jnp.arange(columns, dtype=jnp.int32)
    inside = (row_ids[None, :, None] < heights[:, None, None]) & (
        col_ids[None, None, :] < widths[:, None, None]
    )
    inside = inside.astype(jnp.float32).reshape(pixels, 1)
    flat_tokens = token_f.reshape(pixels, channels)
    output = (
        (flat_tokens + inside * layer_scale * branch).astype(jnp.bfloat16).reshape(tokens.shape)
    )
    over_rows = (((0,), (0,)), ((), ()))
    over_cols = (((1,), (1,)), ((), ()))
    g_flat = cotangent.astype(jnp.float32).reshape(pixels, channels)
    g_masked = g_flat * inside
    g_branch = (g_masked * layer_scale).astype(jnp.bfloat16)
    d_layer_scale = jnp.sum(g_masked * branch, axis=0)
    d_b_down = jnp.sum(g_branch.astype(jnp.float32), axis=0)
    g_branch_all = lax.all_gather(g_branch, "ch", axis=1, tiled=True)
    d_w_down = lax.dot_general(active, g_branch_all, over_rows, preferred_element_type=jnp.float32)
    g_active = lax.dot_general(g_branch_all, w_down, over_cols, preferred_element_type=jnp.float32)
    gelu_pull = jax.vjp(lambda values: jax.nn.gelu(values, approximate=False), hidden)[1]
    g_hidden = gelu_pull(g_active)[0].astype(jnp.bfloat16)
    d_b_up = jnp.sum(g_hidden.astype(jnp.float32), axis=0)
    d_w_up = lax.dot_general(
        lax.all_gather(normed, "ch", axis=1, tiled=True),
        g_hidden,
        over_rows,
        preferred_element_type=jnp.float32,
    )
    g_terms = lax.dot_general(g_hidden, w_up, over_cols, preferred_element_type=jnp.float32)
    g_normed = lax.psum_scatter(g_terms, "ch", scatter_dimension=1, tiled=True)
    d_ln_gain = jnp.sum(g_normed * x_hat, axis=0)
    d_ln_bias = jnp.sum(g_normed, axis=0)
    g_hat = g_normed * ln_gain
    sum_grad, sum_cross = lax.psum((jnp.sum(g_hat, axis=1), jnp.sum(g_hat * x_hat, axis=1)), "ch")
    g_mixed = inv_std * (
        g_hat - sum_grad[:, None] / all_channels - x_hat * sum_cross[:, None] / all_channels
    )
    d_skip_gain = jnp.sum(g_mixed * flat_tokens, axis=0)
    g_spatial = g_mixed.astype(jnp.bfloat16).reshape(tokens.shape)
    pencil_grad = lax.all_to_all(g_spatial, "rows", split_axis=3, concat_axis=1, tiled=True)
    gp_re, gp_im = to_spectrum(pencil_grad.astype(jnp.float32), height_tables, "fh,ghwc->gfwc")
    vp_re, vp_im = p_re, p_im
    g_pencil_along = from_spectrum(
        gp_re * kh_re + gp_im * kh_im, gp_im * kh_re - gp_re * kh_im, height_tables, "fh,gfwc->ghwc"
    ).astype(jnp.bfloat16)
    cross_re = jnp.sum(vp_re * gp_re + vp_im * gp_im, axis=(0, 2))
    cross_im = jnp.sum(vp_re * gp_im - vp_im * gp_re, axis=(0, 2))
    dk_height = kernel_from_cross(cross_re, cross_im, height_tables)
    g_along = g_pencil_along
    ga_re, ga_im = to_spectrum(g_along.astype(jnp.float32), width_tables, "fw,grwc->grfc")
    g_conv = from_spectrum(
        ga_re * kw_re + ga_im * kw_im, ga_im * kw_re - ga_re * kw_im, width_tables, "fw,grfc->grwc"
    )
    g_conv = lax.all_to_all(
        g_conv.astype(jnp.bfloat16), "rows", split_axis=1, concat_axis=3, tiled=True
    ).astype(jnp.float32)
    wide_re = jnp.sum(x_re * ga_re + x_im * ga_im, axis=(0, 1))
    wide_im = jnp.sum(x_re * ga_im - x_im * ga_re, axis=(0, 1))
    dk_width = kernel_from_cross(wide_re, wide_im, width_tables)
    d_tokens = ((g_flat + g_mixed * skip_gain).reshape(tokens.shape) + g_conv).astype(jnp.bfloat16)
    width_grads = width_pull(dk_width)[0]
    height_grads = height_pull(dk_height)[0]

    def gathered(pieces, dim_num):
        return lax.all_gather(jnp.stack(pieces), "rows", axis=dim_num, tiled=True)

    param_grads = tuple(
        gathered(pair, dim_num)
        for pair, dim_num in zip(zip(height_grads, width_grads), (1, 1, 1, 2, 2))
    )
    d_w_down, d_w_up, d_skip_gain, d_ln_gain, d_ln_bias, d_b_up, d_b_down, d_layer_scale = lax.psum(
        (d_w_down, d_w_up, d_skip_gain, d_ln_gain, d_ln_bias, d_b_up, d_b_down, d_layer_scale),
        "rows",
    )
    return (output, d_tokens) + param_grads + (
        d_skip_gain,
        d_ln_gain,
        d_ln_bias,
        d_w_up,
        d_b_up,
        d_w_down,
        d_b_down,
        d_layer_scale,
    )


def solution(mesh):
    one_row_each = mesh.shape["rows"] == RANKS and mesh.shape["ch"] == 2
    return jax.shard_map(
        block_shards if one_row_each else shards,
        mesh=mesh,
        in_specs=(
            P(None, "rows", None, "ch"),
            P(),
            P(),
            P(None, "ch"),
            P(None, "ch", None),
            P(None, "ch", None),
            P(None, None, "ch", None),
            P(None, None, "ch", None),
            P("ch"),
            P("ch"),
            P("ch"),
            P(None, "ch"),
            P("ch"),
            P("ch", None),
            P("ch"),
            P("ch"),
            P(None, "rows", None, "ch"),
        ),
        out_specs=(
            P(None, "rows", None, "ch"),
            P(None, "rows", None, "ch"),
            P(None, "ch"),
            P(None, "ch", None),
            P(None, "ch", None),
            P(None, None, "ch", None),
            P(None, None, "ch", None),
            P("ch"),
            P("ch"),
            P("ch"),
            P(None, "ch"),
            P("ch"),
            P("ch", None),
            P("ch"),
            P("ch"),
        ),
        check_vma=False,
    )
```

```python
import functools
import types

import jax
import jax.numpy as jnp
import numpy as np
from jax import lax
from jax.experimental import pallas as pl
from jax.experimental.pallas import tpu as pltpu
from jax.sharding import PartitionSpec as P

PRECISE = lax.Precision.HIGHEST
EPSILON = 1e-06
MESH = pl.DeviceIdType.MESH


def make_tables(length):
    freq_ids = jnp.arange(length + 1, dtype=jnp.int32)[:, None]
    places = jnp.arange(length, dtype=jnp.int32)[None, :]
    turns = freq_ids * places % (2 * length)
    angles = turns.astype(jnp.float32) * (jnp.pi / length)
    cosine = jnp.cos(angles)
    sine_t = jnp.sin(angles)
    weights = jnp.where((freq_ids == 0) | (freq_ids == length), 1.0, 2.0) / (2.0 * length)
    return (cosine, sine_t, cosine * weights, sine_t * weights)


def to_spectrum(values, tables, pattern):
    real_part = jnp.einsum(pattern, tables[0], values, precision=PRECISE)
    imag_part = -jnp.einsum(pattern, tables[1], values, precision=PRECISE)
    return (real_part, imag_part)


def from_spectrum(real_part, imag_part, tables, pattern):
    return jnp.einsum(pattern, tables[2], real_part, precision=PRECISE) - jnp.einsum(
        pattern, tables[3], imag_part, precision=PRECISE
    )


def kernel_spectrum(kernel, tables):
    real_part = jnp.dot(tables[0], kernel, precision=PRECISE)
    imag_part = -jnp.dot(tables[1], kernel, precision=PRECISE)
    return (real_part, imag_part)


def kernel_from_cross(cross_re, cross_im, tables):
    contract = (((0,), (0,)), ((), ()))
    return lax.dot_general(tables[2], cross_re, contract, precision=PRECISE) - lax.dot_general(
        tables[3], cross_im, contract, precision=PRECISE
    )


def make_kernel(params, length):
    log_step, log_decay, frequency, b_in, c_out = params
    step_size = jnp.exp(log_step)[:, None]
    decay_re = -jnp.exp(log_decay)
    step_re = step_size * decay_re
    step_im = step_size * frequency
    half_sin = jnp.sin(0.5 * step_im)
    num_re = jnp.expm1(step_re) * jnp.cos(step_im) - 2.0 * half_sin * half_sin
    num_im = jnp.exp(step_re) * jnp.sin(step_im)
    divisor = decay_re * decay_re + frequency * frequency
    zoh_re = (num_re * decay_re + num_im * frequency) / divisor
    zoh_im = (num_im * decay_re - num_re * frequency) / divisor
    prod_re = b_in[0] * c_out[0] - b_in[1] * c_out[1]
    prod_im = b_in[0] * c_out[1] + b_in[1] * c_out[0]
    coef_re = prod_re * zoh_re - prod_im * zoh_im
    coef_im = prod_re * zoh_im + prod_im * zoh_re
    places = jnp.arange(length, dtype=jnp.float32)[:, None, None]
    fading = jnp.exp(step_re[None] * places)
    turning = step_im[None] * places
    return 2.0 * jnp.sum(fading * (coef_re * jnp.cos(turning) - coef_im * jnp.sin(turning)), axis=2)


RANKS = 16
STAGES = 10
CUTS = 2
ASYNC = (
    ("cotangent_in", "cotangent"),
    ("log_step_in", "log_step"),
    ("log_decay_in", "log_decay"),
    ("frequency_in", "frequency"),
    ("b_in_in", "b_in"),
    ("c_out_in", "c_out"),
    ("to_hi_in", "to_hi"),
    ("to_lo_in", "to_lo"),
    ("from_hi_in", "from_hi"),
    ("from_lo_in", "from_lo"),
)
BF16 = jnp.bfloat16
F32 = jnp.float32
NT = (((1,), (1,)), ((), ()))
TN = (((0,), (0,)), ((), ()))


def spectral_tables(length):
    turns = np.outer(np.arange(length), np.arange(length)) % (2 * length)
    cosine = np.cos(np.pi * turns / length)
    sine = np.sin(np.pi * turns / length)
    sign = np.where(np.arange(length) % 2, -1.0, 1.0)
    to_re, to_im = cosine.copy(), -sine
    to_im[:, 0] = sign
    from_re, from_im = cosine / length, -sine / length
    from_re[0] /= 2
    from_im[0] = sign / (2 * length)
    tables = []
    for table in (np.concatenate([to_re, to_im], 1), np.concatenate([from_re, from_im], 0)):
        high = table.astype(BF16)
        tables += [high, (table - high.astype(np.float64)).astype(BF16)]
    return tuple(tables)


def by_table(values, high, low):
    def dot(a, b):
        return jnp.dot(a, b[...], preferred_element_type=F32)

    if values.dtype == BF16:
        return dot(values, high) + dot(values, low)
    first = values.astype(BF16)
    second = (values - first.astype(F32)).astype(BF16)
    return dot(first, high) + (dot(first, low) + dot(second, high))


def times(a, b):
    return a[0] * b[0] - a[1] * b[1], a[0] * b[1] + a[1] * b[0]


def up_cut(shape, q):
    rows, cols = shape[0] * 2 // CUTS, shape[1] // 2
    return (
        slice(q // 2 * rows, (q // 2 + 1) * rows),
        slice(q % 2 * cols, (q % 2 + 1) * cols),
    )


def reduce_stage(stage, c, role, places, lines, send, recv):
    near, inner, outer = places
    far = 1 - near

    def start(kind, src, dst, target):
        pltpu.make_async_remote_copy(
            src_ref=src,
            dst_ref=dst,
            send_sem=send.at[kind],
            recv_sem=recv.at[kind, c],
            device_id=target,
            device_id_type=MESH,
        ).start()

    def landed(kind, ref):
        pltpu.make_async_copy(ref, ref, recv.at[kind, c]).wait()

    halves = lines[0].part.at[c]
    quarters = lines[0].from_first.at[c]

    def added(*refs):
        total = refs[0][...].astype(F32)
        for ref in refs[1:]:
            total = total + ref[...].astype(F32)
        return total.astype(BF16)

    def give(kind, which, target):
        for line in lines:
            place = line.full.at[c, line.keep, which]
            start(kind, place, place, target)

    def give_back():
        for line in lines:
            place = line.full.at[c, line.keep]
            start(8, place, place, line.first)

    if stage == 0:

        @pl.when(role > 0)
        def _():
            for line in lines:
                start(0, line.part.at[c, 1 - line.keep], line.from_first.at[c], line.first)

    elif stage == 1:

        @pl.when(role > 0)
        def _():
            landed(0, halves)
            for line in lines:
                line.part[c, line.keep] = added(line.part.at[c, line.keep], line.from_first.at[c])

        @pl.when(role == 1)
        def _():
            for line in lines:
                start(1, line.part.at[c, line.keep, far], line.from_outer.at[c], inner)

    elif stage == 2:

        @pl.when(role == 2)
        def _():
            landed(1, quarters)
            for line in lines:
                mine = line.part.at[c, line.keep, far]
                mine[...] = added(mine, line.from_outer.at[c])
                start(2, mine, line.from_inner.at[c], inner)

    elif stage == 3:

        @pl.when(role == 2)
        def _():
            landed(2, quarters)
            for line in lines:
                mine = line.part.at[c, line.keep, near]
                mine[...] = added(mine, line.from_inner.at[c])
                start(3, mine, line.from_inner.at[c], outer)

    elif stage == 4:

        @pl.when(role == 1)
        def _():
            landed(3, quarters)
            for line in lines:
                mine = line.part.at[c, line.keep, near]
                mine[...] = added(mine, line.from_inner.at[c])
                start(4, mine, line.from_third.at[c], line.third)

    elif stage == 5:

        @pl.when(role == 1)
        def _():
            landed(4, quarters)
            for line in lines:
                mine = line.part.at[c, line.keep, near]
                line.full[c, line.keep, near] = added(mine, line.from_third.at[c])
            give(5, near, inner)

    elif stage == 6:

        @pl.when(role == 2)
        def _():
            landed(5, quarters)
            give(6, near, inner)

    elif stage == 7:

        @pl.when(role == 2)
        def _():
            landed(6, quarters)
            give(7, far, outer)
            give_back()

    elif stage == 8:

        @pl.when(role == 1)
        def _():
            landed(7, quarters)
            give_back()

    else:

        @pl.when(role > 0)
        def _():
            landed(8, halves)


def reduce_sent(middle, lines, send):
    halves, quarters = lines[0].part, lines[0].from_first

    def gone(kinds):
        for kind in kinds:
            ref = halves if kind in (0, 8) else quarters
            pltpu.make_async_copy(ref, ref, send.at[kind]).wait()

    gone((0, 8))

    @pl.when(middle == 0)
    def _():
        gone((1, 4, 5))

    @pl.when(middle == 1)
    def _():
        gone((2, 3, 6, 7))


def mode_values(modes):
    log_step, log_decay, freq, b_re, b_im, c_re, c_im = (modes[2 * q : 2 * q + 2] for q in range(7))
    step = jnp.exp(log_step)
    decay = -jnp.exp(log_decay)
    step_re = step * decay
    step_im = step * freq
    half_sin = jnp.sin(0.5 * step_im)
    series = jnp.ones_like(step_re)
    for order in range(11, 1, -1):
        series = 1.0 + series * step_re * (1.0 / order)
    grown = jnp.exp(step_re)
    less_one = jnp.where(step_re > -0.5, step_re * series, grown - 1.0)
    num_re = less_one * jnp.cos(step_im) - 2.0 * half_sin * half_sin
    num_im = grown * jnp.sin(step_im)
    inverse = 1.0 / (decay * decay + freq * freq)
    over = (decay * inverse, -freq * inverse)
    zoh = times((num_re, num_im), over)
    b, c = (b_re, b_im), (c_re, c_im)
    prod = times(b, c)
    return types.SimpleNamespace(
        step=step,
        rate=(decay, freq),
        over=over,
        step_re=step_re,
        step_im=step_im,
        once=(num_re + 1.0, num_im),
        zoh=zoh,
        b=b,
        c=c,
        prod=prod,
        coef=times(prod, zoh),
    )


def block_kernel(names, *refs):
    v = types.SimpleNamespace(**dict(zip(names, refs)))
    rank, core = lax.axis_index("rows"), lax.axis_index("ch")
    x, y, z = rank % 2, (rank // 2) % 2, rank // 4
    near = z // 2
    toward = 4 * (2 * near - 1)
    middle = jnp.minimum(z * (3 - z), 1)
    beside, across = (rank + 1 - 2 * x, core), (rank + 2 - 4 * y, core)
    places = (near, (rank - toward, core), (rank + toward, core))
    twin = (rank, 1 - core)
    heights, widths = v.heights, v.widths
    chunks, part = v.wd.shape[0], v.wd.shape[1]
    pieces = CUTS * chunks
    slab, columns = v.rb1.shape[1:]
    own = slab // 2
    here = own * RANKS
    pixels = 2 * columns
    per = v.log_decay.shape[1]
    lanes = own * per

    def copy(src, dst, sems, index, target):
        return pltpu.make_async_remote_copy(
            src_ref=src,
            dst_ref=dst,
            send_sem=sems.at[0, index],
            recv_sem=sems.at[1, index],
            device_id=target,
            device_id_type=MESH,
        )

    def loop(count, body, start=0):
        def step(i, carry):
            body(i)
            return carry

        lax.fori_loop(start, count, step, 0)

    def wide(column):
        return jnp.concatenate([column] * (pixels // column.shape[1]), axis=1)

    def partner(k):
        return rank ^ lax.rem(15 * k, RANKS)

    def slab_copy(sems, index, src, dst, d):
        return pltpu.make_async_remote_copy(
            src_ref=src,
            dst_ref=dst,
            send_sem=sems.at[0, 0],
            recv_sem=sems.at[1, index],
            device_id=(d, core),
            device_id_type=MESH,
        )

    def scatter(sems, src, dst, each=False, first=1, count=RANKS - 1):
        def start(k):
            d = partner(k)

            @pl.when(k < RANKS)
            def _():
                slab_copy(sems, k if each else 0, src.at[d], dst, d).start()

        loop(first + count, start, first)

    def all_slabs(sems, which, ref):
        most = ref.at[pl.ds(0, RANKS - 1)]
        pltpu.make_async_copy(most, most, sems.at[which, 0]).wait()

    def bring(which):
        far_ref, near_ref = ASYNC[which]
        return pltpu.make_async_copy(getattr(v, far_ref), getattr(v, near_ref), v.bring.at[which])

    barrier = pltpu.get_barrier_semaphore()

    def greet(k):
        pl.semaphore_signal(
            barrier, inc=1, device_id=(lax.rem(rank + k, RANKS), core), device_id_type=MESH
        )

    loop(RANKS, greet, 1)
    pl.semaphore_signal(barrier, inc=1, device_id=twin, device_id_type=MESH)

    def fetch_up(m):
        cols = pl.ds(pl.multiple_of(m * part, part), part)
        return pltpu.make_async_copy(v.w_up.at[:, cols], v.wu.at[m], v.fetch.at[0])

    def fetch_down(m):
        rows = pl.ds(pl.multiple_of(m * part, part), part)
        return pltpu.make_async_copy(v.w_down.at[rows], v.wd.at[m], v.fetch.at[1])

    def fetch(m):
        fetch_up(m).start()
        fetch_down(m).start()


    for g in range(2):
        v.tok[:, g * columns : (g + 1) * columns] = v.tokens[g, 0].astype(F32).T

    def cut_tokens(d):
        rows = v.tok[pl.ds(pl.multiple_of(d * own, 8), own), :]
        both = jnp.concatenate([rows[:, :columns], rows[:, columns:]], axis=0)
        v.tb[core, d] = both.astype(BF16)

    loop(RANKS, cut_tokens)
    lines = []
    for vector in (v.b_up, v.skip_gain, v.ln_gain, v.ln_bias, v.layer_scale, v.b_down):
        line = vector[...].reshape(1, vector.shape[0])
        lines += [line[:, q * 128 : (q + 1) * 128] for q in range(vector.shape[0] // 128)]
    lines.append(jnp.zeros((32 - len(lines), 128), F32))
    v.vx[core] = jnp.concatenate(lines, axis=0)
    pl.semaphore_wait(barrier, RANKS)
    scatter(v.a1, v.tb.at[core], v.rb1.at[rank])
    v.rb1[rank] = v.tb[core, rank]
    for which in range(len(ASYNC)):
        bring(which).start()
    copy(v.tb.at[core], v.tb.at[core], v.tw, 0, twin).start()
    copy(v.vx.at[core], v.vx.at[core], v.tw, 1, twin).start()

    def spread(which, rows):
        block = jnp.concatenate([rows, jnp.zeros((128 - rows.shape[0], 128), F32)], axis=0)
        cols = block.T
        for q in range(15):
            v.vb[q // 3, which, q % 3 * 128 : (q % 3 + 1) * 128, :] = jnp.broadcast_to(
                cols[:, 12 + q : 13 + q], (128, 128)
            )
        return cols

    cols = spread(core, v.vx[core])
    for m in range(chunks):
        for q in range(2):
            v.bias[m, q * 128 : (q + 1) * 128, :] = jnp.broadcast_to(
                cols[:, 2 * m + q : 2 * m + q + 1], (128, 128)
            )
    for which in range(len(ASYNC)):
        bring(which).wait()
    for g in range(2):
        v.cot[:, g * columns : (g + 1) * columns] = v.cotangent[g, 0].astype(F32).T
    places_w = lax.broadcasted_iota(jnp.int32, (1, columns), 1)
    inside = jnp.concatenate(
        [(places_w < jnp.where(rank < heights[g], widths[g], 0)).astype(F32) for g in range(2)],
        axis=1,
    )
    v.inside[...] = jnp.broadcast_to(inside, (8, pixels))

    def mask_rows(q):
        rows = pl.ds(pl.multiple_of(q * 128, 128), 128)
        masked = v.cot[rows, :] * v.inside[0:1, :]
        v.gb[core, rows, :] = (masked * wide(v.vb[3, core, rows, :])).astype(BF16)

    loop(here // 128, mask_rows)
    copy(v.gb.at[core], v.gb.at[core], v.tw, 2, twin).start()

    lane = lax.broadcasted_iota(jnp.int32, (slab, lanes), 1) // per
    row = lax.broadcasted_iota(jnp.int32, (slab, lanes), 0)
    row = jnp.where(row >= own, row - own, row)
    v.pick[...] = (lane == row).astype(F32)
    chosen = lax.broadcasted_iota(jnp.int32, (here, lanes), 1) // per + rank * own
    chosen = (lax.broadcasted_iota(jnp.int32, (here, lanes), 0) == chosen).astype(F32)
    all_modes = jnp.concatenate(
        [v.log_step[...], jnp.zeros((6, here), F32)]
        + [v.log_decay[a] for a in range(2)]
        + [v.frequency[a] for a in range(2)]
        + [v.b_in[a, i] for i in range(2) for a in range(2)]
        + [v.c_out[a, i] for i in range(2) for a in range(2)],
        axis=0,
    )
    all_modes = jnp.dot(all_modes, chosen, precision=PRECISE, preferred_element_type=F32)
    mode = lax.broadcasted_iota(jnp.int32, (per, lanes), 1) % per
    mode = (mode == lax.broadcasted_iota(jnp.int32, (per, lanes), 0)).astype(F32)
    v.of_mode[...] = mode
    own_modes = jnp.sum(all_modes[8:].reshape(12, per, lanes) * mode[None], axis=1)
    v.modes[...] = jnp.concatenate([all_modes[:2], own_modes, own_modes[:2]], axis=0)
    mv = mode_values(v.modes[...])

    def powers(axis, place):
        angle = mv.step_im[axis : axis + 1] * place
        fade = jnp.exp(mv.step_re[axis : axis + 1] * place)
        return fade * jnp.cos(angle), fade * jnp.sin(angle)

    high_place = lax.broadcasted_iota(jnp.int32, (RANKS, lanes), 0).astype(F32)
    v.eh[0], v.eh[1] = powers(0, high_place)
    low_place = lax.broadcasted_iota(jnp.int32, (8, lanes), 0).astype(F32)
    base = powers(1, low_place)
    many = columns // 8
    v.ej[0], v.ej[1] = powers(
        1, 8.0 * lax.broadcasted_iota(jnp.int32, (many, lanes), 0).astype(F32)
    )
    coef_w = tuple(2.0 * part_of[1:2] for part_of in mv.coef)

    def fill(j):
        at = pl.ds(pl.multiple_of(j * 8, 8), 8)
        jump = (v.ej[0, pl.ds(j, 1), :], v.ej[1, pl.ds(j, 1), :])
        e_re, e_im = times(base, jump)
        v.ew[0, at, :] = e_re
        v.ew[1, at, :] = e_im
        v.kt[at, :] = coef_w[0] * e_re - coef_w[1] * e_im

    loop(many, fill)
    k_width = lax.dot_general(
        v.pick[...], v.kt[...], NT, precision=PRECISE, preferred_element_type=F32
    )
    k_both = by_table(k_width, v.to_hi, v.to_lo)
    k_re, k_im = k_both[:, :columns], k_both[:, columns:]
    first_lane = lax.broadcasted_iota(jnp.int32, (slab, columns), 1) == 0
    v.ks[0] = k_re
    v.ks[1] = jnp.where(first_lane, 0.0, k_im)
    v.ks[2] = jnp.where(first_lane, k_im, k_re)
    coef_h = tuple(2.0 * part_of[0:1] for part_of in mv.coef)
    v.kt[0:RANKS, :] = coef_h[0] * v.eh[0] - coef_h[1] * v.eh[1]

    taps = lax.dot_general(
        v.pick[...], v.kt[0:RANKS, :], NT, precision=PRECISE, preferred_element_type=F32
    )
    for l in range(RANKS):
        v.kh[l] = jnp.broadcast_to(taps[:, l : l + 1], (slab, 128))

    def turn(m):
        v.wut[m] = v.wu[m].T
        v.wdt[m] = v.wd[m].T


    all_slabs(v.a1, 1, v.rb1)
    loop(chunks, fetch)
    step_rows = 4

    def convolve(b):
        at = pl.ds(b * step_rows, step_rows)
        values = v.rb1[at].reshape(step_rows * slab, columns)
        shape = (step_rows, slab, columns)
        x_both = by_table(values, v.to_hi, v.to_lo)
        x_re, x_im = x_both[:, :columns].reshape(shape), x_both[:, columns:].reshape(shape)
        v.xs[0, at] = x_re
        v.xs[1, at] = x_im
        k0, k1, k2 = v.ks[0], v.ks[1], v.ks[2]
        y_both = jnp.concatenate([x_re * k0 - x_im * k1, x_re * k1 + x_im * k2], axis=2)
        y_both = y_both.reshape(step_rows * slab, 2 * columns)
        along = by_table(y_both, v.from_hi, v.from_lo)
        v.along[at] = along.astype(BF16).astype(F32).reshape(shape)

    loop(RANKS // step_rows, convolve)

    def by_tiles(body):
        def rows(r):
            for half in range(columns // 128):
                body(pl.ds(pl.multiple_of(r * 8, 8), 8), slice(half * 128, half * 128 + 128))

        loop(slab // 8, rows)

    def down_rows(at, cut):
        taps = [v.kh[l, at, :] for l in range(RANKS)]
        values = [v.along[i, at, cut] for i in range(RANKS)]
        for i in range(RANKS):
            total = taps[0] * values[i]
            for l in range(1, i + 1):
                total += taps[l] * values[i - l]
            v.tall[i, at, cut] = total

    by_tiles(down_rows)
    v.sb2[...] = v.tall[...].astype(BF16)
    scatter(v.a2, v.sb2, v.rb2.at[core, rank], each=True)
    v.rb2[core, rank] = v.sb2[rank]
    copy(v.rb2.at[core, rank], v.rb2.at[core, rank], v.fw, 0, twin).start()

    copy(v.vx.at[core], v.vx.at[1 - core], v.tw, 1, twin).wait_recv()
    spread(1 - core, v.vx[1 - core])
    pltpu.make_async_copy(v.wu, v.wu, v.fetch.at[0]).wait()
    pltpu.make_async_copy(v.wd, v.wd, v.fetch.at[1]).wait()
    loop(chunks, turn)
    v.branch[...] = jnp.zeros_like(v.branch)
    v.gn[...] = jnp.zeros_like(v.gn)

    def forward(k):
        d = partner(k)
        slab_copy(v.a2, k, v.sb2.at[d], v.rb2.at[core, d], d).wait_recv()
        copy(v.rb2.at[core, d], v.rb2.at[core, d], v.fw, 0, twin).start()

    loop(RANKS, forward, 1)
    copy(v.tb.at[core], v.tb.at[1 - core], v.tw, 0, twin).wait_recv()
    copy(v.rb2.at[core], v.rb2.at[1 - core], v.fw, 0, twin).wait_recv()

    eight = jnp.zeros((8, pixels), F32)

    def folded(values):
        return values.reshape(own // 8, 8, pixels).sum(axis=0)

    def mix(i, total):
        which, d = i // RANKS, lax.rem(i, RANKS)
        spatial = v.rb2[which, d].astype(F32)
        token = v.tb[which, d].astype(F32)
        skip = wide(v.vb[0, which, pl.ds(pl.multiple_of(d * own, 8), own), :])
        spatial = jnp.concatenate([spatial[:own], spatial[own:]], axis=1)
        token = jnp.concatenate([token[:own], token[own:]], axis=1)
        mixed = spatial + skip * token
        v.xhat[i] = mixed
        return total + folded(mixed)

    channels = 2 * here
    total = lax.fori_loop(0, 2 * RANKS, mix, eight)
    centre = jnp.sum(total, axis=0, keepdims=True) * (1.0 / channels)

    def squares(i, total):
        off = v.xhat[i] - centre
        return total + folded(off * off)

    total = lax.fori_loop(0, 2 * RANKS, squares, eight)
    spread_of = jnp.sum(total, axis=0, keepdims=True) * (1.0 / channels)
    inv_std = lax.rsqrt(spread_of + EPSILON)
    v.inv[...] = jnp.broadcast_to(inv_std, (8, pixels))

    def normalize(q):
        rows = []
        for k in range(2):
            i = 2 * q + k
            which, d = i // RANKS, lax.rem(i, RANKS)
            at = pl.ds(pl.multiple_of(d * own, 8), own)
            x_hat = (v.xhat[i] - centre) * inv_std
            v.xhat[i] = x_hat
            rows.append(x_hat * wide(v.vb[1, which, at, :]) + wide(v.vb[2, which, at, :]))
        at = pl.ds(pl.multiple_of(q * 2 * own, 16), 2 * own)
        v.normed[at, :] = jnp.concatenate(rows, axis=0).astype(BF16)

    loop(RANKS, normalize)
    copy(v.gb.at[core], v.gb.at[1 - core], v.tw, 2, twin).wait_recv()

    def feed(t):
        normed = v.normed[...]
        g_branch = v.gb[...].reshape(channels, pixels)
        hidden = jnp.dot(v.wut[t], normed, preferred_element_type=F32) + wide(v.bias[t])
        phi = 0.5 + 0.5 * lax.erf(hidden * (0.5**0.5))
        density = jnp.exp(-0.5 * hidden * hidden) * ((2.0 * jnp.pi) ** -0.5)
        active = (hidden * phi).astype(BF16)
        slope = phi + hidden * density
        g_active = jnp.dot(v.wd[t], g_branch, preferred_element_type=F32)
        g_hidden = (g_active * slope).astype(BF16)
        down = lax.dot_general(active, g_branch, NT, preferred_element_type=F32)
        down = down.astype(BF16).reshape(CUTS, 2, 2, part // CUTS // 4, channels)
        v.pd[pl.ds(CUTS * t, CUTS)] = down
        up = lax.dot_general(normed, g_hidden, NT, preferred_element_type=F32)
        up = up.astype(BF16)
        for q in range(CUTS):
            v.pu[CUTS * t + q] = up[up_cut(up.shape, q)].reshape(v.pu.shape[1:])
        v.gn[...] += jnp.dot(v.wu[t], g_hidden, preferred_element_type=F32)
        v.branch[...] += jnp.dot(v.wdt[t], active, preferred_element_type=F32)
        ones = jnp.ones((8, pixels), BF16)
        v.dbu[t] = lax.dot_general(ones, g_hidden, NT, preferred_element_type=F32)

    def share():
        v.gn_out[...] = v.gn[...].astype(BF16)
        copy(v.gn_out, v.gn_in, v.tw, 3, twin).start()
        theirs = pl.ds(pl.multiple_of((1 - core) * here, here), here)
        v.br_out[...] = v.branch[theirs, :].astype(BF16)
        copy(v.br_out, v.br_in, v.tw, 4, twin).start()

    def lane_sum(values):
        return sum(values[:, q * 128 : (q + 1) * 128] for q in range(pixels // 128))

    def norm_back():
        copy(v.gn_out, v.gn_in, v.tw, 3, twin).wait_recv()

        def whole(q, totals):
            at = pl.ds(pl.multiple_of(q * 2 * own, 16), 2 * own)
            g_normed = v.gn[at, :] + v.gn_in[at, :].astype(F32)
            v.gn[at, :] = g_normed
            one, two = totals
            for k in range(2):
                i = 2 * q + k
                which, d = i // RANKS, lax.rem(i, RANKS)
                gain = wide(v.vb[1, which, pl.ds(pl.multiple_of(d * own, 8), own), :])
                g_hat = g_normed[k * own : (k + 1) * own] * gain
                one = one + folded(g_hat)
                two = two + folded(g_hat * v.xhat[i])
            return one, two

        one, two = lax.fori_loop(0, RANKS, whole, (eight, eight))
        one = jnp.sum(one, axis=0, keepdims=True) * (1.0 / channels)
        two = jnp.sum(two, axis=0, keepdims=True) * (1.0 / channels)
        scale = v.inv[0:1, :]

        def each(d):
            at = pl.ds(pl.multiple_of(d * own, 8), own)
            x_hat = v.xhat[core * RANKS + d]
            g_normed = v.gn[pl.ds(pl.multiple_of(core * here + d * own, 8), own), :]
            g_mixed = scale * (g_normed * wide(v.vb[1, core, at, :]) - one - x_hat * two)
            v.gmix[at, :] = g_mixed
            v.sums[0, at, :] = lane_sum(g_mixed * v.tok[at, :])
            v.sums[1, at, :] = lane_sum(g_normed * x_hat)
            v.sums[2, at, :] = lane_sum(g_normed)
            both = jnp.concatenate([g_mixed[:, :columns], g_mixed[:, columns:]], axis=0)
            v.sb3[d] = both.astype(BF16)

        loop(RANKS, each)
        v.rb3[rank] = v.sb3[rank]

    def outputs():
        copy(v.br_out, v.br_in, v.tw, 4, twin).wait_recv()
        mask = v.inside[0:1, :]

        def rows(q):
            at = pl.ds(pl.multiple_of(q * 128, 128), 128)
            branch = v.branch[pl.ds(pl.multiple_of(core * here + q * 128, 128), 128), :]
            branch = branch + v.br_in[at, :].astype(F32) + wide(v.vb[4, core, at, :])
            masked = branch * mask
            v.sums[3, at, :] = lane_sum(v.gb[core, at, :].astype(F32))
            v.sums[4, at, :] = lane_sum(masked * v.cot[at, :])
            v.res[at, :] = v.tok[at, :] + masked * wide(v.vb[3, core, at, :])

        loop(here // 128, rows)
        for g in range(2):
            v.o_out[g, 0] = v.res[:, g * columns : (g + 1) * columns].T.astype(BF16)
        pltpu.make_async_copy(v.o_out, v.output, v.leave.at[2]).start()

    def convolve_back():
        all_slabs(v.a3, 1, v.rb3)
        v.tall[...] = v.rb3[...].astype(F32)

        def up_rows(at, cut):
            taps = [v.kh[l, at, :] for l in range(RANKS)]
            values = [v.tall[i, at, cut] for i in range(RANKS)]
            for i in range(RANKS):
                total = taps[0] * values[i]
                for l in range(1, RANKS - i):
                    total += taps[l] * values[i + l]
                v.galong[i, at, cut] = total.astype(BF16).astype(F32)

        by_tiles(up_rows)

        def lag_rows(at, cut):
            grads = [v.tall[i, at, cut] for i in range(RANKS)]
            values = [v.along[i, at, cut] for i in range(RANKS)]
            for l in range(RANKS):
                total = grads[l] * values[0]
                for i in range(l + 1, RANKS):
                    total += grads[i] * values[i - l]
                v.lags[l, at, cut] = total

        by_tiles(lag_rows)
        v.cross[...] = jnp.zeros_like(v.cross)

    def convolve_step(turn_of):
        block = lax.rem(z + turn_of, RANKS // step_rows)
        at = pl.ds(block * step_rows, step_rows)
        shape = (step_rows, slab, columns)
        values = v.galong[at].reshape(step_rows * slab, columns).astype(BF16)
        g_both = by_table(values, v.to_hi, v.to_lo)
        g_re, g_im = g_both[:, :columns].reshape(shape), g_both[:, columns:].reshape(shape)
        x_re, x_im = v.xs[0, at], v.xs[1, at]
        k0, k1, k2 = v.ks[0], v.ks[1], v.ks[2]
        y_both = jnp.concatenate([g_re * k0 + g_im * k1, g_im * k2 - g_re * k1], axis=2)
        y_both = y_both.reshape(step_rows * slab, 2 * columns)
        conv = by_table(y_both, v.from_hi, v.from_lo)
        v.sb4[at] = conv.reshape(shape).astype(BF16)
        v.cross[0] += (x_re * g_re).sum(axis=0)
        v.cross[1] += (x_im * g_im).sum(axis=0)
        v.cross[2] += (x_re * g_im - x_im * g_re).sum(axis=0)
        for q in range(step_rows):
            d = block * step_rows + q

            @pl.when(d != rank)
            def _():
                slab_copy(v.a4, 0, v.sb4.at[d], v.rb4.at[rank], d).start()

            @pl.when(d == rank)
            def _():
                v.rb4[rank] = v.sb4[rank]

    def kernel_grads():
        cross = [v.cross[q] for q in range(3)]
        zero_lane = lax.broadcasted_iota(jnp.int32, (slab, columns), 1) == 0
        c_re = cross[0] + jnp.where(zero_lane, 0.0, cross[1])
        c_im = jnp.where(zero_lane, cross[1], cross[2])
        dk_width = by_table(jnp.concatenate([c_re, c_im], axis=1), v.from_hi, v.from_lo)
        v.kt[...] = lax.dot_general(
            dk_width, v.pick[...], TN, precision=PRECISE, preferred_element_type=F32
        )

        lags = v.lags[...].reshape(RANKS * slab, columns)
        first = lags.astype(BF16)
        second = (lags - first.astype(F32)).astype(BF16)
        ones = jnp.ones((columns, 128), BF16)
        lags = jnp.dot(first, ones, preferred_element_type=F32)
        lags += jnp.dot(second, ones, preferred_element_type=F32)
        lags = lags.reshape(RANKS, slab, 128)
        for q in range(lanes // 128):
            cut = slice(q * 128, (q + 1) * 128)
            v.kth[:, cut] = jnp.sum(lags * v.pick[:, cut][None], axis=1)

    def parameters():
        def moments(dk, e_re, e_im):
            place = lax.broadcasted_iota(jnp.int32, dk.shape, 0).astype(F32)
            terms = (dk * e_re, dk * e_im)
            plain = [jnp.sum(term, axis=0, keepdims=True) for term in terms]
            timed = [jnp.sum(term * place, axis=0, keepdims=True) for term in terms]
            return plain + timed

        rows_h = moments(v.kth[...], v.eh[0], v.eh[1])
        rows_w = moments(v.kt[...], v.ew[0], v.ew[1])
        p_re, p_im, t_re, t_im = (
            2.0 * jnp.concatenate([h, w], axis=0) for h, w in zip(rows_h, rows_w)
        )
        plain, timed = (p_re, p_im), (t_re, t_im)
        mv = mode_values(v.modes[...])
        step, rate = mv.step, mv.rate
        zoh_plain = times(mv.zoh, plain)
        g_b = times(mv.c, zoh_plain)
        g_c = times(mv.b, zoh_plain)
        coef_timed = times(mv.coef, timed)
        prod_plain = times(mv.prod, plain)
        slope = times(
            (step * mv.once[0] - mv.zoh[0], step * mv.once[1] - mv.zoh[1]), mv.over
        )
        g_rate = times(prod_plain, slope)
        g_rate = (g_rate[0] + step * coef_timed[0], g_rate[1] + step * coef_timed[1])
        g_step = times(prod_plain, mv.once)[0] + times(coef_timed, rate)[0]
        rows = [
            step * g_step,
            g_rate[0] * rate[0],
            -g_rate[1],
            g_b[0],
            -g_b[1],
            g_c[0],
            -g_c[1],
            jnp.zeros_like(step),
        ]
        table = jnp.concatenate(rows, axis=0)
        z, y, x = rank // 4, (rank // 2) % 2, rank % 2
        blocks = [jnp.zeros((per, 128), F32) for _ in range(3)]
        at = lax.broadcasted_iota(jnp.int32, (128, lanes), 0)
        at -= lax.broadcasted_iota(jnp.int32, (128, lanes), 1) // per
        for k in range(5):
            chosen = (at == k * own).astype(BF16)
            for five in range(3 if k < 4 else 2):
                r = 5 * five + k
                values = (v.of_mode[...] * table[r : r + 1]).astype(BF16)
                blocks[five] += lax.dot_general(values, chosen, NT, preferred_element_type=F32)
        for five in range(3):
            v.pack[five * per : (five + 1) * per, :] = blocks[five].astype(BF16)
        ones = jnp.ones((8, 128), F32)
        vectors = [
            v.dbu[m, 0:1, q * 128 : (q + 1) * 128] for m in range(chunks) for q in range(part // 128)
        ]
        for k in range(5):
            line = lax.dot_general(
                ones, v.sums[k], NT, precision=PRECISE, preferred_element_type=F32
            )
            vectors += [line[0:1, q * 128 : (q + 1) * 128] for q in range(here // 128)]
        vectors.append(jnp.zeros((32 - len(vectors), 128), F32))
        v.pack[3 * per :, :] = jnp.concatenate(vectors, axis=0).astype(BF16)
        v.gathered[z, y, x] = v.pack[...]

        def to(k):
            target = (lax.rem(z + k, 4) * 4 + y * 2 + x, core)
            copy(v.pack, v.gathered.at[z, y, x], v.ga, k, target).start()

        loop(4, to, 1)

    def gather_across():
        def wait(k):
            s = lax.rem(z + 4 - k, 4)
            copy(v.pack, v.gathered.at[s, y, x], v.ga, k, (s * 4 + y * 2 + x, core)).wait_recv()

        loop(4, wait, 1)
        mine = v.gathered.at[:, y, x]
        copy(mine, mine, v.ga, 4, across).start()

    def gather_beside():
        theirs = v.gathered.at[:, 1 - y, x]
        copy(theirs, theirs, v.ga, 4, across).wait_recv()
        mine = v.gathered.at[:, :, x]
        copy(mine, mine, v.ga, 5, beside).start()

    def gather_done():
        theirs = v.gathered.at[:, :, 1 - x]
        copy(theirs, theirs, v.ga, 5, beside).wait_recv()
        pltpu.make_async_copy(v.gathered, v.all_gathered, v.leave.at[4]).start()

    def token_grads():
        all_slabs(v.a4, 1, v.rb4)

        def rows(d):
            at = pl.ds(pl.multiple_of(d * own, 8), own)
            conv = v.rb4[d].astype(F32)
            conv = jnp.concatenate([conv[:own], conv[own:]], axis=1)
            skip = wide(v.vb[0, core, at, :])
            v.res[at, :] = v.cot[at, :] + skip * v.gmix[at, :] + conv

        loop(RANKS, rows)
        for g in range(2):
            v.t_out[g, 0] = v.res[:, g * columns : (g + 1) * columns].T.astype(BF16)
        pltpu.make_async_copy(v.t_out, v.d_tokens, v.leave.at[3]).start()

    down = types.SimpleNamespace(
        part=v.pd,
        from_first=v.d1,
        from_outer=v.d2,
        from_inner=v.d3,
        from_third=v.d4,
        full=v.fd,
        keep=x,
        first=beside,
        third=across,
    )
    up = types.SimpleNamespace(
        part=v.pu,
        from_first=v.u1,
        from_outer=v.u2,
        from_inner=v.u3,
        from_third=v.u4,
        full=v.fu,
        keep=y,
        first=across,
        third=beside,
    )

    def leave(c):
        return (
            pltpu.make_async_copy(v.fd.at[c], v.down.at[c], v.leave.at[0]),
            pltpu.make_async_copy(v.fu.at[c], v.up.at[c], v.leave.at[1]),
        )


    def advance(stage, c, role):
        reduce_stage(stage, c, role, places, (down, up), v.sent, v.landed)

    def known(stage, c):
        live = (c * (pieces - 1 - c) >= 0).astype(jnp.int32)
        advance(stage, c, live * (1 + middle))
        if stage == STAGES - 1:

            @pl.when(live > 0)
            def _():
                for one in leave(c):
                    one.start()

    events = {
        0: norm_back,
        1: outputs,
        3: convolve_back,
        7: kernel_grads,
        8: parameters,
        10: gather_across,
        12: gather_beside,
        20: gather_done,
        16: token_grads,
    }

    def feed_and_send(t):
        feed(t)
        for q in range(CUTS):
            c = CUTS * t + q
            advance(0, c, (c < 6).astype(jnp.int32) * (1 + middle))
        known(1, t - 3)
        known(2, t - 3 - 2)

    loop(chunks, feed_and_send)
    share()
    for ahead in range(chunks - 3, 4):
        known(1, jnp.int32(ahead))
        known(2, jnp.int32(ahead - 2))
        known(3, jnp.int32(ahead - 4))

    def tick(t, carry):
        for when, event in events.items():
            pl.when(t == when)(event)
        batch = t - 0

        @pl.when(batch * (2 - 1 - batch) >= 0)
        def _():
            scatter(v.a3, v.sb3, v.rb3.at[rank], first=1 + 8 * batch, count=8)

        turn_of = t - 3

        @pl.when(turn_of * (RANKS // step_rows - 1 - turn_of) >= 0)
        def _():
            convolve_step(turn_of)

        for q in range(1):
            c = 6 + 1 * (t - 0) + q
            known(0, jnp.where(t < 0, pieces, c))
        for stage, start in enumerate((0,2,4,6,8,10,12,14,16), 1):
            known(stage, t + 4 - start)
        return carry

    lax.fori_loop(0, pieces + (0,2,4,6,8,10,12,14,16)[-1] - 4, tick, 0)

    pltpu.make_async_copy(v.gathered, v.all_gathered, v.leave.at[4]).wait()
    pltpu.make_async_copy(v.fd, v.down, v.leave.at[0]).wait()
    pltpu.make_async_copy(v.fu, v.up, v.leave.at[1]).wait()
    pltpu.make_async_copy(v.o_out, v.output, v.leave.at[2]).wait()
    pltpu.make_async_copy(v.t_out, v.d_tokens, v.leave.at[3]).wait()
    all_slabs(v.a1, 0, v.rb1)
    all_slabs(v.a2, 0, v.sb2)
    all_slabs(v.a3, 0, v.sb3)
    all_slabs(v.a4, 0, v.sb4)
    reduce_sent(middle, (down, up), v.sent)
    copy(v.tb.at[core], v.tb.at[core], v.tw, 0, twin).wait_send()
    copy(v.vx.at[core], v.vx.at[core], v.tw, 1, twin).wait_send()
    copy(v.gb.at[core], v.gb.at[core], v.tw, 2, twin).wait_send()
    copy(v.gn_out, v.gn_in, v.tw, 3, twin).wait_send()
    copy(v.br_out, v.br_in, v.tw, 4, twin).wait_send()

    copy(v.rb2.at[core], v.rb2.at[core], v.fw, 0, twin).wait_send()

    def gather_sent(k):
        target = (lax.rem(z + k, 4) * 4 + y * 2 + x, core)
        copy(v.pack, v.gathered.at[z, y, x], v.ga, k, target).wait_send()

    loop(4, gather_sent, 1)
    mine = v.gathered.at[:, y, x]
    copy(mine, mine, v.ga, 4, across).wait_send()
    mine = v.gathered.at[:, :, x]
    copy(mine, mine, v.ga, 5, beside).wait_send()


def finish_kernel(own, *refs):
    ins, outs, small, near, wide, sems = refs[:5], refs[5:20], refs[20:33], refs[33:36], refs[36:38], refs[38:]
    brought, moved, left = sems
    pieces, rows = near[0].shape[0], wide[0].shape[1]
    group = pieces // brought.shape[1]

    def bring(which, m):
        some = pl.ds(m * group, group)
        return pltpu.make_async_copy(
            ins[which].at[some], near[which].at[some], brought.at[which, m]
        )

    def leave(which, m):
        if which == 0:
            place = outs[0].at[pl.ds(pl.multiple_of(m * rows, rows), rows)]
        else:
            up_rows, up_cols = wide[1].shape[1:]
            place = outs[1].at[
                pl.ds(pl.multiple_of(m % CUTS // 2 * up_rows, 16), up_rows),
                pl.ds(pl.multiple_of((m // CUTS * 2 + m % 2) * up_cols, 128), up_cols),
            ]
        return pltpu.make_async_copy(wide[which].at[m], place, left.at[which])

    brings = [
        pltpu.make_async_copy(src, dst, brought.at[2, k])
        for k, (src, dst) in enumerate(zip(ins[2:], (near[2],) + small[:2]))
    ]
    moves = [
        pltpu.make_async_copy(src, dst, moved.at[k])
        for k, (src, dst) in enumerate(zip(small, outs[2:]))
    ]

    def each(count, body):
        def step(m, carry):
            for which in range(2):
                body(which, m)
            return carry

        lax.fori_loop(0, count, step, 0)

    def widen(which, m):
        bring(which, m).wait()
        for q in range(group):
            one = group * m + q
            wide[which][one] = near[which][one].reshape(wide[which].shape[1:]).astype(F32)
            leave(which, one).start()

    for one in brings:
        one.start()
    each(brought.shape[1], lambda which, m: bring(which, m).start())
    for one in brings:
        one.wait()
    widen_small(own, near[2], small[2:])
    for one in moves:
        one.start()
    each(brought.shape[1], widen)
    for which in range(2):
        pltpu.make_async_copy(wide[which], wide[which], left.at[which]).wait()
    for one in moves:
        one.wait()


def widen_small(own, gathered, small):
    d_log_step, d_log_decay, d_frequency, d_b_in, d_c_out = small[:5]
    per, here = d_log_decay.shape[1:]
    lane = lax.broadcasted_iota(jnp.int32, (per, 128), 1)
    whole = []
    for r in range(14):
        five, k = divmod(r, 5)
        windows = [jnp.zeros((per, 128), F32) for _ in range(here // 128)]
        for s in range(RANKS):
            block = gathered[s // 4, s // 2 % 2, s % 2, five * per : (five + 1) * per, :]
            turned = pltpu.roll(block.astype(F32), (own * (s - k)) % 128, 1)
            window, low = divmod(own * s, 128)
            inside = (lane >= low) & (lane < low + own)
            windows[window] = jnp.where(inside, turned, windows[window])
            if low + own > 128:
                inside = lane < low + own - 128
                windows[window + 1] = jnp.where(inside, turned, windows[window + 1])
        whole.append(jnp.concatenate(windows, axis=1))
    for a in range(2):
        d_log_step[a : a + 1, :] = jnp.sum(whole[a], axis=0, keepdims=True)
        d_log_decay[a] = whole[2 + a]
        d_frequency[a] = whole[4 + a]
        for i in range(2):
            d_b_in[a, i] = whole[6 + 2 * i + a]
            d_c_out[a, i] = whole[10 + 2 * i + a]
    sums = jnp.zeros((32, 128), F32)
    for s in range(RANKS):
        sums += gathered[s // 4, s // 2 % 2, s % 2, 3 * per :, :].astype(F32)
    row = 0
    for vector in small[5:]:
        for q in range(vector.shape[0] // 128):
            vector[pl.ds(q * 128, 128)] = sums[row]
            row += 1


def block_shards(
    tokens,
    heights,
    widths,
    log_step,
    log_decay,
    frequency,
    b_in,
    c_out,
    skip_gain,
    ln_gain,
    ln_bias,
    w_up,
    b_up,
    w_down,
    b_down,
    layer_scale,
    cotangent,
):
    columns, here = tokens.shape[2:]
    modes_each = log_decay.shape[2]
    hidden = w_up.shape[1]
    own = here // RANKS
    chunks = hidden // 256
    part = hidden // chunks
    channels = 2 * here
    pixels = 2 * columns
    lanes = own * modes_each
    tables = spectral_tables(columns)
    slabs = (RANKS, 2 * own, columns)
    tall = pltpu.VMEM(slabs, F32)
    in_vmem = pl.BlockSpec(memory_space=pltpu.VMEM)
    in_smem = pl.BlockSpec(memory_space=pltpu.SMEM)
    anywhere = pl.BlockSpec(memory_space=pl.ANY)
    inputs = dict(
        tokens=(tokens, in_vmem),
        cotangent_in=(cotangent, anywhere),
        heights=(heights, in_smem),
        widths=(widths, in_smem),
        log_step_in=(log_step, anywhere),
        log_decay_in=(log_decay.swapaxes(-1, -2), anywhere),
        frequency_in=(frequency.swapaxes(-1, -2), anywhere),
        b_in_in=(b_in.swapaxes(-1, -2), anywhere),
        c_out_in=(c_out.swapaxes(-1, -2), anywhere),
        b_up=(b_up, in_vmem),
        skip_gain=(skip_gain, in_vmem),
        ln_gain=(ln_gain, in_vmem),
        ln_bias=(ln_bias, in_vmem),
        layer_scale=(layer_scale, in_vmem),
        b_down=(b_down, in_vmem),
        w_up=(w_up, anywhere),
        w_down=(w_down, anywhere),
        to_hi_in=(tables[0], anywhere),
        to_lo_in=(tables[1], anywhere),
        from_hi_in=(tables[2], anywhere),
        from_lo_in=(tables[3], anywhere),
    )
    down_shape = (CUTS * chunks, 2, 2, part // CUTS // 4, channels)
    up_shape = (CUTS * chunks, 2, 2, channels // (2 * CUTS), part // 2)
    outs = dict(
        output=(jax.ShapeDtypeStruct(tokens.shape, BF16), anywhere),
        d_tokens=(jax.ShapeDtypeStruct(tokens.shape, BF16), anywhere),
        down=(jax.ShapeDtypeStruct(down_shape, BF16), anywhere),
        up=(jax.ShapeDtypeStruct(up_shape, BF16), anywhere),
        all_gathered=(
            jax.ShapeDtypeStruct((4, 2, 2, 3 * modes_each + 32, 128), BF16),
            anywhere,
        ),
    )
    low_slabs = pltpu.VMEM(slabs, BF16)
    both_slabs = pltpu.VMEM((2,) + slabs, BF16)
    scratch = dict(
        wu=pltpu.VMEM((chunks, channels, part), BF16),
        wd=pltpu.VMEM((chunks, part, channels), BF16),
        wut=pltpu.VMEM((chunks, part, channels), BF16),
        wdt=pltpu.VMEM((chunks, channels, part), BF16),
        tok=pltpu.VMEM((here, pixels), F32),
        cot=pltpu.VMEM((here, pixels), F32),
        gmix=pltpu.VMEM((here, pixels), F32),
        res=pltpu.VMEM((here, pixels), F32),
        tb=both_slabs,
        rb1=low_slabs,
        sb2=low_slabs,
        rb2=both_slabs,
        sb3=low_slabs,
        rb3=low_slabs,
        sb4=low_slabs,
        rb4=low_slabs,
        vx=pltpu.VMEM((2, 32, 128), F32),
        vb=pltpu.VMEM((5, 2, here, 128), F32),
        bias=pltpu.VMEM((chunks, part, 128), F32),
        inside=pltpu.VMEM((8, pixels), F32),
        inv=pltpu.VMEM((8, pixels), F32),
        gb=pltpu.VMEM((2, here, pixels), BF16),
        modes=pltpu.VMEM((16, lanes), F32),
        of_mode=pltpu.VMEM((modes_each, lanes), F32),
        cross=pltpu.VMEM((3, 2 * own, columns), F32),
        pick=pltpu.VMEM((2 * own, lanes), F32),
        eh=pltpu.VMEM((2, RANKS, lanes), F32),
        ej=pltpu.VMEM((2, columns // 8, lanes), F32),
        ew=pltpu.VMEM((2, columns, lanes), F32),
        kt=pltpu.VMEM((columns, lanes), F32),
        kth=pltpu.VMEM((RANKS, lanes), F32),
        ks=pltpu.VMEM((3, 2 * own, columns), F32),
        kh=pltpu.VMEM((RANKS, 2 * own, 128), F32),
        xs=pltpu.VMEM((2,) + slabs, F32),
        along=tall,
        tall=tall,
        galong=tall,
        lags=tall,
        xhat=pltpu.VMEM((2 * RANKS, own, pixels), F32),
        normed=pltpu.VMEM((channels, pixels), BF16),
        branch=pltpu.VMEM((channels, pixels), F32),
        gn=pltpu.VMEM((channels, pixels), F32),
        gn_out=pltpu.VMEM((channels, pixels), BF16),
        gn_in=pltpu.VMEM((channels, pixels), BF16),
        br_out=pltpu.VMEM((here, pixels), BF16),
        br_in=pltpu.VMEM((here, pixels), BF16),
        dbu=pltpu.VMEM((chunks, 8, part), F32),
        sums=pltpu.VMEM((5, here, 128), F32),
        pack=pltpu.VMEM((3 * modes_each + 32, 128), BF16),
        fetch=pltpu.SemaphoreType.DMA((2,)),
        leave=pltpu.SemaphoreType.DMA((5,)),
        gathered=pltpu.VMEM((4, 2, 2, 3 * modes_each + 32, 128), BF16),
        bring=pltpu.SemaphoreType.DMA((len(ASYNC),)),
        o_out=pltpu.VMEM(tokens.shape, BF16),
        t_out=pltpu.VMEM(tokens.shape, BF16),
        cotangent=pltpu.VMEM(cotangent.shape, BF16),
        log_step=pltpu.VMEM(log_step.shape, F32),
        log_decay=pltpu.VMEM((2, modes_each, here), F32),
        frequency=pltpu.VMEM((2, modes_each, here), F32),
        b_in=pltpu.VMEM((2, 2, modes_each, here), F32),
        c_out=pltpu.VMEM((2, 2, modes_each, here), F32),
        to_hi=pltpu.VMEM(tables[0].shape, BF16),
        to_lo=pltpu.VMEM(tables[1].shape, BF16),
        from_hi=pltpu.VMEM(tables[2].shape, BF16),
        from_lo=pltpu.VMEM(tables[3].shape, BF16),
    )

    def reduction(shape):
        count, halves, pieces, rows, width = shape
        whole = pltpu.VMEM(shape, BF16)
        half = pltpu.VMEM((count, pieces, rows, width), BF16)
        piece = pltpu.VMEM((count, rows, width), BF16)
        return whole, half, piece, piece, piece, whole

    down_scratch, up_scratch = reduction(down_shape), reduction(up_shape)
    scratch.update(
        zip(("pd", "d1", "d2", "d3", "d4", "fd"), down_scratch),
    )
    scratch.update(
        zip(("pu", "u1", "u2", "u3", "u4", "fu"), up_scratch),
    )
    one_each = pltpu.SemaphoreType.DMA((2, 1))
    scratch.update(a1=one_each, a3=one_each, a4=one_each, fw=one_each)
    scratch.update(a2=pltpu.SemaphoreType.DMA((2, RANKS)))
    scratch.update(sent=pltpu.SemaphoreType.DMA((9,)))
    scratch.update(landed=pltpu.SemaphoreType.DMA((9, CUTS * chunks)))
    scratch.update(tw=pltpu.SemaphoreType.DMA((2, 5)), ga=pltpu.SemaphoreType.DMA((2, 6)))
    names = tuple(inputs) + tuple(outs) + tuple(scratch)
    output, d_tokens, down, up, gathered = pl.pallas_call(
        functools.partial(block_kernel, names),
        out_shape=tuple(shape for shape, _ in outs.values()),
        in_specs=[spec for _, spec in inputs.values()],
        out_specs=tuple(spec for _, spec in outs.values()),
        scratch_shapes=list(scratch.values()),
        compiler_params=pltpu.CompilerParams(
            collective_id=0, has_side_effects=True, vmem_limit_bytes=62 << 20
        ),
    )(*(value for value, _ in inputs.values()))
    result = (
        jax.ShapeDtypeStruct((hidden, channels), F32),
        jax.ShapeDtypeStruct((channels, hidden), F32),
        output,
        d_tokens,
        log_step,
        jax.ShapeDtypeStruct((2, modes_each, here), F32),
        jax.ShapeDtypeStruct((2, modes_each, here), F32),
        jax.ShapeDtypeStruct((2, 2, modes_each, here), F32),
        jax.ShapeDtypeStruct((2, 2, modes_each, here), F32),
        b_up,
        skip_gain,
        ln_gain,
        ln_bias,
        b_down,
        layer_scale,
    )
    result = tuple(jax.ShapeDtypeStruct(one.shape, one.dtype) for one in result)
    (
        d_w_down,
        d_w_up,
        output,
        d_tokens,
        d_log_step,
        d_log_decay,
        d_frequency,
        d_b_in,
        d_c_out,
        d_b_up,
        d_skip_gain,
        d_ln_gain,
        d_ln_bias,
        d_b_down,
        d_layer_scale,
    ) = pl.pallas_call(
        functools.partial(finish_kernel, own),
        out_shape=result,
        in_specs=[anywhere] * 5,
        out_specs=(anywhere,) * 15,
        scratch_shapes=[pltpu.VMEM(one.shape, one.dtype) for one in result[2:]]
        + [pltpu.VMEM(one.shape, BF16) for one in (down, up, gathered)]
        + [
            pltpu.VMEM((CUTS * chunks, part // CUTS, channels), F32),
            pltpu.VMEM((CUTS * chunks, channels * 2 // CUTS, part // 2), F32),
            pltpu.SemaphoreType.DMA((3, chunks)),
            pltpu.SemaphoreType.DMA((13,)),
            pltpu.SemaphoreType.DMA((2,)),
        ],
        compiler_params=pltpu.CompilerParams(vmem_limit_bytes=62 << 20),
    )(down, up, gathered, output, d_tokens)
    return (
        output,
        d_tokens,
        d_log_step,
        d_log_decay.swapaxes(-1, -2),
        d_frequency.swapaxes(-1, -2),
        d_b_in.swapaxes(-1, -2),
        d_c_out.swapaxes(-1, -2),
        d_skip_gain,
        d_ln_gain,
        d_ln_bias,
        d_w_up,
        d_b_up,
        d_w_down,
        d_b_down,
        d_layer_scale,
    )


def shards(
    tokens,
    heights,
    widths,
    log_step,
    log_decay,
    frequency,
    b_in,
    c_out,
    skip_gain,
    ln_gain,
    ln_bias,
    w_up,
    b_up,
    w_down,
    b_down,
    layer_scale,
    cotangent,
):
    row_count = lax.axis_size("rows")
    row_rank = lax.axis_index("rows")
    grid_count, rows_here, columns, channels = tokens.shape
    all_channels = channels * lax.axis_size("ch")
    height = rows_here * row_count
    own_count = channels // row_count
    first_chan = row_rank * own_count
    pixels = grid_count * rows_here * columns
    token_f = tokens.astype(jnp.float32)
    width_tables = make_tables(columns)
    height_tables = make_tables(height)
    own_params = tuple(
        lax.dynamic_slice_in_dim(param, first_chan, own_count, param.ndim - trailing)
        for param, trailing in (
            (log_step, 1),
            (log_decay, 2),
            (frequency, 2),
            (b_in, 2),
            (c_out, 2),
        )
    )
    width_params = tuple(param[1] for param in own_params)
    height_params = tuple(param[0] for param in own_params)
    k_width, width_pull = jax.vjp(lambda params: make_kernel(params, columns), width_params)
    k_height, height_pull = jax.vjp(lambda params: make_kernel(params, height), height_params)
    kw_re, kw_im = kernel_spectrum(k_width, width_tables)
    kh_re, kh_im = kernel_spectrum(k_height, height_tables)
    kh_re = kh_re[:, None, :]
    kh_im = kh_im[:, None, :]
    pencil_tokens = lax.all_to_all(tokens, "rows", split_axis=3, concat_axis=1, tiled=True)
    x_re, x_im = to_spectrum(pencil_tokens.astype(jnp.float32), width_tables, "fw,grwc->grfc")
    along_width = from_spectrum(
        x_re * kw_re - x_im * kw_im, x_re * kw_im + x_im * kw_re, width_tables, "fw,grfc->grwc"
    ).astype(jnp.bfloat16)
    p_re, p_im = to_spectrum(along_width.astype(jnp.float32), height_tables, "fh,ghwc->gfwc")
    mixed_cols = from_spectrum(
        p_re * kh_re - p_im * kh_im, p_re * kh_im + p_im * kh_re, height_tables, "fh,gfwc->ghwc"
    ).astype(jnp.bfloat16)
    back_rows = lax.all_to_all(mixed_cols, "rows", split_axis=1, concat_axis=3, tiled=True)
    mixed = back_rows.astype(jnp.float32) + skip_gain * token_f
    flat_mixed = mixed.reshape(pixels, channels)
    sum_one, sum_two = lax.psum(
        (jnp.sum(flat_mixed, axis=1), jnp.sum(flat_mixed * flat_mixed, axis=1)), "ch"
    )
    centre = sum_one / all_channels
    spread = sum_two / all_channels - centre * centre
    inv_std = lax.rsqrt(spread + EPSILON)[:, None]
    x_hat = (flat_mixed - centre[:, None]) * inv_std
    normed = (x_hat * ln_gain + ln_bias).astype(jnp.bfloat16)
    hidden = (
        jnp.dot(
            lax.all_gather(normed, "ch", axis=1, tiled=True),
            w_up,
            preferred_element_type=jnp.float32,
        )
        + b_up
    )
    active = jax.nn.gelu(hidden, approximate=False).astype(jnp.bfloat16)
    partials = jnp.dot(active, w_down, preferred_element_type=jnp.float32)
    branch = (
        lax.psum_scatter(
            partials.astype(jnp.bfloat16), "ch", scatter_dimension=1, tiled=True
        ).astype(jnp.float32)
        + b_down
    )
    row_ids = row_rank * rows_here + jnp.arange(rows_here, dtype=jnp.int32)
    col_ids = jnp.arange(columns, dtype=jnp.int32)
    inside = (row_ids[None, :, None] < heights[:, None, None]) & (
        col_ids[None, None, :] < widths[:, None, None]
    )
    inside = inside.astype(jnp.float32).reshape(pixels, 1)
    flat_tokens = token_f.reshape(pixels, channels)
    output = (
        (flat_tokens + inside * layer_scale * branch).astype(jnp.bfloat16).reshape(tokens.shape)
    )
    over_rows = (((0,), (0,)), ((), ()))
    over_cols = (((1,), (1,)), ((), ()))
    g_flat = cotangent.astype(jnp.float32).reshape(pixels, channels)
    g_masked = g_flat * inside
    g_branch = (g_masked * layer_scale).astype(jnp.bfloat16)
    d_layer_scale = jnp.sum(g_masked * branch, axis=0)
    d_b_down = jnp.sum(g_branch.astype(jnp.float32), axis=0)
    g_branch_all = lax.all_gather(g_branch, "ch", axis=1, tiled=True)
    d_w_down = lax.dot_general(active, g_branch_all, over_rows, preferred_element_type=jnp.float32)
    g_active = lax.dot_general(g_branch_all, w_down, over_cols, preferred_element_type=jnp.float32)
    gelu_pull = jax.vjp(lambda values: jax.nn.gelu(values, approximate=False), hidden)[1]
    g_hidden = gelu_pull(g_active)[0].astype(jnp.bfloat16)
    d_b_up = jnp.sum(g_hidden.astype(jnp.float32), axis=0)
    d_w_up = lax.dot_general(
        lax.all_gather(normed, "ch", axis=1, tiled=True),
        g_hidden,
        over_rows,
        preferred_element_type=jnp.float32,
    )
    g_terms = lax.dot_general(g_hidden, w_up, over_cols, preferred_element_type=jnp.float32)
    g_normed = lax.psum_scatter(g_terms, "ch", scatter_dimension=1, tiled=True)
    d_ln_gain = jnp.sum(g_normed * x_hat, axis=0)
    d_ln_bias = jnp.sum(g_normed, axis=0)
    g_hat = g_normed * ln_gain
    sum_grad, sum_cross = lax.psum((jnp.sum(g_hat, axis=1), jnp.sum(g_hat * x_hat, axis=1)), "ch")
    g_mixed = inv_std * (
        g_hat - sum_grad[:, None] / all_channels - x_hat * sum_cross[:, None] / all_channels
    )
    d_skip_gain = jnp.sum(g_mixed * flat_tokens, axis=0)
    g_spatial = g_mixed.astype(jnp.bfloat16).reshape(tokens.shape)
    pencil_grad = lax.all_to_all(g_spatial, "rows", split_axis=3, concat_axis=1, tiled=True)
    gp_re, gp_im = to_spectrum(pencil_grad.astype(jnp.float32), height_tables, "fh,ghwc->gfwc")
    vp_re, vp_im = p_re, p_im
    g_pencil_along = from_spectrum(
        gp_re * kh_re + gp_im * kh_im, gp_im * kh_re - gp_re * kh_im, height_tables, "fh,gfwc->ghwc"
    ).astype(jnp.bfloat16)
    cross_re = jnp.sum(vp_re * gp_re + vp_im * gp_im, axis=(0, 2))
    cross_im = jnp.sum(vp_re * gp_im - vp_im * gp_re, axis=(0, 2))
    dk_height = kernel_from_cross(cross_re, cross_im, height_tables)
    g_along = g_pencil_along
    ga_re, ga_im = to_spectrum(g_along.astype(jnp.float32), width_tables, "fw,grwc->grfc")
    g_conv = from_spectrum(
        ga_re * kw_re + ga_im * kw_im, ga_im * kw_re - ga_re * kw_im, width_tables, "fw,grfc->grwc"
    )
    g_conv = lax.all_to_all(
        g_conv.astype(jnp.bfloat16), "rows", split_axis=1, concat_axis=3, tiled=True
    ).astype(jnp.float32)
    wide_re = jnp.sum(x_re * ga_re + x_im * ga_im, axis=(0, 1))
    wide_im = jnp.sum(x_re * ga_im - x_im * ga_re, axis=(0, 1))
    dk_width = kernel_from_cross(wide_re, wide_im, width_tables)
    d_tokens = ((g_flat + g_mixed * skip_gain).reshape(tokens.shape) + g_conv).astype(jnp.bfloat16)
    width_grads = width_pull(dk_width)[0]
    height_grads = height_pull(dk_height)[0]

    def gathered(pieces, dim_num):
        return lax.all_gather(jnp.stack(pieces), "rows", axis=dim_num, tiled=True)

    param_grads = tuple(
        gathered(pair, dim_num)
        for pair, dim_num in zip(zip(height_grads, width_grads), (1, 1, 1, 2, 2))
    )
    d_w_down, d_w_up, d_skip_gain, d_ln_gain, d_ln_bias, d_b_up, d_b_down, d_layer_scale = lax.psum(
        (d_w_down, d_w_up, d_skip_gain, d_ln_gain, d_ln_bias, d_b_up, d_b_down, d_layer_scale),
        "rows",
    )
    return (output, d_tokens) + param_grads + (
        d_skip_gain,
        d_ln_gain,
        d_ln_bias,
        d_w_up,
        d_b_up,
        d_w_down,
        d_b_down,
        d_layer_scale,
    )


def solution(mesh):
    one_row_each = mesh.shape["rows"] == RANKS and mesh.shape["ch"] == 2
    return jax.shard_map(
        block_shards if one_row_each else shards,
        mesh=mesh,
        in_specs=(
            P(None, "rows", None, "ch"),
            P(),
            P(),
            P(None, "ch"),
            P(None, "ch", None),
            P(None, "ch", None),
            P(None, None, "ch", None),
            P(None, None, "ch", None),
            P("ch"),
            P("ch"),
            P("ch"),
            P(None, "ch"),
            P("ch"),
            P("ch", None),
            P("ch"),
            P("ch"),
            P(None, "rows", None, "ch"),
        ),
        out_specs=(
            P(None, "rows", None, "ch"),
            P(None, "rows", None, "ch"),
            P(None, "ch"),
            P(None, "ch", None),
            P(None, "ch", None),
            P(None, None, "ch", None),
            P(None, None, "ch", None),
            P("ch"),
            P("ch"),
            P("ch"),
            P(None, "ch"),
            P("ch"),
            P("ch", None),
            P("ch"),
            P("ch"),
        ),
        check_vma=False,
    )
```

```python
import functools
import types

import jax
import jax.numpy as jnp
import numpy as np
from jax import lax
from jax.experimental import pallas as pl
from jax.experimental.pallas import tpu as pltpu
from jax.sharding import PartitionSpec as P

PRECISE = lax.Precision.HIGHEST
EPSILON = 1e-06
MESH = pl.DeviceIdType.MESH


def make_tables(length):
    freq_ids = jnp.arange(length + 1, dtype=jnp.int32)[:, None]
    places = jnp.arange(length, dtype=jnp.int32)[None, :]
    turns = freq_ids * places % (2 * length)
    angles = turns.astype(jnp.float32) * (jnp.pi / length)
    cosine = jnp.cos(angles)
    sine_t = jnp.sin(angles)
    weights = jnp.where((freq_ids == 0) | (freq_ids == length), 1.0, 2.0) / (2.0 * length)
    return (cosine, sine_t, cosine * weights, sine_t * weights)


def to_spectrum(values, tables, pattern):
    real_part = jnp.einsum(pattern, tables[0], values, precision=PRECISE)
    imag_part = -jnp.einsum(pattern, tables[1], values, precision=PRECISE)
    return (real_part, imag_part)


def from_spectrum(real_part, imag_part, tables, pattern):
    return jnp.einsum(pattern, tables[2], real_part, precision=PRECISE) - jnp.einsum(
        pattern, tables[3], imag_part, precision=PRECISE
    )


def kernel_spectrum(kernel, tables):
    real_part = jnp.dot(tables[0], kernel, precision=PRECISE)
    imag_part = -jnp.dot(tables[1], kernel, precision=PRECISE)
    return (real_part, imag_part)


def kernel_from_cross(cross_re, cross_im, tables):
    contract = (((0,), (0,)), ((), ()))
    return lax.dot_general(tables[2], cross_re, contract, precision=PRECISE) - lax.dot_general(
        tables[3], cross_im, contract, precision=PRECISE
    )


def make_kernel(params, length):
    log_step, log_decay, frequency, b_in, c_out = params
    step_size = jnp.exp(log_step)[:, None]
    decay_re = -jnp.exp(log_decay)
    step_re = step_size * decay_re
    step_im = step_size * frequency
    half_sin = jnp.sin(0.5 * step_im)
    num_re = jnp.expm1(step_re) * jnp.cos(step_im) - 2.0 * half_sin * half_sin
    num_im = jnp.exp(step_re) * jnp.sin(step_im)
    divisor = decay_re * decay_re + frequency * frequency
    zoh_re = (num_re * decay_re + num_im * frequency) / divisor
    zoh_im = (num_im * decay_re - num_re * frequency) / divisor
    prod_re = b_in[0] * c_out[0] - b_in[1] * c_out[1]
    prod_im = b_in[0] * c_out[1] + b_in[1] * c_out[0]
    coef_re = prod_re * zoh_re - prod_im * zoh_im
    coef_im = prod_re * zoh_im + prod_im * zoh_re
    places = jnp.arange(length, dtype=jnp.float32)[:, None, None]
    fading = jnp.exp(step_re[None] * places)
    turning = step_im[None] * places
    return 2.0 * jnp.sum(fading * (coef_re * jnp.cos(turning) - coef_im * jnp.sin(turning)), axis=2)


RANKS = 16
STAGES = 10
SLOTS = (0, 2, 3, 2, 3, 4, 5, 4, 1)
CUTS = 2
ASYNC = (
    ("cotangent_in", "cotangent"),
    ("log_step_in", "log_step"),
    ("log_decay_in", "log_decay"),
    ("frequency_in", "frequency"),
    ("b_in_in", "b_in"),
    ("c_out_in", "c_out"),
    ("to_hi_in", "to_hi"),
    ("to_lo_in", "to_lo"),
    ("from_hi_in", "from_hi"),
    ("from_lo_in", "from_lo"),
)
BF16 = jnp.bfloat16
F32 = jnp.float32
NT = (((1,), (1,)), ((), ()))
TN = (((0,), (0,)), ((), ()))


def spectral_tables(length):
    turns = np.outer(np.arange(length), np.arange(length)) % (2 * length)
    cosine = np.cos(np.pi * turns / length)
    sine = np.sin(np.pi * turns / length)
    sign = np.where(np.arange(length) % 2, -1.0, 1.0)
    to_re, to_im = cosine.copy(), -sine
    to_im[:, 0] = sign
    from_re, from_im = cosine / length, -sine / length
    from_re[0] /= 2
    from_im[0] = sign / (2 * length)
    tables = []
    for table in (np.concatenate([to_re, to_im], 1), np.concatenate([from_re, from_im], 0)):
        high = table.astype(BF16)
        tables += [high, (table - high.astype(np.float64)).astype(BF16)]
    return tuple(tables)


def by_table(values, high, low):
    def dot(a, b):
        return jnp.dot(a, b[...], preferred_element_type=F32)

    if values.dtype == BF16:
        return dot(values, high) + dot(values, low)
    first = values.astype(BF16)
    second = (values - first.astype(F32)).astype(BF16)
    return dot(first, high) + (dot(first, low) + dot(second, high))


def times(a, b):
    return a[0] * b[0] - a[1] * b[1], a[0] * b[1] + a[1] * b[0]


def up_cut(shape, q):
    rows, cols = shape[0] * 2 // CUTS, shape[1] // 2
    return (
        slice(q // 2 * rows, (q // 2 + 1) * rows),
        slice(q % 2 * cols, (q % 2 + 1) * cols),
    )


def reduce_stage(stage, c, role, places, lines, send, recv):
    near, inner, outer = places
    far = 1 - near

    def start(kind, src, dst, target):
        pltpu.make_async_remote_copy(
            src_ref=src,
            dst_ref=dst,
            send_sem=send.at[kind],
            recv_sem=recv.at[SLOTS[kind], c],
            device_id=target,
            device_id_type=MESH,
        ).start()

    def landed(kind, ref):
        pltpu.make_async_copy(ref, ref, recv.at[SLOTS[kind], c]).wait()

    halves = lines[0].part.at[c]
    quarters = lines[0].from_first.at[c]

    def added(*refs):
        total = refs[0][...].astype(F32)
        for ref in refs[1:]:
            total = total + ref[...].astype(F32)
        return total.astype(BF16)

    def give(kind, which, target):
        for line in lines:
            place = line.full.at[c, line.keep, which]
            start(kind, place, place, target)

    def give_back(which):
        for line in lines:
            place = line.full.at[c, line.keep, which]
            start(8, place, place, line.first)

    if stage == 0:

        @pl.when(role > 0)
        def _():
            for line in lines:
                start(0, line.part.at[c, 1 - line.keep], line.from_first.at[c], line.first)

    elif stage == 1:

        @pl.when(role > 0)
        def _():
            landed(0, halves)
            for line in lines:
                line.part[c, line.keep] = added(line.part.at[c, line.keep], line.from_first.at[c])

        @pl.when(role == 1)
        def _():
            for line in lines:
                start(1, line.part.at[c, line.keep, far], line.from_outer.at[c], inner)

    elif stage == 2:

        @pl.when(role == 2)
        def _():
            landed(1, quarters)
            for line in lines:
                mine = line.part.at[c, line.keep, far]
                mine[...] = added(mine, line.from_outer.at[c])
                start(2, mine, line.from_inner.at[c], inner)

    elif stage == 3:

        @pl.when(role == 2)
        def _():
            landed(2, quarters)
            for line in lines:
                mine = line.part.at[c, line.keep, near]
                mine[...] = added(mine, line.from_inner.at[c])
                start(3, mine, line.from_inner.at[c], outer)

    elif stage == 4:

        @pl.when(role == 1)
        def _():
            landed(3, quarters)
            for line in lines:
                mine = line.part.at[c, line.keep, near]
                mine[...] = added(mine, line.from_inner.at[c])
                start(4, mine, line.from_third.at[c], line.third)

    elif stage == 5:

        @pl.when(role == 1)
        def _():
            landed(4, quarters)
            for line in lines:
                mine = line.part.at[c, line.keep, near]
                line.full[c, line.keep, near] = added(mine, line.from_third.at[c])
            give(5, near, inner)
            give_back(near)

    elif stage == 6:

        @pl.when(role == 2)
        def _():
            landed(5, quarters)
            give(6, near, inner)
            give_back(near)

    elif stage == 7:

        @pl.when(role == 2)
        def _():
            landed(6, quarters)
            give(7, far, outer)
            give_back(far)

    elif stage == 8:

        @pl.when(role == 1)
        def _():
            landed(7, quarters)
            give_back(far)

    else:

        @pl.when(role > 0)
        def _():
            landed(8, halves)


def reduce_sent(middle, lines, send):
    halves, quarters = lines[0].part, lines[0].from_first

    def gone(kinds):
        for kind in kinds:
            ref = halves if kind in (0, 8) else quarters
            pltpu.make_async_copy(ref, ref, send.at[kind]).wait()

    gone((0, 8))

    @pl.when(middle == 0)
    def _():
        gone((1, 4, 5))

    @pl.when(middle == 1)
    def _():
        gone((2, 3, 6, 7))


def mode_values(modes):
    log_step, log_decay, freq, b_re, b_im, c_re, c_im = (modes[2 * q : 2 * q + 2] for q in range(7))
    step = jnp.exp(log_step)
    decay = -jnp.exp(log_decay)
    step_re = step * decay
    step_im = step * freq
    half_sin = jnp.sin(0.5 * step_im)
    series = jnp.ones_like(step_re)
    for order in range(11, 1, -1):
        series = 1.0 + series * step_re * (1.0 / order)
    grown = jnp.exp(step_re)
    less_one = jnp.where(step_re > -0.5, step_re * series, grown - 1.0)
    num_re = less_one * jnp.cos(step_im) - 2.0 * half_sin * half_sin
    num_im = grown * jnp.sin(step_im)
    inverse = 1.0 / (decay * decay + freq * freq)
    over = (decay * inverse, -freq * inverse)
    zoh = times((num_re, num_im), over)
    b, c = (b_re, b_im), (c_re, c_im)
    prod = times(b, c)
    return types.SimpleNamespace(
        step=step,
        rate=(decay, freq),
        over=over,
        step_re=step_re,
        step_im=step_im,
        once=(num_re + 1.0, num_im),
        zoh=zoh,
        b=b,
        c=c,
        prod=prod,
        coef=times(prod, zoh),
    )


def block_kernel(names, *refs):
    v = types.SimpleNamespace(**dict(zip(names, refs)))
    rank, core = lax.axis_index("rows"), lax.axis_index("ch")
    x, y, z = rank % 2, (rank // 2) % 2, rank // 4
    near = z // 2
    toward = 4 * (2 * near - 1)
    middle = jnp.minimum(z * (3 - z), 1)
    beside, across = (rank + 1 - 2 * x, core), (rank + 2 - 4 * y, core)
    places = (near, (rank - toward, core), (rank + toward, core))
    twin = (rank, 1 - core)
    heights, widths = v.heights, v.widths
    chunks, part = v.wd.shape[0], v.wd.shape[1]
    pieces = CUTS * chunks
    slab, columns = v.rb1.shape[1:]
    own = slab // 2
    here = own * RANKS
    pixels = 2 * columns
    per = v.log_decay.shape[1]
    lanes = own * per

    def copy(src, dst, sems, index, target):
        return pltpu.make_async_remote_copy(
            src_ref=src,
            dst_ref=dst,
            send_sem=sems.at[0, index],
            recv_sem=sems.at[1, index],
            device_id=target,
            device_id_type=MESH,
        )

    def loop(count, body, start=0):
        def step(i, carry):
            body(i)
            return carry

        lax.fori_loop(start, count, step, 0)

    def wide(column):
        return jnp.concatenate([column] * (pixels // column.shape[1]), axis=1)

    def partner(k):
        return rank ^ lax.rem(15 * k, RANKS)

    def slab_copy(sems, index, src, dst, d):
        return pltpu.make_async_remote_copy(
            src_ref=src,
            dst_ref=dst,
            send_sem=sems.at[0, 0],
            recv_sem=sems.at[1, index],
            device_id=(d, core),
            device_id_type=MESH,
        )

    def scatter(sems, src, dst, each=False, first=1, count=RANKS - 1):
        def start(k):
            d = partner(k)

            @pl.when(k < RANKS)
            def _():
                slab_copy(sems, k if each else 0, src.at[d], dst, d).start()

        loop(first + count, start, first)

    def all_slabs(sems, which, ref):
        most = ref.at[pl.ds(0, RANKS - 1)]
        pltpu.make_async_copy(most, most, sems.at[which, 0]).wait()

    def bring(which):
        far_ref, near_ref = ASYNC[which]
        return pltpu.make_async_copy(getattr(v, far_ref), getattr(v, near_ref), v.bring.at[which])

    barrier = pltpu.get_barrier_semaphore()

    def greet(k):
        pl.semaphore_signal(
            barrier, inc=1, device_id=(lax.rem(rank + k, RANKS), core), device_id_type=MESH
        )

    loop(RANKS, greet, 1)
    pl.semaphore_signal(barrier, inc=1, device_id=twin, device_id_type=MESH)

    def fetch_up(m):
        cols = pl.ds(pl.multiple_of(m * part, part), part)
        return pltpu.make_async_copy(v.w_up.at[:, cols], v.wu.at[m], v.fetch.at[0])

    def fetch_down(m):
        rows = pl.ds(pl.multiple_of(m * part, part), part)
        return pltpu.make_async_copy(v.w_down.at[rows], v.wd.at[m], v.fetch.at[1])

    def fetch(m):
        fetch_up(m).start()
        fetch_down(m).start()


    for g in range(2):
        v.tok[:, g * columns : (g + 1) * columns] = v.tokens[g, 0].astype(F32).T

    def cut_tokens(d):
        rows = v.tok[pl.ds(pl.multiple_of(d * own, 8), own), :]
        both = jnp.concatenate([rows[:, :columns], rows[:, columns:]], axis=0)
        v.tb[core, d] = both.astype(BF16)

    loop(RANKS, cut_tokens)
    lines = []
    for vector in (v.b_up, v.skip_gain, v.ln_gain, v.ln_bias, v.layer_scale, v.b_down):
        line = vector[...].reshape(1, vector.shape[0])
        lines += [line[:, q * 128 : (q + 1) * 128] for q in range(vector.shape[0] // 128)]
    lines.append(jnp.zeros((32 - len(lines), 128), F32))
    v.vx[core] = jnp.concatenate(lines, axis=0)
    pl.semaphore_wait(barrier, RANKS)
    scatter(v.a1, v.tb.at[core], v.rb1.at[rank])
    v.rb1[rank] = v.tb[core, rank]
    for which in range(len(ASYNC)):
        bring(which).start()
    copy(v.tb.at[core], v.tb.at[core], v.tw, 0, twin).start()
    copy(v.vx.at[core], v.vx.at[core], v.tw, 1, twin).start()

    def spread(which, rows):
        block = jnp.concatenate([rows, jnp.zeros((128 - rows.shape[0], 128), F32)], axis=0)
        cols = block.T
        for q in range(15):
            v.vb[q // 3, which, q % 3 * 128 : (q % 3 + 1) * 128, :] = jnp.broadcast_to(
                cols[:, 12 + q : 13 + q], (128, 128)
            )
        return cols

    cols = spread(core, v.vx[core])
    for m in range(chunks):
        for q in range(2):
            v.bias[m, q * 128 : (q + 1) * 128, :] = jnp.broadcast_to(
                cols[:, 2 * m + q : 2 * m + q + 1], (128, 128)
            )
    for which in range(len(ASYNC)):
        bring(which).wait()
    for g in range(2):
        v.cot[:, g * columns : (g + 1) * columns] = v.cotangent[g, 0].astype(F32).T
    places_w = lax.broadcasted_iota(jnp.int32, (1, columns), 1)
    inside = jnp.concatenate(
        [(places_w < jnp.where(rank < heights[g], widths[g], 0)).astype(F32) for g in range(2)],
        axis=1,
    )
    v.inside[...] = jnp.broadcast_to(inside, (8, pixels))

    def mask_rows(q):
        rows = pl.ds(pl.multiple_of(q * 128, 128), 128)
        masked = v.cot[rows, :] * v.inside[0:1, :]
        v.gb[core, rows, :] = (masked * wide(v.vb[3, core, rows, :])).astype(BF16)

    loop(here // 128, mask_rows)
    copy(v.gb.at[core], v.gb.at[core], v.tw, 2, twin).start()

    lane = lax.broadcasted_iota(jnp.int32, (slab, lanes), 1) // per
    row = lax.broadcasted_iota(jnp.int32, (slab, lanes), 0)
    row = jnp.where(row >= own, row - own, row)
    v.pick[...] = (lane == row).astype(F32)
    chosen = lax.broadcasted_iota(jnp.int32, (here, lanes), 1) // per + rank * own
    chosen = (lax.broadcasted_iota(jnp.int32, (here, lanes), 0) == chosen).astype(F32)
    all_modes = jnp.concatenate(
        [v.log_step[...], jnp.zeros((6, here), F32)]
        + [v.log_decay[a] for a in range(2)]
        + [v.frequency[a] for a in range(2)]
        + [v.b_in[a, i] for i in range(2) for a in range(2)]
        + [v.c_out[a, i] for i in range(2) for a in range(2)],
        axis=0,
    )
    all_modes = jnp.dot(all_modes, chosen, precision=PRECISE, preferred_element_type=F32)
    mode = lax.broadcasted_iota(jnp.int32, (per, lanes), 1) % per
    mode = (mode == lax.broadcasted_iota(jnp.int32, (per, lanes), 0)).astype(F32)
    v.of_mode[...] = mode
    own_modes = jnp.sum(all_modes[8:].reshape(12, per, lanes) * mode[None], axis=1)
    v.modes[...] = jnp.concatenate([all_modes[:2], own_modes, own_modes[:2]], axis=0)
    mv = mode_values(v.modes[...])

    def powers(axis, place):
        angle = mv.step_im[axis : axis + 1] * place
        fade = jnp.exp(mv.step_re[axis : axis + 1] * place)
        return fade * jnp.cos(angle), fade * jnp.sin(angle)

    high_place = lax.broadcasted_iota(jnp.int32, (RANKS, lanes), 0).astype(F32)
    v.eh[0], v.eh[1] = powers(0, high_place)
    low_place = lax.broadcasted_iota(jnp.int32, (8, lanes), 0).astype(F32)
    base = powers(1, low_place)
    many = columns // 8
    v.ej[0], v.ej[1] = powers(
        1, 8.0 * lax.broadcasted_iota(jnp.int32, (many, lanes), 0).astype(F32)
    )
    coef_w = tuple(2.0 * part_of[1:2] for part_of in mv.coef)

    def fill(j):
        at = pl.ds(pl.multiple_of(j * 8, 8), 8)
        jump = (v.ej[0, pl.ds(j, 1), :], v.ej[1, pl.ds(j, 1), :])
        e_re, e_im = times(base, jump)
        v.ew[0, at, :] = e_re
        v.ew[1, at, :] = e_im
        v.kt[at, :] = coef_w[0] * e_re - coef_w[1] * e_im

    loop(many, fill)
    k_width = lax.dot_general(
        v.pick[...], v.kt[...], NT, precision=PRECISE, preferred_element_type=F32
    )
    k_both = by_table(k_width, v.to_hi, v.to_lo)
    k_re, k_im = k_both[:, :columns], k_both[:, columns:]
    first_lane = lax.broadcasted_iota(jnp.int32, (slab, columns), 1) == 0
    v.ks[0] = k_re
    v.ks[1] = jnp.where(first_lane, 0.0, k_im)
    v.ks[2] = jnp.where(first_lane, k_im, k_re)
    coef_h = tuple(2.0 * part_of[0:1] for part_of in mv.coef)
    v.kt[0:RANKS, :] = coef_h[0] * v.eh[0] - coef_h[1] * v.eh[1]

    taps = lax.dot_general(
        v.pick[...], v.kt[0:RANKS, :], NT, precision=PRECISE, preferred_element_type=F32
    )
    for l in range(RANKS):
        v.kh[l] = jnp.broadcast_to(taps[:, l : l + 1], (slab, 128))

    def turn(m):
        v.wut[m] = v.wu[m].T
        v.wdt[m] = v.wd[m].T


    all_slabs(v.a1, 1, v.rb1)
    loop(chunks, fetch)
    step_rows = 4

    def convolve(b):
        at = pl.ds(b * step_rows, step_rows)
        values = v.rb1[at].reshape(step_rows * slab, columns)
        shape = (step_rows, slab, columns)
        x_both = by_table(values, v.to_hi, v.to_lo)
        x_re, x_im = x_both[:, :columns].reshape(shape), x_both[:, columns:].reshape(shape)
        v.xs[0, at] = x_re
        v.xs[1, at] = x_im
        k0, k1, k2 = v.ks[0], v.ks[1], v.ks[2]
        y_both = jnp.concatenate([x_re * k0 - x_im * k1, x_re * k1 + x_im * k2], axis=2)
        y_both = y_both.reshape(step_rows * slab, 2 * columns)
        along = by_table(y_both, v.from_hi, v.from_lo)
        v.along[at] = along.astype(BF16).astype(F32).reshape(shape)

    loop(RANKS // step_rows, convolve)

    def by_tiles(body):
        def rows(r):
            for half in range(columns // 128):
                body(pl.ds(pl.multiple_of(r * 8, 8), 8), slice(half * 128, half * 128 + 128))

        loop(slab // 8, rows)

    def down_rows(at, cut):
        taps = [v.kh[l, at, :] for l in range(RANKS)]
        values = [v.along[i, at, cut] for i in range(RANKS)]
        for i in range(RANKS):
            total = taps[0] * values[i]
            for l in range(1, i + 1):
                total += taps[l] * values[i - l]
            v.tall[i, at, cut] = total

    by_tiles(down_rows)
    v.sb2[...] = v.tall[...].astype(BF16)
    scatter(v.a2, v.sb2, v.rb2.at[core, rank], each=True)
    v.rb2[core, rank] = v.sb2[rank]
    copy(v.rb2.at[core, rank], v.rb2.at[core, rank], v.fw, 0, twin).start()

    copy(v.vx.at[core], v.vx.at[1 - core], v.tw, 1, twin).wait_recv()
    spread(1 - core, v.vx[1 - core])
    pltpu.make_async_copy(v.wu, v.wu, v.fetch.at[0]).wait()
    pltpu.make_async_copy(v.wd, v.wd, v.fetch.at[1]).wait()
    loop(chunks, turn)
    v.branch[...] = jnp.zeros_like(v.branch)
    v.gn[...] = jnp.zeros_like(v.gn)

    def forward(k):
        d = partner(k)
        slab_copy(v.a2, k, v.sb2.at[d], v.rb2.at[core, d], d).wait_recv()
        copy(v.rb2.at[core, d], v.rb2.at[core, d], v.fw, 0, twin).start()

    loop(RANKS, forward, 1)
    copy(v.tb.at[core], v.tb.at[1 - core], v.tw, 0, twin).wait_recv()
    copy(v.rb2.at[core], v.rb2.at[1 - core], v.fw, 0, twin).wait_recv()

    eight = jnp.zeros((8, pixels), F32)

    def folded(values):
        return values.reshape(own // 8, 8, pixels).sum(axis=0)

    def mix(i, total):
        which, d = i // RANKS, lax.rem(i, RANKS)
        spatial = v.rb2[which, d].astype(F32)
        token = v.tb[which, d].astype(F32)
        skip = wide(v.vb[0, which, pl.ds(pl.multiple_of(d * own, 8), own), :])
        spatial = jnp.concatenate([spatial[:own], spatial[own:]], axis=1)
        token = jnp.concatenate([token[:own], token[own:]], axis=1)
        mixed = spatial + skip * token
        v.xhat[i] = mixed
        return total + folded(mixed)

    channels = 2 * here
    total = lax.fori_loop(0, 2 * RANKS, mix, eight)
    centre = jnp.sum(total, axis=0, keepdims=True) * (1.0 / channels)

    def squares(i, total):
        off = v.xhat[i] - centre
        return total + folded(off * off)

    total = lax.fori_loop(0, 2 * RANKS, squares, eight)
    spread_of = jnp.sum(total, axis=0, keepdims=True) * (1.0 / channels)
    inv_std = lax.rsqrt(spread_of + EPSILON)
    v.inv[...] = jnp.broadcast_to(inv_std, (8, pixels))

    def normalize(q):
        rows = []
        for k in range(2):
            i = 2 * q + k
            which, d = i // RANKS, lax.rem(i, RANKS)
            at = pl.ds(pl.multiple_of(d * own, 8), own)
            x_hat = (v.xhat[i] - centre) * inv_std
            v.xhat[i] = x_hat
            rows.append(x_hat * wide(v.vb[1, which, at, :]) + wide(v.vb[2, which, at, :]))
        at = pl.ds(pl.multiple_of(q * 2 * own, 16), 2 * own)
        v.normed[at, :] = jnp.concatenate(rows, axis=0).astype(BF16)

    loop(RANKS, normalize)
    copy(v.gb.at[core], v.gb.at[1 - core], v.tw, 2, twin).wait_recv()

    def feed(t):
        normed = v.normed[...]
        g_branch = v.gb[...].reshape(channels, pixels)
        hidden = jnp.dot(v.wut[t], normed, preferred_element_type=F32) + wide(v.bias[t])
        phi = 0.5 + 0.5 * lax.erf(hidden * (0.5**0.5))
        density = jnp.exp(-0.5 * hidden * hidden) * ((2.0 * jnp.pi) ** -0.5)
        active = (hidden * phi).astype(BF16)
        slope = phi + hidden * density
        g_active = jnp.dot(v.wd[t], g_branch, preferred_element_type=F32)
        g_hidden = (g_active * slope).astype(BF16)
        down = lax.dot_general(active, g_branch, NT, preferred_element_type=F32)
        down = down.astype(BF16).reshape(CUTS, 2, 2, part // CUTS // 4, channels)
        v.pd[pl.ds(CUTS * t, CUTS)] = down
        up = lax.dot_general(normed, g_hidden, NT, preferred_element_type=F32)
        up = up.astype(BF16)
        for q in range(CUTS):
            v.pu[CUTS * t + q] = up[up_cut(up.shape, q)].reshape(v.pu.shape[1:])
        v.gn[...] += jnp.dot(v.wu[t], g_hidden, preferred_element_type=F32)
        v.branch[...] += jnp.dot(v.wdt[t], active, preferred_element_type=F32)
        ones = jnp.ones((8, pixels), BF16)
        v.dbu[t] = lax.dot_general(ones, g_hidden, NT, preferred_element_type=F32)

    def share():
        v.gn_out[...] = v.gn[...].astype(BF16)
        copy(v.gn_out, v.gn_in, v.tw, 3, twin).start()
        theirs = pl.ds(pl.multiple_of((1 - core) * here, here), here)
        v.br_out[...] = v.branch[theirs, :].astype(BF16)
        copy(v.br_out, v.br_in, v.tw, 4, twin).start()

    def lane_sum(values):
        return sum(values[:, q * 128 : (q + 1) * 128] for q in range(pixels // 128))

    def norm_back():
        copy(v.gn_out, v.gn_in, v.tw, 3, twin).wait_recv()

        def whole(q, totals):
            at = pl.ds(pl.multiple_of(q * 2 * own, 16), 2 * own)
            g_normed = v.gn[at, :] + v.gn_in[at, :].astype(F32)
            v.gn[at, :] = g_normed
            one, two = totals
            for k in range(2):
                i = 2 * q + k
                which, d = i // RANKS, lax.rem(i, RANKS)
                gain = wide(v.vb[1, which, pl.ds(pl.multiple_of(d * own, 8), own), :])
                g_hat = g_normed[k * own : (k + 1) * own] * gain
                one = one + folded(g_hat)
                two = two + folded(g_hat * v.xhat[i])
            return one, two

        one, two = lax.fori_loop(0, RANKS, whole, (eight, eight))
        one = jnp.sum(one, axis=0, keepdims=True) * (1.0 / channels)
        two = jnp.sum(two, axis=0, keepdims=True) * (1.0 / channels)
        scale = v.inv[0:1, :]

        def each(d):
            at = pl.ds(pl.multiple_of(d * own, 8), own)
            x_hat = v.xhat[core * RANKS + d]
            g_normed = v.gn[pl.ds(pl.multiple_of(core * here + d * own, 8), own), :]
            g_mixed = scale * (g_normed * wide(v.vb[1, core, at, :]) - one - x_hat * two)
            v.gmix[at, :] = g_mixed
            v.sums[0, at, :] = lane_sum(g_mixed * v.tok[at, :])
            v.sums[1, at, :] = lane_sum(g_normed * x_hat)
            v.sums[2, at, :] = lane_sum(g_normed)
            both = jnp.concatenate([g_mixed[:, :columns], g_mixed[:, columns:]], axis=0)
            v.sb3[d] = both.astype(BF16)

        loop(RANKS, each)
        v.rb3[rank] = v.sb3[rank]

    def outputs():
        copy(v.br_out, v.br_in, v.tw, 4, twin).wait_recv()
        mask = v.inside[0:1, :]

        def rows(q):
            at = pl.ds(pl.multiple_of(q * 128, 128), 128)
            branch = v.branch[pl.ds(pl.multiple_of(core * here + q * 128, 128), 128), :]
            branch = branch + v.br_in[at, :].astype(F32) + wide(v.vb[4, core, at, :])
            masked = branch * mask
            v.sums[3, at, :] = lane_sum(v.gb[core, at, :].astype(F32))
            v.sums[4, at, :] = lane_sum(masked * v.cot[at, :])
            v.res[at, :] = v.tok[at, :] + masked * wide(v.vb[3, core, at, :])

        loop(here // 128, rows)
        for g in range(2):
            v.o_out[g, 0] = v.res[:, g * columns : (g + 1) * columns].T.astype(BF16)
        pltpu.make_async_copy(v.o_out, v.output, v.leave.at[2]).start()

    def convolve_back():
        all_slabs(v.a3, 1, v.rb3)
        v.tall[...] = v.rb3[...].astype(F32)

        def up_rows(at, cut):
            taps = [v.kh[l, at, :] for l in range(RANKS)]
            values = [v.tall[i, at, cut] for i in range(RANKS)]
            for i in range(RANKS):
                total = taps[0] * values[i]
                for l in range(1, RANKS - i):
                    total += taps[l] * values[i + l]
                v.galong[i, at, cut] = total.astype(BF16).astype(F32)

        by_tiles(up_rows)

        def lag_rows(at, cut):
            grads = [v.tall[i, at, cut] for i in range(RANKS)]
            values = [v.along[i, at, cut] for i in range(RANKS)]
            for l in range(RANKS):
                total = grads[l] * values[0]
                for i in range(l + 1, RANKS):
                    total += grads[i] * values[i - l]
                v.lags[l, at, cut] = total

        by_tiles(lag_rows)
        v.cross[...] = jnp.zeros_like(v.cross)

    def convolve_step(turn_of):
        block = lax.rem(z + turn_of, RANKS // step_rows)
        at = pl.ds(block * step_rows, step_rows)
        shape = (step_rows, slab, columns)
        values = v.galong[at].reshape(step_rows * slab, columns).astype(BF16)
        g_both = by_table(values, v.to_hi, v.to_lo)
        g_re, g_im = g_both[:, :columns].reshape(shape), g_both[:, columns:].reshape(shape)
        x_re, x_im = v.xs[0, at], v.xs[1, at]
        k0, k1, k2 = v.ks[0], v.ks[1], v.ks[2]
        y_both = jnp.concatenate([g_re * k0 + g_im * k1, g_im * k2 - g_re * k1], axis=2)
        y_both = y_both.reshape(step_rows * slab, 2 * columns)
        conv = by_table(y_both, v.from_hi, v.from_lo)
        v.sb4[at] = conv.reshape(shape).astype(BF16)
        v.cross[0] += (x_re * g_re).sum(axis=0)
        v.cross[1] += (x_im * g_im).sum(axis=0)
        v.cross[2] += (x_re * g_im - x_im * g_re).sum(axis=0)
        for q in range(step_rows):
            d = block * step_rows + q

            @pl.when(d != rank)
            def _():
                slab_copy(v.a4, 0, v.sb4.at[d], v.rb4.at[rank], d).start()

            @pl.when(d == rank)
            def _():
                v.rb4[rank] = v.sb4[rank]

    def kernel_grads():
        cross = [v.cross[q] for q in range(3)]
        zero_lane = lax.broadcasted_iota(jnp.int32, (slab, columns), 1) == 0
        c_re = cross[0] + jnp.where(zero_lane, 0.0, cross[1])
        c_im = jnp.where(zero_lane, cross[1], cross[2])
        dk_width = by_table(jnp.concatenate([c_re, c_im], axis=1), v.from_hi, v.from_lo)
        v.kt[...] = lax.dot_general(
            dk_width, v.pick[...], TN, precision=PRECISE, preferred_element_type=F32
        )

        lags = v.lags[...].reshape(RANKS * slab, columns)
        first = lags.astype(BF16)
        second = (lags - first.astype(F32)).astype(BF16)
        ones = jnp.ones((columns, 128), BF16)
        lags = jnp.dot(first, ones, preferred_element_type=F32)
        lags += jnp.dot(second, ones, preferred_element_type=F32)
        lags = lags.reshape(RANKS, slab, 128)
        for q in range(lanes // 128):
            cut = slice(q * 128, (q + 1) * 128)
            v.kth[:, cut] = jnp.sum(lags * v.pick[:, cut][None], axis=1)

    def parameters():
        def moments(dk, e_re, e_im):
            place = lax.broadcasted_iota(jnp.int32, dk.shape, 0).astype(F32)
            terms = (dk * e_re, dk * e_im)
            plain = [jnp.sum(term, axis=0, keepdims=True) for term in terms]
            timed = [jnp.sum(term * place, axis=0, keepdims=True) for term in terms]
            return plain + timed

        rows_h = moments(v.kth[...], v.eh[0], v.eh[1])
        rows_w = moments(v.kt[...], v.ew[0], v.ew[1])
        p_re, p_im, t_re, t_im = (
            2.0 * jnp.concatenate([h, w], axis=0) for h, w in zip(rows_h, rows_w)
        )
        plain, timed = (p_re, p_im), (t_re, t_im)
        mv = mode_values(v.modes[...])
        step, rate = mv.step, mv.rate
        zoh_plain = times(mv.zoh, plain)
        g_b = times(mv.c, zoh_plain)
        g_c = times(mv.b, zoh_plain)
        coef_timed = times(mv.coef, timed)
        prod_plain = times(mv.prod, plain)
        slope = times(
            (step * mv.once[0] - mv.zoh[0], step * mv.once[1] - mv.zoh[1]), mv.over
        )
        g_rate = times(prod_plain, slope)
        g_rate = (g_rate[0] + step * coef_timed[0], g_rate[1] + step * coef_timed[1])
        g_step = times(prod_plain, mv.once)[0] + times(coef_timed, rate)[0]
        rows = [
            step * g_step,
            g_rate[0] * rate[0],
            -g_rate[1],
            g_b[0],
            -g_b[1],
            g_c[0],
            -g_c[1],
            jnp.zeros_like(step),
        ]
        table = jnp.concatenate(rows, axis=0)
        z, y, x = rank // 4, (rank // 2) % 2, rank % 2
        blocks = [jnp.zeros((per, 128), F32) for _ in range(3)]
        at = lax.broadcasted_iota(jnp.int32, (128, lanes), 0)
        at -= lax.broadcasted_iota(jnp.int32, (128, lanes), 1) // per
        for k in range(5):
            chosen = (at == k * own).astype(BF16)
            for five in range(3 if k < 4 else 2):
                r = 5 * five + k
                values = (v.of_mode[...] * table[r : r + 1]).astype(BF16)
                blocks[five] += lax.dot_general(values, chosen, NT, preferred_element_type=F32)
        for five in range(3):
            v.pack[five * per : (five + 1) * per, :] = blocks[five].astype(BF16)
        ones = jnp.ones((8, 128), F32)
        vectors = [
            v.dbu[m, 0:1, q * 128 : (q + 1) * 128] for m in range(chunks) for q in range(part // 128)
        ]
        for k in range(5):
            line = lax.dot_general(
                ones, v.sums[k], NT, precision=PRECISE, preferred_element_type=F32
            )
            vectors += [line[0:1, q * 128 : (q + 1) * 128] for q in range(here // 128)]
        vectors.append(jnp.zeros((32 - len(vectors), 128), F32))
        v.pack[3 * per :, :] = jnp.concatenate(vectors, axis=0).astype(BF16)
        v.gathered[z, y, x] = v.pack[...]

        def to(k):
            target = (lax.rem(z + k, 4) * 4 + y * 2 + x, core)
            copy(v.pack, v.gathered.at[z, y, x], v.ga, k, target).start()

        loop(4, to, 1)

    def gather_across():
        def wait(k):
            s = lax.rem(z + 4 - k, 4)
            copy(v.pack, v.gathered.at[s, y, x], v.ga, k, (s * 4 + y * 2 + x, core)).wait_recv()

        loop(4, wait, 1)
        mine = v.gathered.at[:, y, x]
        copy(mine, mine, v.ga, 4, across).start()

    def gather_beside():
        theirs = v.gathered.at[:, 1 - y, x]
        copy(theirs, theirs, v.ga, 4, across).wait_recv()
        mine = v.gathered.at[:, :, x]
        copy(mine, mine, v.ga, 5, beside).start()

    def gather_done():
        theirs = v.gathered.at[:, :, 1 - x]
        copy(theirs, theirs, v.ga, 5, beside).wait_recv()
        pltpu.make_async_copy(v.gathered, v.all_gathered, v.leave.at[4]).start()

    def token_grads():
        all_slabs(v.a4, 1, v.rb4)

        def rows(d):
            at = pl.ds(pl.multiple_of(d * own, 8), own)
            conv = v.rb4[d].astype(F32)
            conv = jnp.concatenate([conv[:own], conv[own:]], axis=1)
            skip = wide(v.vb[0, core, at, :])
            v.res[at, :] = v.cot[at, :] + skip * v.gmix[at, :] + conv

        loop(RANKS, rows)
        for g in range(2):
            v.t_out[g, 0] = v.res[:, g * columns : (g + 1) * columns].T.astype(BF16)
        pltpu.make_async_copy(v.t_out, v.d_tokens, v.leave.at[3]).start()

    down = types.SimpleNamespace(
        part=v.pd,
        from_first=v.d1,
        from_outer=v.d2,
        from_inner=v.d3,
        from_third=v.d4,
        full=v.fd,
        keep=x,
        first=beside,
        third=across,
    )
    up = types.SimpleNamespace(
        part=v.pu,
        from_first=v.u1,
        from_outer=v.u2,
        from_inner=v.u3,
        from_third=v.u4,
        full=v.fu,
        keep=y,
        first=across,
        third=beside,
    )

    def leave(c):
        return (
            pltpu.make_async_copy(v.fd.at[c], v.down.at[c], v.leave.at[0]),
            pltpu.make_async_copy(v.fu.at[c], v.up.at[c], v.leave.at[1]),
        )


    def advance(stage, c, role):
        reduce_stage(stage, c, role, places, (down, up), v.sent, v.landed)

    def known(stage, c):
        live = (c * (pieces - 1 - c) >= 0).astype(jnp.int32)
        advance(stage, c, live * (1 + middle))
        if stage == STAGES - 1:

            @pl.when(live > 0)
            def _():
                for one in leave(c):
                    one.start()

    events = {
        0: norm_back,
        1: outputs,
        3: convolve_back,
        7: kernel_grads,
        8: parameters,
        10: gather_across,
        12: gather_beside,
        20: gather_done,
        16: token_grads,
    }

    def feed_and_send(t):
        feed(t)
        for q in range(CUTS):
            c = CUTS * t + q
            advance(0, c, (c < 6).astype(jnp.int32) * (1 + middle))
        known(1, t - 3)
        known(2, t - 3 - 2)

    loop(chunks, feed_and_send)
    share()
    for ahead in range(chunks - 3, 4):
        known(1, jnp.int32(ahead))
        known(2, jnp.int32(ahead - 2))
        known(3, jnp.int32(ahead - 4))

    def tick(t, carry):
        for when, event in events.items():
            pl.when(t == when)(event)
        batch = t - 0

        @pl.when(batch * (2 - 1 - batch) >= 0)
        def _():
            scatter(v.a3, v.sb3, v.rb3.at[rank], first=1 + 8 * batch, count=8)

        turn_of = t - 3

        @pl.when(turn_of * (RANKS // step_rows - 1 - turn_of) >= 0)
        def _():
            convolve_step(turn_of)

        for q in range(1):
            c = 6 + 1 * (t - 0) + q
            known(0, jnp.where(t < 0, pieces, c))
        for stage, start in enumerate((0,2,4,6,8,10,12,14,16), 1):
            known(stage, t + 4 - start)
        return carry

    lax.fori_loop(0, pieces + (0,2,4,6,8,10,12,14,16)[-1] - 4, tick, 0)

    pltpu.make_async_copy(v.gathered, v.all_gathered, v.leave.at[4]).wait()
    pltpu.make_async_copy(v.fd, v.down, v.leave.at[0]).wait()
    pltpu.make_async_copy(v.fu, v.up, v.leave.at[1]).wait()
    pltpu.make_async_copy(v.o_out, v.output, v.leave.at[2]).wait()
    pltpu.make_async_copy(v.t_out, v.d_tokens, v.leave.at[3]).wait()
    all_slabs(v.a1, 0, v.rb1)
    all_slabs(v.a2, 0, v.sb2)
    all_slabs(v.a3, 0, v.sb3)
    all_slabs(v.a4, 0, v.sb4)
    reduce_sent(middle, (down, up), v.sent)
    copy(v.tb.at[core], v.tb.at[core], v.tw, 0, twin).wait_send()
    copy(v.vx.at[core], v.vx.at[core], v.tw, 1, twin).wait_send()
    copy(v.gb.at[core], v.gb.at[core], v.tw, 2, twin).wait_send()
    copy(v.gn_out, v.gn_in, v.tw, 3, twin).wait_send()
    copy(v.br_out, v.br_in, v.tw, 4, twin).wait_send()

    copy(v.rb2.at[core], v.rb2.at[core], v.fw, 0, twin).wait_send()

    def gather_sent(k):
        target = (lax.rem(z + k, 4) * 4 + y * 2 + x, core)
        copy(v.pack, v.gathered.at[z, y, x], v.ga, k, target).wait_send()

    loop(4, gather_sent, 1)
    mine = v.gathered.at[:, y, x]
    copy(mine, mine, v.ga, 4, across).wait_send()
    mine = v.gathered.at[:, :, x]
    copy(mine, mine, v.ga, 5, beside).wait_send()


def finish_kernel(own, *refs):
    ins, outs, small, near, wide, sems = refs[:5], refs[5:20], refs[20:33], refs[33:36], refs[36:38], refs[38:]
    brought, moved, left = sems
    pieces, rows = near[0].shape[0], wide[0].shape[1]
    group = pieces // brought.shape[1]

    def bring(which, m):
        some = pl.ds(m * group, group)
        return pltpu.make_async_copy(
            ins[which].at[some], near[which].at[some], brought.at[which, m]
        )

    def leave(which, m):
        if which == 0:
            place = outs[0].at[pl.ds(pl.multiple_of(m * rows, rows), rows)]
        else:
            up_rows, up_cols = wide[1].shape[1:]
            place = outs[1].at[
                pl.ds(pl.multiple_of(m % CUTS // 2 * up_rows, 16), up_rows),
                pl.ds(pl.multiple_of((m // CUTS * 2 + m % 2) * up_cols, 128), up_cols),
            ]
        return pltpu.make_async_copy(wide[which].at[m], place, left.at[which])

    brings = [
        pltpu.make_async_copy(src, dst, brought.at[2, k])
        for k, (src, dst) in enumerate(zip(ins[2:], (near[2],) + small[:2]))
    ]
    moves = [
        pltpu.make_async_copy(src, dst, moved.at[k])
        for k, (src, dst) in enumerate(zip(small, outs[2:]))
    ]

    def each(count, body):
        def step(m, carry):
            for which in range(2):
                body(which, m)
            return carry

        lax.fori_loop(0, count, step, 0)

    def widen(which, m):
        bring(which, m).wait()
        for q in range(group):
            one = group * m + q
            wide[which][one] = near[which][one].reshape(wide[which].shape[1:]).astype(F32)
            leave(which, one).start()

    for one in brings:
        one.start()
    each(brought.shape[1], lambda which, m: bring(which, m).start())
    for one in brings:
        one.wait()
    widen_small(own, near[2], small[2:])
    for one in moves:
        one.start()
    each(brought.shape[1], widen)
    for which in range(2):
        pltpu.make_async_copy(wide[which], wide[which], left.at[which]).wait()
    for one in moves:
        one.wait()


def widen_small(own, gathered, small):
    d_log_step, d_log_decay, d_frequency, d_b_in, d_c_out = small[:5]
    per, here = d_log_decay.shape[1:]
    lane = lax.broadcasted_iota(jnp.int32, (per, 128), 1)
    whole = []
    for r in range(14):
        five, k = divmod(r, 5)
        windows = [jnp.zeros((per, 128), F32) for _ in range(here // 128)]
        for s in range(RANKS):
            block = gathered[s // 4, s // 2 % 2, s % 2, five * per : (five + 1) * per, :]
            turned = pltpu.roll(block.astype(F32), (own * (s - k)) % 128, 1)
            window, low = divmod(own * s, 128)
            inside = (lane >= low) & (lane < low + own)
            windows[window] = jnp.where(inside, turned, windows[window])
            if low + own > 128:
                inside = lane < low + own - 128
                windows[window + 1] = jnp.where(inside, turned, windows[window + 1])
        whole.append(jnp.concatenate(windows, axis=1))
    for a in range(2):
        d_log_step[a : a + 1, :] = jnp.sum(whole[a], axis=0, keepdims=True)
        d_log_decay[a] = whole[2 + a]
        d_frequency[a] = whole[4 + a]
        for i in range(2):
            d_b_in[a, i] = whole[6 + 2 * i + a]
            d_c_out[a, i] = whole[10 + 2 * i + a]
    sums = jnp.zeros((32, 128), F32)
    for s in range(RANKS):
        sums += gathered[s // 4, s // 2 % 2, s % 2, 3 * per :, :].astype(F32)
    row = 0
    for vector in small[5:]:
        for q in range(vector.shape[0] // 128):
            vector[pl.ds(q * 128, 128)] = sums[row]
            row += 1


def block_shards(
    tokens,
    heights,
    widths,
    log_step,
    log_decay,
    frequency,
    b_in,
    c_out,
    skip_gain,
    ln_gain,
    ln_bias,
    w_up,
    b_up,
    w_down,
    b_down,
    layer_scale,
    cotangent,
):
    columns, here = tokens.shape[2:]
    modes_each = log_decay.shape[2]
    hidden = w_up.shape[1]
    own = here // RANKS
    chunks = hidden // 256
    part = hidden // chunks
    channels = 2 * here
    pixels = 2 * columns
    lanes = own * modes_each
    tables = spectral_tables(columns)
    slabs = (RANKS, 2 * own, columns)
    tall = pltpu.VMEM(slabs, F32)
    in_vmem = pl.BlockSpec(memory_space=pltpu.VMEM)
    in_smem = pl.BlockSpec(memory_space=pltpu.SMEM)
    anywhere = pl.BlockSpec(memory_space=pl.ANY)
    inputs = dict(
        tokens=(tokens, in_vmem),
        cotangent_in=(cotangent, anywhere),
        heights=(heights, in_smem),
        widths=(widths, in_smem),
        log_step_in=(log_step, anywhere),
        log_decay_in=(log_decay.swapaxes(-1, -2), anywhere),
        frequency_in=(frequency.swapaxes(-1, -2), anywhere),
        b_in_in=(b_in.swapaxes(-1, -2), anywhere),
        c_out_in=(c_out.swapaxes(-1, -2), anywhere),
        b_up=(b_up, in_vmem),
        skip_gain=(skip_gain, in_vmem),
        ln_gain=(ln_gain, in_vmem),
        ln_bias=(ln_bias, in_vmem),
        layer_scale=(layer_scale, in_vmem),
        b_down=(b_down, in_vmem),
        w_up=(w_up, anywhere),
        w_down=(w_down, anywhere),
        to_hi_in=(tables[0], anywhere),
        to_lo_in=(tables[1], anywhere),
        from_hi_in=(tables[2], anywhere),
        from_lo_in=(tables[3], anywhere),
    )
    down_shape = (CUTS * chunks, 2, 2, part // CUTS // 4, channels)
    up_shape = (CUTS * chunks, 2, 2, channels // (2 * CUTS), part // 2)
    outs = dict(
        output=(jax.ShapeDtypeStruct(tokens.shape, BF16), anywhere),
        d_tokens=(jax.ShapeDtypeStruct(tokens.shape, BF16), anywhere),
        down=(jax.ShapeDtypeStruct(down_shape, BF16), anywhere),
        up=(jax.ShapeDtypeStruct(up_shape, BF16), anywhere),
        all_gathered=(
            jax.ShapeDtypeStruct((4, 2, 2, 3 * modes_each + 32, 128), BF16),
            anywhere,
        ),
    )
    low_slabs = pltpu.VMEM(slabs, BF16)
    both_slabs = pltpu.VMEM((2,) + slabs, BF16)
    scratch = dict(
        wu=pltpu.VMEM((chunks, channels, part), BF16),
        wd=pltpu.VMEM((chunks, part, channels), BF16),
        wut=pltpu.VMEM((chunks, part, channels), BF16),
        wdt=pltpu.VMEM((chunks, channels, part), BF16),
        tok=pltpu.VMEM((here, pixels), F32),
        cot=pltpu.VMEM((here, pixels), F32),
        gmix=pltpu.VMEM((here, pixels), F32),
        res=pltpu.VMEM((here, pixels), F32),
        tb=both_slabs,
        rb1=low_slabs,
        sb2=low_slabs,
        rb2=both_slabs,
        sb3=low_slabs,
        rb3=low_slabs,
        sb4=low_slabs,
        rb4=low_slabs,
        vx=pltpu.VMEM((2, 32, 128), F32),
        vb=pltpu.VMEM((5, 2, here, 128), F32),
        bias=pltpu.VMEM((chunks, part, 128), F32),
        inside=pltpu.VMEM((8, pixels), F32),
        inv=pltpu.VMEM((8, pixels), F32),
        gb=pltpu.VMEM((2, here, pixels), BF16),
        modes=pltpu.VMEM((16, lanes), F32),
        of_mode=pltpu.VMEM((modes_each, lanes), F32),
        cross=pltpu.VMEM((3, 2 * own, columns), F32),
        pick=pltpu.VMEM((2 * own, lanes), F32),
        eh=pltpu.VMEM((2, RANKS, lanes), F32),
        ej=pltpu.VMEM((2, columns // 8, lanes), F32),
        ew=pltpu.VMEM((2, columns, lanes), F32),
        kt=pltpu.VMEM((columns, lanes), F32),
        kth=pltpu.VMEM((RANKS, lanes), F32),
        ks=pltpu.VMEM((3, 2 * own, columns), F32),
        kh=pltpu.VMEM((RANKS, 2 * own, 128), F32),
        xs=pltpu.VMEM((2,) + slabs, F32),
        along=tall,
        tall=tall,
        galong=tall,
        lags=tall,
        xhat=pltpu.VMEM((2 * RANKS, own, pixels), F32),
        normed=pltpu.VMEM((channels, pixels), BF16),
        branch=pltpu.VMEM((channels, pixels), F32),
        gn=pltpu.VMEM((channels, pixels), F32),
        gn_out=pltpu.VMEM((channels, pixels), BF16),
        gn_in=pltpu.VMEM((channels, pixels), BF16),
        br_out=pltpu.VMEM((here, pixels), BF16),
        br_in=pltpu.VMEM((here, pixels), BF16),
        dbu=pltpu.VMEM((chunks, 8, part), F32),
        sums=pltpu.VMEM((5, here, 128), F32),
        pack=pltpu.VMEM((3 * modes_each + 32, 128), BF16),
        fetch=pltpu.SemaphoreType.DMA((2,)),
        leave=pltpu.SemaphoreType.DMA((5,)),
        gathered=pltpu.VMEM((4, 2, 2, 3 * modes_each + 32, 128), BF16),
        bring=pltpu.SemaphoreType.DMA((len(ASYNC),)),
        o_out=pltpu.VMEM(tokens.shape, BF16),
        t_out=pltpu.VMEM(tokens.shape, BF16),
        cotangent=pltpu.VMEM(cotangent.shape, BF16),
        log_step=pltpu.VMEM(log_step.shape, F32),
        log_decay=pltpu.VMEM((2, modes_each, here), F32),
        frequency=pltpu.VMEM((2, modes_each, here), F32),
        b_in=pltpu.VMEM((2, 2, modes_each, here), F32),
        c_out=pltpu.VMEM((2, 2, modes_each, here), F32),
        to_hi=pltpu.VMEM(tables[0].shape, BF16),
        to_lo=pltpu.VMEM(tables[1].shape, BF16),
        from_hi=pltpu.VMEM(tables[2].shape, BF16),
        from_lo=pltpu.VMEM(tables[3].shape, BF16),
    )

    def reduction(shape):
        count, halves, pieces, rows, width = shape
        whole = pltpu.VMEM(shape, BF16)
        half = pltpu.VMEM((count, pieces, rows, width), BF16)
        piece = pltpu.VMEM((count, rows, width), BF16)
        return whole, half, piece, piece, piece, whole

    down_scratch, up_scratch = reduction(down_shape), reduction(up_shape)
    scratch.update(
        zip(("pd", "d1", "d2", "d3", "d4", "fd"), down_scratch),
    )
    scratch.update(
        zip(("pu", "u1", "u2", "u3", "u4", "fu"), up_scratch),
    )
    one_each = pltpu.SemaphoreType.DMA((2, 1))
    scratch.update(a1=one_each, a3=one_each, a4=one_each, fw=one_each)
    scratch.update(a2=pltpu.SemaphoreType.DMA((2, RANKS)))
    scratch.update(sent=pltpu.SemaphoreType.DMA((9,)))
    scratch.update(landed=pltpu.SemaphoreType.DMA((6, CUTS * chunks)))
    scratch.update(tw=pltpu.SemaphoreType.DMA((2, 5)), ga=pltpu.SemaphoreType.DMA((2, 6)))
    names = tuple(inputs) + tuple(outs) + tuple(scratch)
    output, d_tokens, down, up, gathered = pl.pallas_call(
        functools.partial(block_kernel, names),
        out_shape=tuple(shape for shape, _ in outs.values()),
        in_specs=[spec for _, spec in inputs.values()],
        out_specs=tuple(spec for _, spec in outs.values()),
        scratch_shapes=list(scratch.values()),
        compiler_params=pltpu.CompilerParams(
            collective_id=0, has_side_effects=True, vmem_limit_bytes=62 << 20
        ),
    )(*(value for value, _ in inputs.values()))
    result = (
        jax.ShapeDtypeStruct((hidden, channels), F32),
        jax.ShapeDtypeStruct((channels, hidden), F32),
        output,
        d_tokens,
        log_step,
        jax.ShapeDtypeStruct((2, modes_each, here), F32),
        jax.ShapeDtypeStruct((2, modes_each, here), F32),
        jax.ShapeDtypeStruct((2, 2, modes_each, here), F32),
        jax.ShapeDtypeStruct((2, 2, modes_each, here), F32),
        b_up,
        skip_gain,
        ln_gain,
        ln_bias,
        b_down,
        layer_scale,
    )
    result = tuple(jax.ShapeDtypeStruct(one.shape, one.dtype) for one in result)
    (
        d_w_down,
        d_w_up,
        output,
        d_tokens,
        d_log_step,
        d_log_decay,
        d_frequency,
        d_b_in,
        d_c_out,
        d_b_up,
        d_skip_gain,
        d_ln_gain,
        d_ln_bias,
        d_b_down,
        d_layer_scale,
    ) = pl.pallas_call(
        functools.partial(finish_kernel, own),
        out_shape=result,
        in_specs=[anywhere] * 5,
        out_specs=(anywhere,) * 15,
        scratch_shapes=[pltpu.VMEM(one.shape, one.dtype) for one in result[2:]]
        + [pltpu.VMEM(one.shape, BF16) for one in (down, up, gathered)]
        + [
            pltpu.VMEM((CUTS * chunks, part // CUTS, channels), F32),
            pltpu.VMEM((CUTS * chunks, channels * 2 // CUTS, part // 2), F32),
            pltpu.SemaphoreType.DMA((3, chunks)),
            pltpu.SemaphoreType.DMA((13,)),
            pltpu.SemaphoreType.DMA((2,)),
        ],
        compiler_params=pltpu.CompilerParams(vmem_limit_bytes=62 << 20),
    )(down, up, gathered, output, d_tokens)
    return (
        output,
        d_tokens,
        d_log_step,
        d_log_decay.swapaxes(-1, -2),
        d_frequency.swapaxes(-1, -2),
        d_b_in.swapaxes(-1, -2),
        d_c_out.swapaxes(-1, -2),
        d_skip_gain,
        d_ln_gain,
        d_ln_bias,
        d_w_up,
        d_b_up,
        d_w_down,
        d_b_down,
        d_layer_scale,
    )


def shards(
    tokens,
    heights,
    widths,
    log_step,
    log_decay,
    frequency,
    b_in,
    c_out,
    skip_gain,
    ln_gain,
    ln_bias,
    w_up,
    b_up,
    w_down,
    b_down,
    layer_scale,
    cotangent,
):
    row_count = lax.axis_size("rows")
    row_rank = lax.axis_index("rows")
    grid_count, rows_here, columns, channels = tokens.shape
    all_channels = channels * lax.axis_size("ch")
    height = rows_here * row_count
    own_count = channels // row_count
    first_chan = row_rank * own_count
    pixels = grid_count * rows_here * columns
    token_f = tokens.astype(jnp.float32)
    width_tables = make_tables(columns)
    height_tables = make_tables(height)
    own_params = tuple(
        lax.dynamic_slice_in_dim(param, first_chan, own_count, param.ndim - trailing)
        for param, trailing in (
            (log_step, 1),
            (log_decay, 2),
            (frequency, 2),
            (b_in, 2),
            (c_out, 2),
        )
    )
    width_params = tuple(param[1] for param in own_params)
    height_params = tuple(param[0] for param in own_params)
    k_width, width_pull = jax.vjp(lambda params: make_kernel(params, columns), width_params)
    k_height, height_pull = jax.vjp(lambda params: make_kernel(params, height), height_params)
    kw_re, kw_im = kernel_spectrum(k_width, width_tables)
    kh_re, kh_im = kernel_spectrum(k_height, height_tables)
    kh_re = kh_re[:, None, :]
    kh_im = kh_im[:, None, :]
    pencil_tokens = lax.all_to_all(tokens, "rows", split_axis=3, concat_axis=1, tiled=True)
    x_re, x_im = to_spectrum(pencil_tokens.astype(jnp.float32), width_tables, "fw,grwc->grfc")
    along_width = from_spectrum(
        x_re * kw_re - x_im * kw_im, x_re * kw_im + x_im * kw_re, width_tables, "fw,grfc->grwc"
    ).astype(jnp.bfloat16)
    p_re, p_im = to_spectrum(along_width.astype(jnp.float32), height_tables, "fh,ghwc->gfwc")
    mixed_cols = from_spectrum(
        p_re * kh_re - p_im * kh_im, p_re * kh_im + p_im * kh_re, height_tables, "fh,gfwc->ghwc"
    ).astype(jnp.bfloat16)
    back_rows = lax.all_to_all(mixed_cols, "rows", split_axis=1, concat_axis=3, tiled=True)
    mixed = back_rows.astype(jnp.float32) + skip_gain * token_f
    flat_mixed = mixed.reshape(pixels, channels)
    sum_one, sum_two = lax.psum(
        (jnp.sum(flat_mixed, axis=1), jnp.sum(flat_mixed * flat_mixed, axis=1)), "ch"
    )
    centre = sum_one / all_channels
    spread = sum_two / all_channels - centre * centre
    inv_std = lax.rsqrt(spread + EPSILON)[:, None]
    x_hat = (flat_mixed - centre[:, None]) * inv_std
    normed = (x_hat * ln_gain + ln_bias).astype(jnp.bfloat16)
    hidden = (
        jnp.dot(
            lax.all_gather(normed, "ch", axis=1, tiled=True),
            w_up,
            preferred_element_type=jnp.float32,
        )
        + b_up
    )
    active = jax.nn.gelu(hidden, approximate=False).astype(jnp.bfloat16)
    partials = jnp.dot(active, w_down, preferred_element_type=jnp.float32)
    branch = (
        lax.psum_scatter(
            partials.astype(jnp.bfloat16), "ch", scatter_dimension=1, tiled=True
        ).astype(jnp.float32)
        + b_down
    )
    row_ids = row_rank * rows_here + jnp.arange(rows_here, dtype=jnp.int32)
    col_ids = jnp.arange(columns, dtype=jnp.int32)
    inside = (row_ids[None, :, None] < heights[:, None, None]) & (
        col_ids[None, None, :] < widths[:, None, None]
    )
    inside = inside.astype(jnp.float32).reshape(pixels, 1)
    flat_tokens = token_f.reshape(pixels, channels)
    output = (
        (flat_tokens + inside * layer_scale * branch).astype(jnp.bfloat16).reshape(tokens.shape)
    )
    over_rows = (((0,), (0,)), ((), ()))
    over_cols = (((1,), (1,)), ((), ()))
    g_flat = cotangent.astype(jnp.float32).reshape(pixels, channels)
    g_masked = g_flat * inside
    g_branch = (g_masked * layer_scale).astype(jnp.bfloat16)
    d_layer_scale = jnp.sum(g_masked * branch, axis=0)
    d_b_down = jnp.sum(g_branch.astype(jnp.float32), axis=0)
    g_branch_all = lax.all_gather(g_branch, "ch", axis=1, tiled=True)
    d_w_down = lax.dot_general(active, g_branch_all, over_rows, preferred_element_type=jnp.float32)
    g_active = lax.dot_general(g_branch_all, w_down, over_cols, preferred_element_type=jnp.float32)
    gelu_pull = jax.vjp(lambda values: jax.nn.gelu(values, approximate=False), hidden)[1]
    g_hidden = gelu_pull(g_active)[0].astype(jnp.bfloat16)
    d_b_up = jnp.sum(g_hidden.astype(jnp.float32), axis=0)
    d_w_up = lax.dot_general(
        lax.all_gather(normed, "ch", axis=1, tiled=True),
        g_hidden,
        over_rows,
        preferred_element_type=jnp.float32,
    )
    g_terms = lax.dot_general(g_hidden, w_up, over_cols, preferred_element_type=jnp.float32)
    g_normed = lax.psum_scatter(g_terms, "ch", scatter_dimension=1, tiled=True)
    d_ln_gain = jnp.sum(g_normed * x_hat, axis=0)
    d_ln_bias = jnp.sum(g_normed, axis=0)
    g_hat = g_normed * ln_gain
    sum_grad, sum_cross = lax.psum((jnp.sum(g_hat, axis=1), jnp.sum(g_hat * x_hat, axis=1)), "ch")
    g_mixed = inv_std * (
        g_hat - sum_grad[:, None] / all_channels - x_hat * sum_cross[:, None] / all_channels
    )
    d_skip_gain = jnp.sum(g_mixed * flat_tokens, axis=0)
    g_spatial = g_mixed.astype(jnp.bfloat16).reshape(tokens.shape)
    pencil_grad = lax.all_to_all(g_spatial, "rows", split_axis=3, concat_axis=1, tiled=True)
    gp_re, gp_im = to_spectrum(pencil_grad.astype(jnp.float32), height_tables, "fh,ghwc->gfwc")
    vp_re, vp_im = p_re, p_im
    g_pencil_along = from_spectrum(
        gp_re * kh_re + gp_im * kh_im, gp_im * kh_re - gp_re * kh_im, height_tables, "fh,gfwc->ghwc"
    ).astype(jnp.bfloat16)
    cross_re = jnp.sum(vp_re * gp_re + vp_im * gp_im, axis=(0, 2))
    cross_im = jnp.sum(vp_re * gp_im - vp_im * gp_re, axis=(0, 2))
    dk_height = kernel_from_cross(cross_re, cross_im, height_tables)
    g_along = g_pencil_along
    ga_re, ga_im = to_spectrum(g_along.astype(jnp.float32), width_tables, "fw,grwc->grfc")
    g_conv = from_spectrum(
        ga_re * kw_re + ga_im * kw_im, ga_im * kw_re - ga_re * kw_im, width_tables, "fw,grfc->grwc"
    )
    g_conv = lax.all_to_all(
        g_conv.astype(jnp.bfloat16), "rows", split_axis=1, concat_axis=3, tiled=True
    ).astype(jnp.float32)
    wide_re = jnp.sum(x_re * ga_re + x_im * ga_im, axis=(0, 1))
    wide_im = jnp.sum(x_re * ga_im - x_im * ga_re, axis=(0, 1))
    dk_width = kernel_from_cross(wide_re, wide_im, width_tables)
    d_tokens = ((g_flat + g_mixed * skip_gain).reshape(tokens.shape) + g_conv).astype(jnp.bfloat16)
    width_grads = width_pull(dk_width)[0]
    height_grads = height_pull(dk_height)[0]

    def gathered(pieces, dim_num):
        return lax.all_gather(jnp.stack(pieces), "rows", axis=dim_num, tiled=True)

    param_grads = tuple(
        gathered(pair, dim_num)
        for pair, dim_num in zip(zip(height_grads, width_grads), (1, 1, 1, 2, 2))
    )
    d_w_down, d_w_up, d_skip_gain, d_ln_gain, d_ln_bias, d_b_up, d_b_down, d_layer_scale = lax.psum(
        (d_w_down, d_w_up, d_skip_gain, d_ln_gain, d_ln_bias, d_b_up, d_b_down, d_layer_scale),
        "rows",
    )
    return (output, d_tokens) + param_grads + (
        d_skip_gain,
        d_ln_gain,
        d_ln_bias,
        d_w_up,
        d_b_up,
        d_w_down,
        d_b_down,
        d_layer_scale,
    )


def solution(mesh):
    one_row_each = mesh.shape["rows"] == RANKS and mesh.shape["ch"] == 2
    return jax.shard_map(
        block_shards if one_row_each else shards,
        mesh=mesh,
        in_specs=(
            P(None, "rows", None, "ch"),
            P(),
            P(),
            P(None, "ch"),
            P(None, "ch", None),
            P(None, "ch", None),
            P(None, None, "ch", None),
            P(None, None, "ch", None),
            P("ch"),
            P("ch"),
            P("ch"),
            P(None, "ch"),
            P("ch"),
            P("ch", None),
            P("ch"),
            P("ch"),
            P(None, "rows", None, "ch"),
        ),
        out_specs=(
            P(None, "rows", None, "ch"),
            P(None, "rows", None, "ch"),
            P(None, "ch"),
            P(None, "ch", None),
            P(None, "ch", None),
            P(None, None, "ch", None),
            P(None, None, "ch", None),
            P("ch"),
            P("ch"),
            P("ch"),
            P(None, "ch"),
            P("ch"),
            P("ch", None),
            P("ch"),
            P("ch"),
        ),
        check_vma=False,
    )
```

```python
import functools
import types

import jax
import jax.numpy as jnp
import numpy as np
from jax import lax
from jax.experimental import pallas as pl
from jax.experimental.pallas import tpu as pltpu
from jax.sharding import PartitionSpec as P

PRECISE = lax.Precision.HIGHEST
EPSILON = 1e-06
MESH = pl.DeviceIdType.MESH


def make_tables(length):
    freq_ids = jnp.arange(length + 1, dtype=jnp.int32)[:, None]
    places = jnp.arange(length, dtype=jnp.int32)[None, :]
    turns = freq_ids * places % (2 * length)
    angles = turns.astype(jnp.float32) * (jnp.pi / length)
    cosine = jnp.cos(angles)
    sine_t = jnp.sin(angles)
    weights = jnp.where((freq_ids == 0) | (freq_ids == length), 1.0, 2.0) / (2.0 * length)
    return (cosine, sine_t, cosine * weights, sine_t * weights)


def to_spectrum(values, tables, pattern):
    real_part = jnp.einsum(pattern, tables[0], values, precision=PRECISE)
    imag_part = -jnp.einsum(pattern, tables[1], values, precision=PRECISE)
    return (real_part, imag_part)


def from_spectrum(real_part, imag_part, tables, pattern):
    return jnp.einsum(pattern, tables[2], real_part, precision=PRECISE) - jnp.einsum(
        pattern, tables[3], imag_part, precision=PRECISE
    )


def kernel_spectrum(kernel, tables):
    real_part = jnp.dot(tables[0], kernel, precision=PRECISE)
    imag_part = -jnp.dot(tables[1], kernel, precision=PRECISE)
    return (real_part, imag_part)


def kernel_from_cross(cross_re, cross_im, tables):
    contract = (((0,), (0,)), ((), ()))
    return lax.dot_general(tables[2], cross_re, contract, precision=PRECISE) - lax.dot_general(
        tables[3], cross_im, contract, precision=PRECISE
    )


def make_kernel(params, length):
    log_step, log_decay, frequency, b_in, c_out = params
    step_size = jnp.exp(log_step)[:, None]
    decay_re = -jnp.exp(log_decay)
    step_re = step_size * decay_re
    step_im = step_size * frequency
    half_sin = jnp.sin(0.5 * step_im)
    num_re = jnp.expm1(step_re) * jnp.cos(step_im) - 2.0 * half_sin * half_sin
    num_im = jnp.exp(step_re) * jnp.sin(step_im)
    divisor = decay_re * decay_re + frequency * frequency
    zoh_re = (num_re * decay_re + num_im * frequency) / divisor
    zoh_im = (num_im * decay_re - num_re * frequency) / divisor
    prod_re = b_in[0] * c_out[0] - b_in[1] * c_out[1]
    prod_im = b_in[0] * c_out[1] + b_in[1] * c_out[0]
    coef_re = prod_re * zoh_re - prod_im * zoh_im
    coef_im = prod_re * zoh_im + prod_im * zoh_re
    places = jnp.arange(length, dtype=jnp.float32)[:, None, None]
    fading = jnp.exp(step_re[None] * places)
    turning = step_im[None] * places
    return 2.0 * jnp.sum(fading * (coef_re * jnp.cos(turning) - coef_im * jnp.sin(turning)), axis=2)


RANKS = 16
STAGES = 10
SLOTS = (0, 2, 3, 2, 3, 4, 5, 4, 1)
CUTS = 2
ASYNC = (
    ("cotangent_in", "cotangent"),
    ("log_step_in", "log_step"),
    ("log_decay_in", "log_decay"),
    ("frequency_in", "frequency"),
    ("b_in_in", "b_in"),
    ("c_out_in", "c_out"),
    ("to_hi_in", "to_hi"),
    ("to_lo_in", "to_lo"),
    ("from_hi_in", "from_hi"),
    ("from_lo_in", "from_lo"),
)
BF16 = jnp.bfloat16
F32 = jnp.float32
NT = (((1,), (1,)), ((), ()))
TN = (((0,), (0,)), ((), ()))


def spectral_tables(length):
    turns = np.outer(np.arange(length), np.arange(length)) % (2 * length)
    cosine = np.cos(np.pi * turns / length)
    sine = np.sin(np.pi * turns / length)
    sign = np.where(np.arange(length) % 2, -1.0, 1.0)
    to_re, to_im = cosine.copy(), -sine
    to_im[:, 0] = sign
    from_re, from_im = cosine / length, -sine / length
    from_re[0] /= 2
    from_im[0] = sign / (2 * length)
    tables = []
    for table in (np.concatenate([to_re, to_im], 1), np.concatenate([from_re, from_im], 0)):
        high = table.astype(BF16)
        tables += [high, (table - high.astype(np.float64)).astype(BF16)]
    return tuple(tables)


def by_table(values, high, low):
    def dot(a, b):
        return jnp.dot(a, b[...], preferred_element_type=F32)

    if values.dtype == BF16:
        return dot(values, high) + dot(values, low)
    first = values.astype(BF16)
    second = (values - first.astype(F32)).astype(BF16)
    return dot(first, high) + (dot(first, low) + dot(second, high))


def times(a, b):
    return a[0] * b[0] - a[1] * b[1], a[0] * b[1] + a[1] * b[0]


def up_cut(shape, q):
    rows, cols = shape[0] * 2 // CUTS, shape[1] // 2
    return (
        slice(q // 2 * rows, (q // 2 + 1) * rows),
        slice(q % 2 * cols, (q % 2 + 1) * cols),
    )


def reduce_stage(stage, c, role, places, lines, send, recv):
    near, inner, outer = places
    far = 1 - near

    def start(kind, src, dst, target):
        pltpu.make_async_remote_copy(
            src_ref=src,
            dst_ref=dst,
            send_sem=send.at[kind],
            recv_sem=recv.at[SLOTS[kind], c],
            device_id=target,
            device_id_type=MESH,
        ).start()

    def landed(kind, ref):
        pltpu.make_async_copy(ref, ref, recv.at[SLOTS[kind], c]).wait()

    halves = lines[0].part.at[c]
    quarters = lines[0].from_first.at[c]

    def added(*refs):
        total = refs[0][...].astype(F32)
        for ref in refs[1:]:
            total = total + ref[...].astype(F32)
        return total.astype(BF16)

    def give(kind, which, target):
        for line in lines:
            place = line.full.at[c, line.keep, which]
            start(kind, place, place, target)

    def give_back(which):
        for line in lines:
            place = line.full.at[c, line.keep, which]
            start(8, place, place, line.first)

    if stage == 0:

        @pl.when(role > 0)
        def _():
            for line in lines:
                start(0, line.part.at[c, 1 - line.keep], line.from_first.at[c], line.first)

    elif stage == 1:

        @pl.when(role > 0)
        def _():
            landed(0, halves)
            for line in lines:
                line.part[c, line.keep] = added(line.part.at[c, line.keep], line.from_first.at[c])

        @pl.when(role == 1)
        def _():
            for line in lines:
                start(1, line.part.at[c, line.keep, far], line.from_outer.at[c], inner)

    elif stage == 2:

        @pl.when(role == 2)
        def _():
            landed(1, quarters)
            for line in lines:
                mine = line.part.at[c, line.keep, far]
                mine[...] = added(mine, line.from_outer.at[c])
                start(2, mine, line.from_inner.at[c], inner)

    elif stage == 3:

        @pl.when(role == 2)
        def _():
            landed(2, quarters)
            for line in lines:
                mine = line.part.at[c, line.keep, near]
                mine[...] = added(mine, line.from_inner.at[c])
                start(3, mine, line.from_inner.at[c], outer)

    elif stage == 4:

        @pl.when(role == 1)
        def _():
            landed(3, quarters)
            for line in lines:
                mine = line.part.at[c, line.keep, near]
                mine[...] = added(mine, line.from_inner.at[c])
                start(4, mine, line.from_third.at[c], line.third)

    elif stage == 5:

        @pl.when(role == 1)
        def _():
            landed(4, quarters)
            for line in lines:
                mine = line.part.at[c, line.keep, near]
                line.full[c, line.keep, near] = added(mine, line.from_third.at[c])
            give(5, near, inner)
            give_back(near)

    elif stage == 6:

        @pl.when(role == 2)
        def _():
            landed(5, quarters)
            give(6, near, inner)
            give_back(near)

    elif stage == 7:

        @pl.when(role == 2)
        def _():
            landed(6, quarters)
            give(7, far, outer)
            give_back(far)

    elif stage == 8:

        @pl.when(role == 1)
        def _():
            landed(7, quarters)
            give_back(far)

    else:

        @pl.when(role > 0)
        def _():
            landed(8, halves)


def reduce_sent(middle, lines, send):
    halves, quarters = lines[0].part, lines[0].from_first

    def gone(kinds):
        for kind in kinds:
            ref = halves if kind in (0, 8) else quarters
            pltpu.make_async_copy(ref, ref, send.at[kind]).wait()

    gone((0, 8))

    @pl.when(middle == 0)
    def _():
        gone((1, 4, 5))

    @pl.when(middle == 1)
    def _():
        gone((2, 3, 6, 7))


def mode_values(modes):
    log_step, log_decay, freq, b_re, b_im, c_re, c_im = (modes[2 * q : 2 * q + 2] for q in range(7))
    step = jnp.exp(log_step)
    decay = -jnp.exp(log_decay)
    step_re = step * decay
    step_im = step * freq
    half_sin = jnp.sin(0.5 * step_im)
    series = jnp.ones_like(step_re)
    for order in range(11, 1, -1):
        series = 1.0 + series * step_re * (1.0 / order)
    grown = jnp.exp(step_re)
    less_one = jnp.where(step_re > -0.5, step_re * series, grown - 1.0)
    num_re = less_one * jnp.cos(step_im) - 2.0 * half_sin * half_sin
    num_im = grown * jnp.sin(step_im)
    inverse = 1.0 / (decay * decay + freq * freq)
    over = (decay * inverse, -freq * inverse)
    zoh = times((num_re, num_im), over)
    b, c = (b_re, b_im), (c_re, c_im)
    prod = times(b, c)
    return types.SimpleNamespace(
        step=step,
        rate=(decay, freq),
        over=over,
        step_re=step_re,
        step_im=step_im,
        once=(num_re + 1.0, num_im),
        zoh=zoh,
        b=b,
        c=c,
        prod=prod,
        coef=times(prod, zoh),
    )


def block_kernel(names, *refs):
    v = types.SimpleNamespace(**dict(zip(names, refs)))
    rank, core = lax.axis_index("rows"), lax.axis_index("ch")
    x, y, z = rank % 2, (rank // 2) % 2, rank // 4
    near = z // 2
    toward = 4 * (2 * near - 1)
    middle = jnp.minimum(z * (3 - z), 1)
    beside, across = (rank + 1 - 2 * x, core), (rank + 2 - 4 * y, core)
    places = (near, (rank - toward, core), (rank + toward, core))
    twin = (rank, 1 - core)
    heights, widths = v.heights, v.widths
    chunks, part = v.wd.shape[0], v.wd.shape[1]
    pieces = CUTS * chunks
    slab, columns = v.rb1.shape[1:]
    own = slab // 2
    here = own * RANKS
    pixels = 2 * columns
    per = v.log_decay.shape[1]
    lanes = own * per

    def copy(src, dst, sems, index, target):
        return pltpu.make_async_remote_copy(
            src_ref=src,
            dst_ref=dst,
            send_sem=sems.at[0, index],
            recv_sem=sems.at[1, index],
            device_id=target,
            device_id_type=MESH,
        )

    def loop(count, body, start=0):
        def step(i, carry):
            body(i)
            return carry

        lax.fori_loop(start, count, step, 0)

    def wide(column):
        return jnp.concatenate([column] * (pixels // column.shape[1]), axis=1)

    def partner(k):
        return rank ^ lax.rem(15 * k, RANKS)

    def slab_copy(sems, index, src, dst, d):
        return pltpu.make_async_remote_copy(
            src_ref=src,
            dst_ref=dst,
            send_sem=sems.at[0, 0],
            recv_sem=sems.at[1, index],
            device_id=(d, core),
            device_id_type=MESH,
        )

    def scatter(sems, src, dst, each=False, first=1, count=RANKS - 1):
        def start(k):
            d = partner(k)

            @pl.when(k < RANKS)
            def _():
                slab_copy(sems, k if each else 0, src.at[d], dst, d).start()

        loop(first + count, start, first)

    def all_slabs(sems, which, ref):
        most = ref.at[pl.ds(0, RANKS - 1)]
        pltpu.make_async_copy(most, most, sems.at[which, 0]).wait()

    def bring(which):
        far_ref, near_ref = ASYNC[which]
        return pltpu.make_async_copy(getattr(v, far_ref), getattr(v, near_ref), v.bring.at[which])

    barrier = pltpu.get_barrier_semaphore()

    def greet(k):
        pl.semaphore_signal(
            barrier, inc=1, device_id=(lax.rem(rank + k, RANKS), core), device_id_type=MESH
        )

    loop(RANKS, greet, 1)
    pl.semaphore_signal(barrier, inc=1, device_id=twin, device_id_type=MESH)

    def fetch_up(m):
        cols = pl.ds(pl.multiple_of(m * part, part), part)
        return pltpu.make_async_copy(v.w_up.at[:, cols], v.wu.at[m], v.fetch.at[0])

    def fetch_down(m):
        rows = pl.ds(pl.multiple_of(m * part, part), part)
        return pltpu.make_async_copy(v.w_down.at[rows], v.wd.at[m], v.fetch.at[1])

    def fetch(m):
        fetch_up(m).start()
        fetch_down(m).start()


    for g in range(2):
        v.tok[:, g * columns : (g + 1) * columns] = v.tokens[g, 0].astype(F32).T

    def cut_tokens(d):
        rows = v.tok[pl.ds(pl.multiple_of(d * own, 8), own), :]
        both = jnp.concatenate([rows[:, :columns], rows[:, columns:]], axis=0)
        v.tb[core, d] = both.astype(BF16)

    loop(RANKS, cut_tokens)
    lines = []
    for vector in (v.b_up, v.skip_gain, v.ln_gain, v.ln_bias, v.layer_scale, v.b_down):
        line = vector[...].reshape(1, vector.shape[0])
        lines += [line[:, q * 128 : (q + 1) * 128] for q in range(vector.shape[0] // 128)]
    lines.append(jnp.zeros((32 - len(lines), 128), F32))
    v.vx[core] = jnp.concatenate(lines, axis=0)
    pl.semaphore_wait(barrier, RANKS)
    scatter(v.a1, v.tb.at[core], v.rb1.at[rank])
    v.rb1[rank] = v.tb[core, rank]
    for which in range(len(ASYNC)):
        bring(which).start()
    copy(v.tb.at[core], v.tb.at[core], v.tw, 0, twin).start()
    copy(v.vx.at[core], v.vx.at[core], v.tw, 1, twin).start()

    def spread(which, rows):
        block = jnp.concatenate([rows, jnp.zeros((128 - rows.shape[0], 128), F32)], axis=0)
        cols = block.T
        for q in range(15):
            v.vb[q // 3, which, q % 3 * 128 : (q % 3 + 1) * 128, :] = jnp.broadcast_to(
                cols[:, 12 + q : 13 + q], (128, 128)
            )
        return cols

    cols = spread(core, v.vx[core])
    for m in range(chunks):
        for q in range(2):
            v.bias[m, q * 128 : (q + 1) * 128, :] = jnp.broadcast_to(
                cols[:, 2 * m + q : 2 * m + q + 1], (128, 128)
            )
    for which in range(len(ASYNC)):
        bring(which).wait()
    for g in range(2):
        v.cot[:, g * columns : (g + 1) * columns] = v.cotangent[g, 0].astype(F32).T
    places_w = lax.broadcasted_iota(jnp.int32, (1, columns), 1)
    inside = jnp.concatenate(
        [(places_w < jnp.where(rank < heights[g], widths[g], 0)).astype(F32) for g in range(2)],
        axis=1,
    )
    v.inside[...] = jnp.broadcast_to(inside, (8, pixels))

    def mask_rows(q):
        rows = pl.ds(pl.multiple_of(q * 128, 128), 128)
        masked = v.cot[rows, :] * v.inside[0:1, :]
        v.gb[core, rows, :] = (masked * wide(v.vb[3, core, rows, :])).astype(BF16)

    loop(here // 128, mask_rows)
    copy(v.gb.at[core], v.gb.at[core], v.tw, 2, twin).start()

    lane = lax.broadcasted_iota(jnp.int32, (slab, lanes), 1) // per
    row = lax.broadcasted_iota(jnp.int32, (slab, lanes), 0)
    row = jnp.where(row >= own, row - own, row)
    v.pick[...] = (lane == row).astype(F32)
    chosen = lax.broadcasted_iota(jnp.int32, (here, lanes), 1) // per + rank * own
    chosen = (lax.broadcasted_iota(jnp.int32, (here, lanes), 0) == chosen).astype(F32)
    all_modes = jnp.concatenate(
        [v.log_step[...], jnp.zeros((6, here), F32)]
        + [v.log_decay[a] for a in range(2)]
        + [v.frequency[a] for a in range(2)]
        + [v.b_in[a, i] for i in range(2) for a in range(2)]
        + [v.c_out[a, i] for i in range(2) for a in range(2)],
        axis=0,
    )
    all_modes = jnp.dot(all_modes, chosen, precision=PRECISE, preferred_element_type=F32)
    mode = lax.broadcasted_iota(jnp.int32, (per, lanes), 1) % per
    mode = (mode == lax.broadcasted_iota(jnp.int32, (per, lanes), 0)).astype(F32)
    v.of_mode[...] = mode
    own_modes = jnp.sum(all_modes[8:].reshape(12, per, lanes) * mode[None], axis=1)
    v.modes[...] = jnp.concatenate([all_modes[:2], own_modes, own_modes[:2]], axis=0)
    mv = mode_values(v.modes[...])

    def powers(axis, place):
        angle = mv.step_im[axis : axis + 1] * place
        fade = jnp.exp(mv.step_re[axis : axis + 1] * place)
        return fade * jnp.cos(angle), fade * jnp.sin(angle)

    high_place = lax.broadcasted_iota(jnp.int32, (RANKS, lanes), 0).astype(F32)
    v.eh[0], v.eh[1] = powers(0, high_place)
    low_place = lax.broadcasted_iota(jnp.int32, (8, lanes), 0).astype(F32)
    base = powers(1, low_place)
    many = columns // 8
    v.ej[0], v.ej[1] = powers(
        1, 8.0 * lax.broadcasted_iota(jnp.int32, (many, lanes), 0).astype(F32)
    )
    coef_w = tuple(2.0 * part_of[1:2] for part_of in mv.coef)

    def fill(j):
        at = pl.ds(pl.multiple_of(j * 8, 8), 8)
        jump = (v.ej[0, pl.ds(j, 1), :], v.ej[1, pl.ds(j, 1), :])
        e_re, e_im = times(base, jump)
        v.ew[0, at, :] = e_re
        v.ew[1, at, :] = e_im
        v.kt[at, :] = coef_w[0] * e_re - coef_w[1] * e_im

    loop(many, fill)
    k_width = lax.dot_general(
        v.pick[...], v.kt[...], NT, precision=PRECISE, preferred_element_type=F32
    )
    k_both = by_table(k_width, v.to_hi, v.to_lo)
    k_re, k_im = k_both[:, :columns], k_both[:, columns:]
    first_lane = lax.broadcasted_iota(jnp.int32, (slab, columns), 1) == 0
    v.ks[0] = k_re
    v.ks[1] = jnp.where(first_lane, 0.0, k_im)
    v.ks[2] = jnp.where(first_lane, k_im, k_re)
    coef_h = tuple(2.0 * part_of[0:1] for part_of in mv.coef)
    v.kt[0:RANKS, :] = coef_h[0] * v.eh[0] - coef_h[1] * v.eh[1]

    taps = lax.dot_general(
        v.pick[...], v.kt[0:RANKS, :], NT, precision=PRECISE, preferred_element_type=F32
    )
    for l in range(RANKS):
        v.kh[l] = jnp.broadcast_to(taps[:, l : l + 1], (slab, 128))

    def turn(m):
        v.wut[m] = v.wu[m].T
        v.wdt[m] = v.wd[m].T


    all_slabs(v.a1, 1, v.rb1)
    loop(chunks, fetch)
    step_rows = 4

    def convolve(b):
        at = pl.ds(b * step_rows, step_rows)
        values = v.rb1[at].reshape(step_rows * slab, columns)
        shape = (step_rows, slab, columns)
        x_both = by_table(values, v.to_hi, v.to_lo)
        x_re, x_im = x_both[:, :columns].reshape(shape), x_both[:, columns:].reshape(shape)
        v.xs[0, at] = x_re
        v.xs[1, at] = x_im
        k0, k1, k2 = v.ks[0], v.ks[1], v.ks[2]
        y_both = jnp.concatenate([x_re * k0 - x_im * k1, x_re * k1 + x_im * k2], axis=2)
        y_both = y_both.reshape(step_rows * slab, 2 * columns)
        along = by_table(y_both, v.from_hi, v.from_lo)
        v.along[at] = along.astype(BF16).astype(F32).reshape(shape)

    loop(RANKS // step_rows, convolve)

    def by_tiles(body):
        def rows(r):
            for half in range(columns // 128):
                body(pl.ds(pl.multiple_of(r * 8, 8), 8), slice(half * 128, half * 128 + 128))

        loop(slab // 8, rows)

    def down_rows(at, cut):
        taps = [v.kh[l, at, :] for l in range(RANKS)]
        values = [v.along[i, at, cut] for i in range(RANKS)]
        for i in range(RANKS):
            total = taps[0] * values[i]
            for l in range(1, i + 1):
                total += taps[l] * values[i - l]
            v.tall[i, at, cut] = total

    by_tiles(down_rows)
    v.sb2[...] = v.tall[...].astype(BF16)
    scatter(v.a2, v.sb2, v.rb2.at[core, rank], each=True)
    v.rb2[core, rank] = v.sb2[rank]
    copy(v.rb2.at[core, rank], v.rb2.at[core, rank], v.fw, 0, twin).start()

    copy(v.vx.at[core], v.vx.at[1 - core], v.tw, 1, twin).wait_recv()
    spread(1 - core, v.vx[1 - core])
    pltpu.make_async_copy(v.wu, v.wu, v.fetch.at[0]).wait()
    pltpu.make_async_copy(v.wd, v.wd, v.fetch.at[1]).wait()
    loop(chunks, turn)
    v.gn[...] = jnp.zeros_like(v.gn)

    def forward(k):
        d = partner(k)
        slab_copy(v.a2, k, v.sb2.at[d], v.rb2.at[core, d], d).wait_recv()
        copy(v.rb2.at[core, d], v.rb2.at[core, d], v.fw, 0, twin).start()

    loop(RANKS, forward, 1)
    copy(v.tb.at[core], v.tb.at[1 - core], v.tw, 0, twin).wait_recv()
    copy(v.rb2.at[core], v.rb2.at[1 - core], v.fw, 0, twin).wait_recv()

    eight = jnp.zeros((8, pixels), F32)

    def folded(values):
        return values.reshape(own // 8, 8, pixels).sum(axis=0)

    def mix(i, total):
        which, d = i // RANKS, lax.rem(i, RANKS)
        spatial = v.rb2[which, d].astype(F32)
        token = v.tb[which, d].astype(F32)
        skip = wide(v.vb[0, which, pl.ds(pl.multiple_of(d * own, 8), own), :])
        spatial = jnp.concatenate([spatial[:own], spatial[own:]], axis=1)
        token = jnp.concatenate([token[:own], token[own:]], axis=1)
        mixed = spatial + skip * token
        v.xhat[i] = mixed
        return total + folded(mixed)

    channels = 2 * here
    total = lax.fori_loop(0, 2 * RANKS, mix, eight)
    centre = jnp.sum(total, axis=0, keepdims=True) * (1.0 / channels)

    def squares(i, total):
        off = v.xhat[i] - centre
        return total + folded(off * off)

    total = lax.fori_loop(0, 2 * RANKS, squares, eight)
    spread_of = jnp.sum(total, axis=0, keepdims=True) * (1.0 / channels)
    inv_std = lax.rsqrt(spread_of + EPSILON)
    v.inv[...] = jnp.broadcast_to(inv_std, (8, pixels))

    def normalize(q):
        rows = []
        for k in range(2):
            i = 2 * q + k
            which, d = i // RANKS, lax.rem(i, RANKS)
            at = pl.ds(pl.multiple_of(d * own, 8), own)
            x_hat = (v.xhat[i] - centre) * inv_std
            v.xhat[i] = x_hat
            rows.append(x_hat * wide(v.vb[1, which, at, :]) + wide(v.vb[2, which, at, :]))
        at = pl.ds(pl.multiple_of(q * 2 * own, 16), 2 * own)
        v.normed[at, :] = jnp.concatenate(rows, axis=0).astype(BF16)

    loop(RANKS, normalize)
    copy(v.gb.at[core], v.gb.at[1 - core], v.tw, 2, twin).wait_recv()

    def feed(t):
        normed = v.normed[...]
        g_branch = v.gb[...].reshape(channels, pixels)
        hidden = jnp.dot(v.wut[t], normed, preferred_element_type=F32) + wide(v.bias[t])
        phi = 0.5 + 0.5 * lax.erf(hidden * (0.5**0.5))
        density = jnp.exp(-0.5 * hidden * hidden) * ((2.0 * jnp.pi) ** -0.5)
        active = (hidden * phi).astype(BF16)
        slope = phi + hidden * density
        g_active = jnp.dot(v.wd[t], g_branch, preferred_element_type=F32)
        g_hidden = (g_active * slope).astype(BF16)
        down = lax.dot_general(active, g_branch, NT, preferred_element_type=F32)
        down = down.astype(BF16).reshape(CUTS, 2, 2, part // CUTS // 4, channels)
        v.pd[pl.ds(CUTS * t, CUTS)] = down
        up = lax.dot_general(normed, g_hidden, NT, preferred_element_type=F32)
        up = up.astype(BF16)
        for q in range(CUTS):
            v.pu[CUTS * t + q] = up[up_cut(up.shape, q)].reshape(v.pu.shape[1:])
        v.gn[...] += jnp.dot(v.wu[t], g_hidden, preferred_element_type=F32)
        v.active[t] = active
        ones = jnp.ones((8, pixels), BF16)
        v.dbu[t] = lax.dot_general(ones, g_hidden, NT, preferred_element_type=F32)

    def share():
        v.gn_out[...] = v.gn[...].astype(BF16)
        copy(v.gn_out, v.gn_in, v.tw, 3, twin).start()

    def branches():
        def rows(q):
            at = pl.ds(pl.multiple_of(q * 128, 128), 128)
            total = jnp.dot(v.wdt[0, at, :], v.active[0], preferred_element_type=F32)
            for m in range(1, chunks):
                total += jnp.dot(v.wdt[m, at, :], v.active[m], preferred_element_type=F32)
            v.branch[at, :] = total

        loop(channels // 128, rows)
        theirs = pl.ds(pl.multiple_of((1 - core) * here, here), here)
        v.br_out[...] = v.branch[theirs, :].astype(BF16)
        copy(v.br_out, v.br_in, v.tw, 4, twin).start()

    def lane_sum(values):
        return sum(values[:, q * 128 : (q + 1) * 128] for q in range(pixels // 128))

    def norm_back():
        copy(v.gn_out, v.gn_in, v.tw, 3, twin).wait_recv()

        def whole(q, totals):
            at = pl.ds(pl.multiple_of(q * 2 * own, 16), 2 * own)
            g_normed = v.gn[at, :] + v.gn_in[at, :].astype(F32)
            v.gn[at, :] = g_normed
            one, two = totals
            for k in range(2):
                i = 2 * q + k
                which, d = i // RANKS, lax.rem(i, RANKS)
                gain = wide(v.vb[1, which, pl.ds(pl.multiple_of(d * own, 8), own), :])
                g_hat = g_normed[k * own : (k + 1) * own] * gain
                one = one + folded(g_hat)
                two = two + folded(g_hat * v.xhat[i])
            return one, two

        one, two = lax.fori_loop(0, RANKS, whole, (eight, eight))
        one = jnp.sum(one, axis=0, keepdims=True) * (1.0 / channels)
        two = jnp.sum(two, axis=0, keepdims=True) * (1.0 / channels)
        scale = v.inv[0:1, :]

        def each(d):
            at = pl.ds(pl.multiple_of(d * own, 8), own)
            x_hat = v.xhat[core * RANKS + d]
            g_normed = v.gn[pl.ds(pl.multiple_of(core * here + d * own, 8), own), :]
            g_mixed = scale * (g_normed * wide(v.vb[1, core, at, :]) - one - x_hat * two)
            v.gmix[at, :] = g_mixed
            v.sums[0, at, :] = lane_sum(g_mixed * v.tok[at, :])
            v.sums[1, at, :] = lane_sum(g_normed * x_hat)
            v.sums[2, at, :] = lane_sum(g_normed)
            both = jnp.concatenate([g_mixed[:, :columns], g_mixed[:, columns:]], axis=0)
            v.sb3[d] = both.astype(BF16)

        loop(RANKS, each)
        v.rb3[rank] = v.sb3[rank]

    def outputs():
        copy(v.br_out, v.br_in, v.tw, 4, twin).wait_recv()
        mask = v.inside[0:1, :]

        def rows(q):
            at = pl.ds(pl.multiple_of(q * 128, 128), 128)
            branch = v.branch[pl.ds(pl.multiple_of(core * here + q * 128, 128), 128), :]
            branch = branch + v.br_in[at, :].astype(F32) + wide(v.vb[4, core, at, :])
            masked = branch * mask
            v.sums[3, at, :] = lane_sum(v.gb[core, at, :].astype(F32))
            v.sums[4, at, :] = lane_sum(masked * v.cot[at, :])
            v.res[at, :] = v.tok[at, :] + masked * wide(v.vb[3, core, at, :])

        loop(here // 128, rows)
        for g in range(2):
            v.o_out[g, 0] = v.res[:, g * columns : (g + 1) * columns].T.astype(BF16)
        pltpu.make_async_copy(v.o_out, v.output, v.leave.at[2]).start()

    def convolve_back():
        all_slabs(v.a3, 1, v.rb3)
        v.tall[...] = v.rb3[...].astype(F32)

        def up_rows(at, cut):
            taps = [v.kh[l, at, :] for l in range(RANKS)]
            values = [v.tall[i, at, cut] for i in range(RANKS)]
            for i in range(RANKS):
                total = taps[0] * values[i]
                for l in range(1, RANKS - i):
                    total += taps[l] * values[i + l]
                v.galong[i, at, cut] = total.astype(BF16).astype(F32)

        by_tiles(up_rows)

        def lag_rows(at, cut):
            grads = [v.tall[i, at, cut] for i in range(RANKS)]
            values = [v.along[i, at, cut] for i in range(RANKS)]
            for l in range(RANKS):
                total = grads[l] * values[0]
                for i in range(l + 1, RANKS):
                    total += grads[i] * values[i - l]
                v.lags[l, at, cut] = total

        by_tiles(lag_rows)
        v.cross[...] = jnp.zeros_like(v.cross)

    def convolve_step(turn_of):
        block = lax.rem(z + turn_of, RANKS // step_rows)
        at = pl.ds(block * step_rows, step_rows)
        shape = (step_rows, slab, columns)
        values = v.galong[at].reshape(step_rows * slab, columns).astype(BF16)
        g_both = by_table(values, v.to_hi, v.to_lo)
        g_re, g_im = g_both[:, :columns].reshape(shape), g_both[:, columns:].reshape(shape)
        x_re, x_im = v.xs[0, at], v.xs[1, at]
        k0, k1, k2 = v.ks[0], v.ks[1], v.ks[2]
        y_both = jnp.concatenate([g_re * k0 + g_im * k1, g_im * k2 - g_re * k1], axis=2)
        y_both = y_both.reshape(step_rows * slab, 2 * columns)
        conv = by_table(y_both, v.from_hi, v.from_lo)
        v.sb4[at] = conv.reshape(shape).astype(BF16)
        v.cross[0] += (x_re * g_re).sum(axis=0)
        v.cross[1] += (x_im * g_im).sum(axis=0)
        v.cross[2] += (x_re * g_im - x_im * g_re).sum(axis=0)
        for q in range(step_rows):
            d = block * step_rows + q

            @pl.when(d != rank)
            def _():
                slab_copy(v.a4, 0, v.sb4.at[d], v.rb4.at[rank], d).start()

            @pl.when(d == rank)
            def _():
                v.rb4[rank] = v.sb4[rank]

    def kernel_grads():
        cross = [v.cross[q] for q in range(3)]
        zero_lane = lax.broadcasted_iota(jnp.int32, (slab, columns), 1) == 0
        c_re = cross[0] + jnp.where(zero_lane, 0.0, cross[1])
        c_im = jnp.where(zero_lane, cross[1], cross[2])
        dk_width = by_table(jnp.concatenate([c_re, c_im], axis=1), v.from_hi, v.from_lo)
        v.kt[...] = lax.dot_general(
            dk_width, v.pick[...], TN, precision=PRECISE, preferred_element_type=F32
        )

        lags = v.lags[...].reshape(RANKS * slab, columns)
        first = lags.astype(BF16)
        second = (lags - first.astype(F32)).astype(BF16)
        ones = jnp.ones((columns, 128), BF16)
        lags = jnp.dot(first, ones, preferred_element_type=F32)
        lags += jnp.dot(second, ones, preferred_element_type=F32)
        lags = lags.reshape(RANKS, slab, 128)
        for q in range(lanes // 128):
            cut = slice(q * 128, (q + 1) * 128)
            v.kth[:, cut] = jnp.sum(lags * v.pick[:, cut][None], axis=1)

    def parameters():
        def moments(dk, e_re, e_im):
            place = lax.broadcasted_iota(jnp.int32, dk.shape, 0).astype(F32)
            terms = (dk * e_re, dk * e_im)
            plain = [jnp.sum(term, axis=0, keepdims=True) for term in terms]
            timed = [jnp.sum(term * place, axis=0, keepdims=True) for term in terms]
            return plain + timed

        rows_h = moments(v.kth[...], v.eh[0], v.eh[1])
        rows_w = moments(v.kt[...], v.ew[0], v.ew[1])
        p_re, p_im, t_re, t_im = (
            2.0 * jnp.concatenate([h, w], axis=0) for h, w in zip(rows_h, rows_w)
        )
        plain, timed = (p_re, p_im), (t_re, t_im)
        mv = mode_values(v.modes[...])
        step, rate = mv.step, mv.rate
        zoh_plain = times(mv.zoh, plain)
        g_b = times(mv.c, zoh_plain)
        g_c = times(mv.b, zoh_plain)
        coef_timed = times(mv.coef, timed)
        prod_plain = times(mv.prod, plain)
        slope = times(
            (step * mv.once[0] - mv.zoh[0], step * mv.once[1] - mv.zoh[1]), mv.over
        )
        g_rate = times(prod_plain, slope)
        g_rate = (g_rate[0] + step * coef_timed[0], g_rate[1] + step * coef_timed[1])
        g_step = times(prod_plain, mv.once)[0] + times(coef_timed, rate)[0]
        rows = [
            step * g_step,
            g_rate[0] * rate[0],
            -g_rate[1],
            g_b[0],
            -g_b[1],
            g_c[0],
            -g_c[1],
            jnp.zeros_like(step),
        ]
        table = jnp.concatenate(rows, axis=0)
        z, y, x = rank // 4, (rank // 2) % 2, rank % 2
        blocks = [jnp.zeros((per, 128), F32) for _ in range(3)]
        at = lax.broadcasted_iota(jnp.int32, (128, lanes), 0)
        at -= lax.broadcasted_iota(jnp.int32, (128, lanes), 1) // per
        for k in range(5):
            chosen = (at == k * own).astype(BF16)
            for five in range(3 if k < 4 else 2):
                r = 5 * five + k
                values = (v.of_mode[...] * table[r : r + 1]).astype(BF16)
                blocks[five] += lax.dot_general(values, chosen, NT, preferred_element_type=F32)
        for five in range(3):
            v.pack[five * per : (five + 1) * per, :] = blocks[five].astype(BF16)
        ones = jnp.ones((8, 128), F32)
        vectors = [
            v.dbu[m, 0:1, q * 128 : (q + 1) * 128] for m in range(chunks) for q in range(part // 128)
        ]
        for k in range(5):
            line = lax.dot_general(
                ones, v.sums[k], NT, precision=PRECISE, preferred_element_type=F32
            )
            vectors += [line[0:1, q * 128 : (q + 1) * 128] for q in range(here // 128)]
        vectors.append(jnp.zeros((32 - len(vectors), 128), F32))
        v.pack[3 * per :, :] = jnp.concatenate(vectors, axis=0).astype(BF16)
        v.gathered[z, y, x] = v.pack[...]

        def to(k):
            target = (lax.rem(z + k, 4) * 4 + y * 2 + x, core)
            copy(v.pack, v.gathered.at[z, y, x], v.ga, k, target).start()

        loop(4, to, 1)

    def gather_across():
        def wait(k):
            s = lax.rem(z + 4 - k, 4)
            copy(v.pack, v.gathered.at[s, y, x], v.ga, k, (s * 4 + y * 2 + x, core)).wait_recv()

        loop(4, wait, 1)
        mine = v.gathered.at[:, y, x]
        copy(mine, mine, v.ga, 4, across).start()

    def gather_beside():
        theirs = v.gathered.at[:, 1 - y, x]
        copy(theirs, theirs, v.ga, 4, across).wait_recv()
        mine = v.gathered.at[:, :, x]
        copy(mine, mine, v.ga, 5, beside).start()

    def gather_done():
        theirs = v.gathered.at[:, :, 1 - x]
        copy(theirs, theirs, v.ga, 5, beside).wait_recv()
        pltpu.make_async_copy(v.gathered, v.all_gathered, v.leave.at[4]).start()

    def token_grads():
        all_slabs(v.a4, 1, v.rb4)

        def rows(d):
            at = pl.ds(pl.multiple_of(d * own, 8), own)
            conv = v.rb4[d].astype(F32)
            conv = jnp.concatenate([conv[:own], conv[own:]], axis=1)
            skip = wide(v.vb[0, core, at, :])
            v.res[at, :] = v.cot[at, :] + skip * v.gmix[at, :] + conv

        loop(RANKS, rows)
        for g in range(2):
            v.t_out[g, 0] = v.res[:, g * columns : (g + 1) * columns].T.astype(BF16)
        pltpu.make_async_copy(v.t_out, v.d_tokens, v.leave.at[3]).start()

    down = types.SimpleNamespace(
        part=v.pd,
        from_first=v.d1,
        from_outer=v.d2,
        from_inner=v.d3,
        from_third=v.d4,
        full=v.fd,
        keep=x,
        first=beside,
        third=across,
    )
    up = types.SimpleNamespace(
        part=v.pu,
        from_first=v.u1,
        from_outer=v.u2,
        from_inner=v.u3,
        from_third=v.u4,
        full=v.fu,
        keep=y,
        first=across,
        third=beside,
    )

    def leave(c):
        return (
            pltpu.make_async_copy(v.fd.at[c], v.down.at[c], v.leave.at[0]),
            pltpu.make_async_copy(v.fu.at[c], v.up.at[c], v.leave.at[1]),
        )


    def advance(stage, c, role):
        reduce_stage(stage, c, role, places, (down, up), v.sent, v.landed)

    def known(stage, c):
        live = (c * (pieces - 1 - c) >= 0).astype(jnp.int32)
        advance(stage, c, live * (1 + middle))
        if stage == STAGES - 1:

            @pl.when(live > 0)
            def _():
                for one in leave(c):
                    one.start()

    events = {
        0: norm_back,
        1: branches,
        6: outputs,
        3: convolve_back,
        8: kernel_grads,
        9: parameters,
        12: gather_across,
        14: gather_beside,
        21: gather_done,
        16: token_grads,
    }

    def feed_and_send(t):
        feed(t)
        for q in range(CUTS):
            c = CUTS * t + q
            advance(0, c, (c < 6).astype(jnp.int32) * (1 + middle))
        known(1, t - 3)
        known(2, t - 3 - 2)

    loop(chunks, feed_and_send)
    share()
    for ahead in range(chunks - 3, 4):
        known(1, jnp.int32(ahead))
        known(2, jnp.int32(ahead - 2))
        known(3, jnp.int32(ahead - 4))

    def tick(t, carry):
        for when, event in events.items():
            pl.when(t == when)(event)
        batch = t - 0

        @pl.when(batch * (2 - 1 - batch) >= 0)
        def _():
            scatter(v.a3, v.sb3, v.rb3.at[rank], first=1 + 8 * batch, count=8)

        turn_of = t - 3

        @pl.when(turn_of * (RANKS // step_rows - 1 - turn_of) >= 0)
        def _():
            convolve_step(turn_of)

        for q in range(1):
            c = 6 + 1 * (t - 0) + q
            known(0, jnp.where(t < 0, pieces, c))
        for stage, start in enumerate((0,2,4,6,8,10,12,14,16), 1):
            known(stage, t + 4 - start)
        return carry

    lax.fori_loop(0, pieces + (0,2,4,6,8,10,12,14,16)[-1] - 4, tick, 0)

    pltpu.make_async_copy(v.gathered, v.all_gathered, v.leave.at[4]).wait()
    pltpu.make_async_copy(v.fd, v.down, v.leave.at[0]).wait()
    pltpu.make_async_copy(v.fu, v.up, v.leave.at[1]).wait()
    pltpu.make_async_copy(v.o_out, v.output, v.leave.at[2]).wait()
    pltpu.make_async_copy(v.t_out, v.d_tokens, v.leave.at[3]).wait()
    all_slabs(v.a1, 0, v.rb1)
    all_slabs(v.a2, 0, v.sb2)
    all_slabs(v.a3, 0, v.sb3)
    all_slabs(v.a4, 0, v.sb4)
    reduce_sent(middle, (down, up), v.sent)
    copy(v.tb.at[core], v.tb.at[core], v.tw, 0, twin).wait_send()
    copy(v.vx.at[core], v.vx.at[core], v.tw, 1, twin).wait_send()
    copy(v.gb.at[core], v.gb.at[core], v.tw, 2, twin).wait_send()
    copy(v.gn_out, v.gn_in, v.tw, 3, twin).wait_send()
    copy(v.br_out, v.br_in, v.tw, 4, twin).wait_send()

    copy(v.rb2.at[core], v.rb2.at[core], v.fw, 0, twin).wait_send()

    def gather_sent(k):
        target = (lax.rem(z + k, 4) * 4 + y * 2 + x, core)
        copy(v.pack, v.gathered.at[z, y, x], v.ga, k, target).wait_send()

    loop(4, gather_sent, 1)
    mine = v.gathered.at[:, y, x]
    copy(mine, mine, v.ga, 4, across).wait_send()
    mine = v.gathered.at[:, :, x]
    copy(mine, mine, v.ga, 5, beside).wait_send()


def finish_kernel(own, *refs):
    ins, outs, small, near, wide, sems = refs[:5], refs[5:20], refs[20:33], refs[33:36], refs[36:38], refs[38:]
    brought, moved, left = sems
    pieces, rows = near[0].shape[0], wide[0].shape[1]
    group = pieces // brought.shape[1]

    def bring(which, m):
        some = pl.ds(m * group, group)
        return pltpu.make_async_copy(
            ins[which].at[some], near[which].at[some], brought.at[which, m]
        )

    def leave(which, m):
        if which == 0:
            place = outs[0].at[pl.ds(pl.multiple_of(m * rows, rows), rows)]
        else:
            up_rows, up_cols = wide[1].shape[1:]
            place = outs[1].at[
                pl.ds(pl.multiple_of(m % CUTS // 2 * up_rows, 16), up_rows),
                pl.ds(pl.multiple_of((m // CUTS * 2 + m % 2) * up_cols, 128), up_cols),
            ]
        return pltpu.make_async_copy(wide[which].at[m], place, left.at[which])

    brings = [
        pltpu.make_async_copy(src, dst, brought.at[2, k])
        for k, (src, dst) in enumerate(zip(ins[2:], (near[2],) + small[:2]))
    ]
    moves = [
        pltpu.make_async_copy(src, dst, moved.at[k])
        for k, (src, dst) in enumerate(zip(small, outs[2:]))
    ]

    def each(count, body):
        def step(m, carry):
            for which in range(2):
                body(which, m)
            return carry

        lax.fori_loop(0, count, step, 0)

    def widen(which, m):
        bring(which, m).wait()
        for q in range(group):
            one = group * m + q
            wide[which][one] = near[which][one].reshape(wide[which].shape[1:]).astype(F32)
            leave(which, one).start()

    for one in brings:
        one.start()
    each(brought.shape[1], lambda which, m: bring(which, m).start())
    for one in brings:
        one.wait()
    widen_small(own, near[2], small[2:])
    for one in moves:
        one.start()
    each(brought.shape[1], widen)
    for which in range(2):
        pltpu.make_async_copy(wide[which], wide[which], left.at[which]).wait()
    for one in moves:
        one.wait()


def widen_small(own, gathered, small):
    d_log_step, d_log_decay, d_frequency, d_b_in, d_c_out = small[:5]
    per, here = d_log_decay.shape[1:]
    lane = lax.broadcasted_iota(jnp.int32, (per, 128), 1)
    whole = []
    for r in range(14):
        five, k = divmod(r, 5)
        windows = [jnp.zeros((per, 128), F32) for _ in range(here // 128)]
        for s in range(RANKS):
            block = gathered[s // 4, s // 2 % 2, s % 2, five * per : (five + 1) * per, :]
            turned = pltpu.roll(block.astype(F32), (own * (s - k)) % 128, 1)
            window, low = divmod(own * s, 128)
            inside = (lane >= low) & (lane < low + own)
            windows[window] = jnp.where(inside, turned, windows[window])
            if low + own > 128:
                inside = lane < low + own - 128
                windows[window + 1] = jnp.where(inside, turned, windows[window + 1])
        whole.append(jnp.concatenate(windows, axis=1))
    for a in range(2):
        d_log_step[a : a + 1, :] = jnp.sum(whole[a], axis=0, keepdims=True)
        d_log_decay[a] = whole[2 + a]
        d_frequency[a] = whole[4 + a]
        for i in range(2):
            d_b_in[a, i] = whole[6 + 2 * i + a]
            d_c_out[a, i] = whole[10 + 2 * i + a]
    sums = jnp.zeros((32, 128), F32)
    for s in range(RANKS):
        sums += gathered[s // 4, s // 2 % 2, s % 2, 3 * per :, :].astype(F32)
    row = 0
    for vector in small[5:]:
        for q in range(vector.shape[0] // 128):
            vector[pl.ds(q * 128, 128)] = sums[row]
            row += 1


def block_shards(
    tokens,
    heights,
    widths,
    log_step,
    log_decay,
    frequency,
    b_in,
    c_out,
    skip_gain,
    ln_gain,
    ln_bias,
    w_up,
    b_up,
    w_down,
    b_down,
    layer_scale,
    cotangent,
):
    columns, here = tokens.shape[2:]
    modes_each = log_decay.shape[2]
    hidden = w_up.shape[1]
    own = here // RANKS
    chunks = hidden // 256
    part = hidden // chunks
    channels = 2 * here
    pixels = 2 * columns
    lanes = own * modes_each
    tables = spectral_tables(columns)
    slabs = (RANKS, 2 * own, columns)
    tall = pltpu.VMEM(slabs, F32)
    in_vmem = pl.BlockSpec(memory_space=pltpu.VMEM)
    in_smem = pl.BlockSpec(memory_space=pltpu.SMEM)
    anywhere = pl.BlockSpec(memory_space=pl.ANY)
    inputs = dict(
        tokens=(tokens, in_vmem),
        cotangent_in=(cotangent, anywhere),
        heights=(heights, in_smem),
        widths=(widths, in_smem),
        log_step_in=(log_step, anywhere),
        log_decay_in=(log_decay.swapaxes(-1, -2), anywhere),
        frequency_in=(frequency.swapaxes(-1, -2), anywhere),
        b_in_in=(b_in.swapaxes(-1, -2), anywhere),
        c_out_in=(c_out.swapaxes(-1, -2), anywhere),
        b_up=(b_up, in_vmem),
        skip_gain=(skip_gain, in_vmem),
        ln_gain=(ln_gain, in_vmem),
        ln_bias=(ln_bias, in_vmem),
        layer_scale=(layer_scale, in_vmem),
        b_down=(b_down, in_vmem),
        w_up=(w_up, anywhere),
        w_down=(w_down, anywhere),
        to_hi_in=(tables[0], anywhere),
        to_lo_in=(tables[1], anywhere),
        from_hi_in=(tables[2], anywhere),
        from_lo_in=(tables[3], anywhere),
    )
    down_shape = (CUTS * chunks, 2, 2, part // CUTS // 4, channels)
    up_shape = (CUTS * chunks, 2, 2, channels // (2 * CUTS), part // 2)
    outs = dict(
        output=(jax.ShapeDtypeStruct(tokens.shape, BF16), anywhere),
        d_tokens=(jax.ShapeDtypeStruct(tokens.shape, BF16), anywhere),
        down=(jax.ShapeDtypeStruct(down_shape, BF16), anywhere),
        up=(jax.ShapeDtypeStruct(up_shape, BF16), anywhere),
        all_gathered=(
            jax.ShapeDtypeStruct((4, 2, 2, 3 * modes_each + 32, 128), BF16),
            anywhere,
        ),
    )
    low_slabs = pltpu.VMEM(slabs, BF16)
    both_slabs = pltpu.VMEM((2,) + slabs, BF16)
    scratch = dict(
        wu=pltpu.VMEM((chunks, channels, part), BF16),
        wd=pltpu.VMEM((chunks, part, channels), BF16),
        wut=pltpu.VMEM((chunks, part, channels), BF16),
        wdt=pltpu.VMEM((chunks, channels, part), BF16),
        tok=pltpu.VMEM((here, pixels), F32),
        cot=pltpu.VMEM((here, pixels), F32),
        gmix=pltpu.VMEM((here, pixels), F32),
        res=pltpu.VMEM((here, pixels), F32),
        tb=both_slabs,
        rb1=low_slabs,
        sb2=low_slabs,
        rb2=both_slabs,
        sb3=low_slabs,
        rb3=low_slabs,
        sb4=low_slabs,
        rb4=low_slabs,
        vx=pltpu.VMEM((2, 32, 128), F32),
        vb=pltpu.VMEM((5, 2, here, 128), F32),
        bias=pltpu.VMEM((chunks, part, 128), F32),
        inside=pltpu.VMEM((8, pixels), F32),
        inv=pltpu.VMEM((8, pixels), F32),
        gb=pltpu.VMEM((2, here, pixels), BF16),
        modes=pltpu.VMEM((16, lanes), F32),
        of_mode=pltpu.VMEM((modes_each, lanes), F32),
        cross=pltpu.VMEM((3, 2 * own, columns), F32),
        pick=pltpu.VMEM((2 * own, lanes), F32),
        eh=pltpu.VMEM((2, RANKS, lanes), F32),
        ej=pltpu.VMEM((2, columns // 8, lanes), F32),
        ew=pltpu.VMEM((2, columns, lanes), F32),
        kt=pltpu.VMEM((columns, lanes), F32),
        kth=pltpu.VMEM((RANKS, lanes), F32),
        ks=pltpu.VMEM((3, 2 * own, columns), F32),
        kh=pltpu.VMEM((RANKS, 2 * own, 128), F32),
        xs=pltpu.VMEM((2,) + slabs, F32),
        along=tall,
        tall=tall,
        galong=tall,
        lags=tall,
        xhat=pltpu.VMEM((2 * RANKS, own, pixels), F32),
        normed=pltpu.VMEM((channels, pixels), BF16),
        branch=pltpu.VMEM((channels, pixels), F32),
        active=pltpu.VMEM((chunks, part, pixels), BF16),
        gn=pltpu.VMEM((channels, pixels), F32),
        gn_out=pltpu.VMEM((channels, pixels), BF16),
        gn_in=pltpu.VMEM((channels, pixels), BF16),
        br_out=pltpu.VMEM((here, pixels), BF16),
        br_in=pltpu.VMEM((here, pixels), BF16),
        dbu=pltpu.VMEM((chunks, 8, part), F32),
        sums=pltpu.VMEM((5, here, 128), F32),
        pack=pltpu.VMEM((3 * modes_each + 32, 128), BF16),
        fetch=pltpu.SemaphoreType.DMA((2,)),
        leave=pltpu.SemaphoreType.DMA((5,)),
        gathered=pltpu.VMEM((4, 2, 2, 3 * modes_each + 32, 128), BF16),
        bring=pltpu.SemaphoreType.DMA((len(ASYNC),)),
        o_out=pltpu.VMEM(tokens.shape, BF16),
        t_out=pltpu.VMEM(tokens.shape, BF16),
        cotangent=pltpu.VMEM(cotangent.shape, BF16),
        log_step=pltpu.VMEM(log_step.shape, F32),
        log_decay=pltpu.VMEM((2, modes_each, here), F32),
        frequency=pltpu.VMEM((2, modes_each, here), F32),
        b_in=pltpu.VMEM((2, 2, modes_each, here), F32),
        c_out=pltpu.VMEM((2, 2, modes_each, here), F32),
        to_hi=pltpu.VMEM(tables[0].shape, BF16),
        to_lo=pltpu.VMEM(tables[1].shape, BF16),
        from_hi=pltpu.VMEM(tables[2].shape, BF16),
        from_lo=pltpu.VMEM(tables[3].shape, BF16),
    )

    def reduction(shape):
        count, halves, pieces, rows, width = shape
        whole = pltpu.VMEM(shape, BF16)
        half = pltpu.VMEM((count, pieces, rows, width), BF16)
        piece = pltpu.VMEM((count, rows, width), BF16)
        return whole, half, piece, piece, piece, whole

    down_scratch, up_scratch = reduction(down_shape), reduction(up_shape)
    scratch.update(
        zip(("pd", "d1", "d2", "d3", "d4", "fd"), down_scratch),
    )
    scratch.update(
        zip(("pu", "u1", "u2", "u3", "u4", "fu"), up_scratch),
    )
    one_each = pltpu.SemaphoreType.DMA((2, 1))
    scratch.update(a1=one_each, a3=one_each, a4=one_each, fw=one_each)
    scratch.update(a2=pltpu.SemaphoreType.DMA((2, RANKS)))
    scratch.update(sent=pltpu.SemaphoreType.DMA((9,)))
    scratch.update(landed=pltpu.SemaphoreType.DMA((6, CUTS * chunks)))
    scratch.update(tw=pltpu.SemaphoreType.DMA((2, 5)), ga=pltpu.SemaphoreType.DMA((2, 6)))
    names = tuple(inputs) + tuple(outs) + tuple(scratch)
    output, d_tokens, down, up, gathered = pl.pallas_call(
        functools.partial(block_kernel, names),
        out_shape=tuple(shape for shape, _ in outs.values()),
        in_specs=[spec for _, spec in inputs.values()],
        out_specs=tuple(spec for _, spec in outs.values()),
        scratch_shapes=list(scratch.values()),
        compiler_params=pltpu.CompilerParams(
            collective_id=0, has_side_effects=True, vmem_limit_bytes=62 << 20
        ),
    )(*(value for value, _ in inputs.values()))
    result = (
        jax.ShapeDtypeStruct((hidden, channels), F32),
        jax.ShapeDtypeStruct((channels, hidden), F32),
        output,
        d_tokens,
        log_step,
        jax.ShapeDtypeStruct((2, modes_each, here), F32),
        jax.ShapeDtypeStruct((2, modes_each, here), F32),
        jax.ShapeDtypeStruct((2, 2, modes_each, here), F32),
        jax.ShapeDtypeStruct((2, 2, modes_each, here), F32),
        b_up,
        skip_gain,
        ln_gain,
        ln_bias,
        b_down,
        layer_scale,
    )
    result = tuple(jax.ShapeDtypeStruct(one.shape, one.dtype) for one in result)
    (
        d_w_down,
        d_w_up,
        output,
        d_tokens,
        d_log_step,
        d_log_decay,
        d_frequency,
        d_b_in,
        d_c_out,
        d_b_up,
        d_skip_gain,
        d_ln_gain,
        d_ln_bias,
        d_b_down,
        d_layer_scale,
    ) = pl.pallas_call(
        functools.partial(finish_kernel, own),
        out_shape=result,
        in_specs=[anywhere] * 5,
        out_specs=(anywhere,) * 15,
        scratch_shapes=[pltpu.VMEM(one.shape, one.dtype) for one in result[2:]]
        + [pltpu.VMEM(one.shape, BF16) for one in (down, up, gathered)]
        + [
            pltpu.VMEM((CUTS * chunks, part // CUTS, channels), F32),
            pltpu.VMEM((CUTS * chunks, channels * 2 // CUTS, part // 2), F32),
            pltpu.SemaphoreType.DMA((3, chunks)),
            pltpu.SemaphoreType.DMA((13,)),
            pltpu.SemaphoreType.DMA((2,)),
        ],
        compiler_params=pltpu.CompilerParams(vmem_limit_bytes=62 << 20),
    )(down, up, gathered, output, d_tokens)
    return (
        output,
        d_tokens,
        d_log_step,
        d_log_decay.swapaxes(-1, -2),
        d_frequency.swapaxes(-1, -2),
        d_b_in.swapaxes(-1, -2),
        d_c_out.swapaxes(-1, -2),
        d_skip_gain,
        d_ln_gain,
        d_ln_bias,
        d_w_up,
        d_b_up,
        d_w_down,
        d_b_down,
        d_layer_scale,
    )


def shards(
    tokens,
    heights,
    widths,
    log_step,
    log_decay,
    frequency,
    b_in,
    c_out,
    skip_gain,
    ln_gain,
    ln_bias,
    w_up,
    b_up,
    w_down,
    b_down,
    layer_scale,
    cotangent,
):
    row_count = lax.axis_size("rows")
    row_rank = lax.axis_index("rows")
    grid_count, rows_here, columns, channels = tokens.shape
    all_channels = channels * lax.axis_size("ch")
    height = rows_here * row_count
    own_count = channels // row_count
    first_chan = row_rank * own_count
    pixels = grid_count * rows_here * columns
    token_f = tokens.astype(jnp.float32)
    width_tables = make_tables(columns)
    height_tables = make_tables(height)
    own_params = tuple(
        lax.dynamic_slice_in_dim(param, first_chan, own_count, param.ndim - trailing)
        for param, trailing in (
            (log_step, 1),
            (log_decay, 2),
            (frequency, 2),
            (b_in, 2),
            (c_out, 2),
        )
    )
    width_params = tuple(param[1] for param in own_params)
    height_params = tuple(param[0] for param in own_params)
    k_width, width_pull = jax.vjp(lambda params: make_kernel(params, columns), width_params)
    k_height, height_pull = jax.vjp(lambda params: make_kernel(params, height), height_params)
    kw_re, kw_im = kernel_spectrum(k_width, width_tables)
    kh_re, kh_im = kernel_spectrum(k_height, height_tables)
    kh_re = kh_re[:, None, :]
    kh_im = kh_im[:, None, :]
    pencil_tokens = lax.all_to_all(tokens, "rows", split_axis=3, concat_axis=1, tiled=True)
    x_re, x_im = to_spectrum(pencil_tokens.astype(jnp.float32), width_tables, "fw,grwc->grfc")
    along_width = from_spectrum(
        x_re * kw_re - x_im * kw_im, x_re * kw_im + x_im * kw_re, width_tables, "fw,grfc->grwc"
    ).astype(jnp.bfloat16)
    p_re, p_im = to_spectrum(along_width.astype(jnp.float32), height_tables, "fh,ghwc->gfwc")
    mixed_cols = from_spectrum(
        p_re * kh_re - p_im * kh_im, p_re * kh_im + p_im * kh_re, height_tables, "fh,gfwc->ghwc"
    ).astype(jnp.bfloat16)
    back_rows = lax.all_to_all(mixed_cols, "rows", split_axis=1, concat_axis=3, tiled=True)
    mixed = back_rows.astype(jnp.float32) + skip_gain * token_f
    flat_mixed = mixed.reshape(pixels, channels)
    sum_one, sum_two = lax.psum(
        (jnp.sum(flat_mixed, axis=1), jnp.sum(flat_mixed * flat_mixed, axis=1)), "ch"
    )
    centre = sum_one / all_channels
    spread = sum_two / all_channels - centre * centre
    inv_std = lax.rsqrt(spread + EPSILON)[:, None]
    x_hat = (flat_mixed - centre[:, None]) * inv_std
    normed = (x_hat * ln_gain + ln_bias).astype(jnp.bfloat16)
    hidden = (
        jnp.dot(
            lax.all_gather(normed, "ch", axis=1, tiled=True),
            w_up,
            preferred_element_type=jnp.float32,
        )
        + b_up
    )
    active = jax.nn.gelu(hidden, approximate=False).astype(jnp.bfloat16)
    partials = jnp.dot(active, w_down, preferred_element_type=jnp.float32)
    branch = (
        lax.psum_scatter(
            partials.astype(jnp.bfloat16), "ch", scatter_dimension=1, tiled=True
        ).astype(jnp.float32)
        + b_down
    )
    row_ids = row_rank * rows_here + jnp.arange(rows_here, dtype=jnp.int32)
    col_ids = jnp.arange(columns, dtype=jnp.int32)
    inside = (row_ids[None, :, None] < heights[:, None, None]) & (
        col_ids[None, None, :] < widths[:, None, None]
    )
    inside = inside.astype(jnp.float32).reshape(pixels, 1)
    flat_tokens = token_f.reshape(pixels, channels)
    output = (
        (flat_tokens + inside * layer_scale * branch).astype(jnp.bfloat16).reshape(tokens.shape)
    )
    over_rows = (((0,), (0,)), ((), ()))
    over_cols = (((1,), (1,)), ((), ()))
    g_flat = cotangent.astype(jnp.float32).reshape(pixels, channels)
    g_masked = g_flat * inside
    g_branch = (g_masked * layer_scale).astype(jnp.bfloat16)
    d_layer_scale = jnp.sum(g_masked * branch, axis=0)
    d_b_down = jnp.sum(g_branch.astype(jnp.float32), axis=0)
    g_branch_all = lax.all_gather(g_branch, "ch", axis=1, tiled=True)
    d_w_down = lax.dot_general(active, g_branch_all, over_rows, preferred_element_type=jnp.float32)
    g_active = lax.dot_general(g_branch_all, w_down, over_cols, preferred_element_type=jnp.float32)
    gelu_pull = jax.vjp(lambda values: jax.nn.gelu(values, approximate=False), hidden)[1]
    g_hidden = gelu_pull(g_active)[0].astype(jnp.bfloat16)
    d_b_up = jnp.sum(g_hidden.astype(jnp.float32), axis=0)
    d_w_up = lax.dot_general(
        lax.all_gather(normed, "ch", axis=1, tiled=True),
        g_hidden,
        over_rows,
        preferred_element_type=jnp.float32,
    )
    g_terms = lax.dot_general(g_hidden, w_up, over_cols, preferred_element_type=jnp.float32)
    g_normed = lax.psum_scatter(g_terms, "ch", scatter_dimension=1, tiled=True)
    d_ln_gain = jnp.sum(g_normed * x_hat, axis=0)
    d_ln_bias = jnp.sum(g_normed, axis=0)
    g_hat = g_normed * ln_gain
    sum_grad, sum_cross = lax.psum((jnp.sum(g_hat, axis=1), jnp.sum(g_hat * x_hat, axis=1)), "ch")
    g_mixed = inv_std * (
        g_hat - sum_grad[:, None] / all_channels - x_hat * sum_cross[:, None] / all_channels
    )
    d_skip_gain = jnp.sum(g_mixed * flat_tokens, axis=0)
    g_spatial = g_mixed.astype(jnp.bfloat16).reshape(tokens.shape)
    pencil_grad = lax.all_to_all(g_spatial, "rows", split_axis=3, concat_axis=1, tiled=True)
    gp_re, gp_im = to_spectrum(pencil_grad.astype(jnp.float32), height_tables, "fh,ghwc->gfwc")
    vp_re, vp_im = p_re, p_im
    g_pencil_along = from_spectrum(
        gp_re * kh_re + gp_im * kh_im, gp_im * kh_re - gp_re * kh_im, height_tables, "fh,gfwc->ghwc"
    ).astype(jnp.bfloat16)
    cross_re = jnp.sum(vp_re * gp_re + vp_im * gp_im, axis=(0, 2))
    cross_im = jnp.sum(vp_re * gp_im - vp_im * gp_re, axis=(0, 2))
    dk_height = kernel_from_cross(cross_re, cross_im, height_tables)
    g_along = g_pencil_along
    ga_re, ga_im = to_spectrum(g_along.astype(jnp.float32), width_tables, "fw,grwc->grfc")
    g_conv = from_spectrum(
        ga_re * kw_re + ga_im * kw_im, ga_im * kw_re - ga_re * kw_im, width_tables, "fw,grfc->grwc"
    )
    g_conv = lax.all_to_all(
        g_conv.astype(jnp.bfloat16), "rows", split_axis=1, concat_axis=3, tiled=True
    ).astype(jnp.float32)
    wide_re = jnp.sum(x_re * ga_re + x_im * ga_im, axis=(0, 1))
    wide_im = jnp.sum(x_re * ga_im - x_im * ga_re, axis=(0, 1))
    dk_width = kernel_from_cross(wide_re, wide_im, width_tables)
    d_tokens = ((g_flat + g_mixed * skip_gain).reshape(tokens.shape) + g_conv).astype(jnp.bfloat16)
    width_grads = width_pull(dk_width)[0]
    height_grads = height_pull(dk_height)[0]

    def gathered(pieces, dim_num):
        return lax.all_gather(jnp.stack(pieces), "rows", axis=dim_num, tiled=True)

    param_grads = tuple(
        gathered(pair, dim_num)
        for pair, dim_num in zip(zip(height_grads, width_grads), (1, 1, 1, 2, 2))
    )
    d_w_down, d_w_up, d_skip_gain, d_ln_gain, d_ln_bias, d_b_up, d_b_down, d_layer_scale = lax.psum(
        (d_w_down, d_w_up, d_skip_gain, d_ln_gain, d_ln_bias, d_b_up, d_b_down, d_layer_scale),
        "rows",
    )
    return (output, d_tokens) + param_grads + (
        d_skip_gain,
        d_ln_gain,
        d_ln_bias,
        d_w_up,
        d_b_up,
        d_w_down,
        d_b_down,
        d_layer_scale,
    )


def solution(mesh):
    one_row_each = mesh.shape["rows"] == RANKS and mesh.shape["ch"] == 2
    return jax.shard_map(
        block_shards if one_row_each else shards,
        mesh=mesh,
        in_specs=(
            P(None, "rows", None, "ch"),
            P(),
            P(),
            P(None, "ch"),
            P(None, "ch", None),
            P(None, "ch", None),
            P(None, None, "ch", None),
            P(None, None, "ch", None),
            P("ch"),
            P("ch"),
            P("ch"),
            P(None, "ch"),
            P("ch"),
            P("ch", None),
            P("ch"),
            P("ch"),
            P(None, "rows", None, "ch"),
        ),
        out_specs=(
            P(None, "rows", None, "ch"),
            P(None, "rows", None, "ch"),
            P(None, "ch"),
            P(None, "ch", None),
            P(None, "ch", None),
            P(None, None, "ch", None),
            P(None, None, "ch", None),
            P("ch"),
            P("ch"),
            P("ch"),
            P(None, "ch"),
            P("ch"),
            P("ch", None),
            P("ch"),
            P("ch"),
        ),
        check_vma=False,
    )
```
